128 devices in a mesh: fsdp: 16 (over y_hi, x, core), seq: 8 (over y_lo, z).
Axes of the slice: x: 4, y: 4 (y_hi: 2, y_lo: 2; y = y_hi * 2 + y_lo), z: 4, core: 2. Of those that a mesh axis runs over, the one named last changes fastest.
Arguments:
- tokens: bfloat16 [16, 2048, 1024], P('fsdp', 'seq'), may hold values from -6 to 6
- encoded: bfloat16 [16, 1024, 1024], P('fsdp', 'seq'), may hold values from -6 to 6
- unit_ids: int32 [16, 2048], P('fsdp', 'seq'), may hold values from 0 to 15, as said below
- text_ids: int32 [16, 1024], P('fsdp', 'seq'), may hold values from 0 to 15, as said below
- cotangent: bfloat16 [16, 2048, 1024], P('fsdp', 'seq'), may hold values from -6 to 6
- attn_in: float32 [6, 1024, 1024], P(None, ('fsdp', 'seq')), may hold values from -0.1875 to 0.1875
- attn_out: float32 [2, 1024, 1024], P(None, ('fsdp', 'seq')), may hold values from -0.75 to 0.75
- w_up: float32 [1024, 4096], P(('fsdp', 'seq')), may hold values from -0.1875 to 0.1875
- w_down: float32 [4096, 1024], P(('fsdp', 'seq')), may hold values from -0.09375 to 0.09375
- norm_gains: float32 [4, 1024], P(None, ('fsdp', 'seq')), may hold values from 0.25 to 1.75
- shifts: float32 [4, 1024], P(None, ('fsdp', 'seq')), may hold values from -1.8 to 1.8
- biases: float32 [7, 1024], P(None, ('fsdp', 'seq')), may hold values from -1.8 to 1.8
- up_bias: float32 [4096], P(('fsdp', 'seq')), may hold values from -1.8 to 1.8
Outputs:
- layer_out: float32 [16, 2048, 1024], P('fsdp', 'seq')
- d_tokens: float32 [16, 2048, 1024], P('fsdp', 'seq')
- d_encoded: float32 [16, 1024, 1024], P('fsdp', 'seq')
- d_attn_in: float32 [6, 1024, 1024], P(None, ('fsdp', 'seq'))
- d_attn_out: float32 [2, 1024, 1024], P(None, ('fsdp', 'seq'))
- d_w_up: float32 [1024, 4096], P(('fsdp', 'seq'))
- d_w_down: float32 [4096, 1024], P(('fsdp', 'seq'))
- d_norm_gains: float32 [4, 1024], P(None, ('fsdp', 'seq'))
- d_shifts: float32 [4, 1024], P(None, ('fsdp', 'seq'))
- d_biases: float32 [7, 1024], P(None, ('fsdp', 'seq'))
- d_up_bias: float32 [4096], P(('fsdp', 'seq'))
The draws below stay inside these ranges and needn't reach their ends.
Inputs may be any that keep to these rules, and one draw needn't show every extreme that they name: `unit_ids`: along a sequence the ids never fall, and each of the 16 documents has one unit token or more. `text_ids`: along a sequence the ids never fall, and each of the 16 documents has one text token or more; the unit tokens of a document attend to the text tokens with the same id in the same sequence.
All inputs are finite; a program needn't handle non-finite values.
Results may differ from the reference program's by a relative error of at most 0.025.
Values may be sent and summed in bfloat16 or wider, within the bound.
No kernel may reach another device: no remote copies, remote signals or barrier semaphores. Data moves between devices by JAX's collectives and lax.ppermute only.
A program may use at most 256 MiB of HBM per device.

```python
import math
import jax
import jax.numpy as jnp
from jax import lax

D = 1024
HEADS = 16
HEAD_DIM = 64
FF = 4096
DOCS = 16
SEQS = 16
SEQ_LEN = 2048
ENC_LEN = 1024


def document_lengths(base_key):

    def one_sequence(seq_key):
        order_key, weight_key = jax.random.split(seq_key)
        longest = SEQ_LEN * 3 // 4
        remaining = SEQ_LEN - longest
        powers = jax.random.randint(weight_key, (DOCS - 1,), 0, 6)
        weights = jnp.power(jnp.int32(2), powers).astype(jnp.int32)
        spare_units = remaining - (DOCS - 1)
        smaller = 1 + spare_units * weights // jnp.sum(weights)
        smaller = smaller.at[0].add(remaining - jnp.sum(smaller))
        units = jnp.concatenate([jnp.full((1,), longest, jnp.int32), smaller.astype(jnp.int32)])
        order = jax.random.permutation(order_key, DOCS)
        units = units[order]
        root_top = int(math.isqrt(SEQ_LEN)) + 1
        table = jnp.arange(1, root_top + 1, dtype=jnp.int32)
        roots = jnp.sum((table[None, :] * table[None, :] <= units[:, None]).astype(jnp.int32), axis=1)
        spare_text = ENC_LEN - DOCS
        text = 1 + spare_text * roots // jnp.sum(roots)
        is_longest = (units == longest).astype(jnp.int32)
        text = text + is_longest * (ENC_LEN - jnp.sum(text))
        return (units.astype(jnp.int32), text.astype(jnp.int32))
    seq_keys = jax.random.split(base_key, SEQS)
    return jax.vmap(one_sequence)(seq_keys)


def ids_from_lengths(lengths, total):
    ends = jnp.cumsum(lengths, axis=-1)
    positions = jnp.arange(total, dtype=jnp.int32)
    passed = positions[None, :, None] >= ends[:, None, :DOCS - 1]
    return jnp.sum(passed.astype(jnp.int32), axis=-1).astype(jnp.int32)


def draw_unit_ids(key, part):
    base_key = jax.random.fold_in(key, 7)
    units, text = document_lengths(base_key)
    return ids_from_lengths(units, SEQ_LEN)


def draw_text_ids(key, part):
    base_key = jax.random.fold_in(key, 7)
    units, text = document_lengths(base_key)
    return ids_from_lengths(text, ENC_LEN)


def block_levels(key, extent, cuts, least, top_value):
    gain = 1.0
    for axis_at, blocks in cuts:
        heights = jax.random.uniform(jax.random.fold_in(jax.random.fold_in(key, 6), axis_at), (blocks,), jnp.float32, least / len(cuts), top_value / len(cuts))
        gain = gain * jnp.repeat(jnp.exp(heights), extent[axis_at] // blocks).reshape((-1,) + (1,) * (len(extent) - 1 - axis_at))
    return gain


def centred(own_key, extent, scale, limit, cuts=(), held_as=jnp.bfloat16):
    gain = block_levels(own_key, extent, cuts, -0.22, 0.18) if cuts else 1.0
    values = jax.random.normal(own_key, extent, jnp.float32) * scale * gain
    return jnp.minimum(jnp.maximum(values, -limit), limit).astype(held_as)


def setup_inputs(seed: int = 0) -> dict:
    streams_of = jax.random.split(jax.random.key(seed), 14)
    return {
        "tokens": centred(streams_of[0], (SEQS, SEQ_LEN, D), 1.0, 6.0, ((0, 16), (1, 8))),
        "encoded": centred(streams_of[1], (SEQS, ENC_LEN, D), 1.0, 6.0, ((0, 16), (1, 8))),
        "unit_ids": draw_unit_ids(jax.random.fold_in(streams_of[13], 71), 0),
        "text_ids": draw_text_ids(jax.random.fold_in(streams_of[13], 71), 0),
        "cotangent": centred(streams_of[4], (SEQS, SEQ_LEN, D), 1.0, 6.0, ((0, 16), (1, 8))),
        "attn_in": centred(streams_of[5], (6, D, D), D ** -0.5, 0.1875, ((1, 128),), jnp.float32),
        "attn_out": centred(streams_of[6], (2, D, D), (D // 16) ** -0.5, 0.75, ((1, 128),), jnp.float32),
        "w_up": centred(streams_of[7], (D, FF), D ** -0.5, 0.1875, ((0, 128),), jnp.float32),
        "w_down": centred(streams_of[8], (FF, D), FF ** -0.5, 0.09375, ((0, 128),), jnp.float32),
        "norm_gains": jnp.clip(1.0 + 0.15 * jax.random.normal(streams_of[9], (4, D), jnp.float32), 0.25, 1.75),
        "shifts": centred(streams_of[10], (4, D), 0.3, 1.8, ((1, 128),), jnp.float32),
        "biases": centred(streams_of[11], (7, D), 0.3, 1.8, ((1, 128),), jnp.float32),
        "up_bias": centred(streams_of[12], (FF,), 0.3, 1.8, ((0, 128),), jnp.float32),
    }


@jax.custom_vjp
def low(v):
    return lax.optimization_barrier(v.astype(jnp.bfloat16)).astype(jnp.float32)

@jax.custom_vjp
def low_back(v):
    return v

def low_keep(v):
    return (low(v), None)

def low_pass(kept, grad):
    return (grad,)

def back_keep(v):
    return (v, None)

def back_low(kept, grad):
    return (low(grad),)
low.defvjp(low_keep, low_pass)
low_back.defvjp(back_keep, back_low)
norm_eps = 1e-05
masked_score = -1e+30

def matmul32(left, right):
    return jnp.dot(left, right, precision=lax.Precision.HIGHEST, preferred_element_type=jnp.float32)

def layer_norm(values, gain_row, shift_row):
    row_mean = lax.optimization_barrier(jnp.mean(values, axis=-1, keepdims=True))
    centered = values - row_mean
    spread = lax.optimization_barrier(jnp.mean(centered * centered, axis=-1, keepdims=True))
    return centered * lax.rsqrt(spread + norm_eps) * gain_row + shift_row

def attend(queries, key_rows, value_rows, query_ids, key_ids, causal):
    row_total = queries.shape[0]
    block_rows = min(512, row_total)
    key_count = key_rows.shape[0]
    k_heads = key_rows.reshape(key_count, HEADS, HEAD_DIM)
    v_heads = value_rows.reshape(key_count, HEADS, HEAD_DIM)
    key_pos = jnp.arange(key_count, dtype=jnp.int32)
    score_scale = 1.0 / math.sqrt(HEAD_DIM)

    def one_block(q_block, ids_block, block_start):
        raw_scores = jnp.einsum('qhd,khd->hqk', q_block, k_heads, precision=lax.Precision.HIGHEST) * score_scale
        scores = low_back(raw_scores)
        allowed = ids_block[:, None] == key_ids[None, :]
        if causal:
            row_pos = block_start + jnp.arange(block_rows, dtype=jnp.int32)
            allowed = allowed & (row_pos[:, None] >= key_pos[None, :])
        scores = jnp.where(allowed[None], scores, masked_score)
        probs_low = low(jax.nn.softmax(scores, axis=-1))
        mixed_rows = jnp.einsum('hqk,khd->qhd', probs_low, v_heads, precision=lax.Precision.HIGHEST)
        return mixed_rows.reshape(block_rows, HEADS * HEAD_DIM)
    checked = jax.checkpoint(one_block)
    blocks = row_total // block_rows
    outputs = lax.map(lambda pieces: checked(pieces[0], pieces[1], pieces[2]), (queries.reshape(blocks, block_rows, HEADS, HEAD_DIM), query_ids.reshape(blocks, block_rows), jnp.arange(blocks, dtype=jnp.int32) * block_rows))
    return outputs.reshape(row_total, HEADS * HEAD_DIM)

def sequence_layer(params, inputs32, enc32, unit_seq, text_seq):
    attn_in, attn_out, w_up, w_down, norm_gains, shifts, biases, up_bias = params
    act_one = low(layer_norm(inputs32, norm_gains[0], shifts[0]))
    queries = low(low_back(matmul32(act_one, attn_in[0])) + biases[0])
    key_rows = low(low_back(matmul32(act_one, attn_in[1])))
    value_rows = low(low_back(matmul32(act_one, attn_in[2])) + biases[1])
    mixed_self = low(low_back(attend(queries, key_rows, value_rows, unit_seq, unit_seq, True)))
    after_self = inputs32 + low_back(matmul32(mixed_self, attn_out[0])) + biases[2]
    act_two = low(layer_norm(after_self, norm_gains[1], shifts[1]))
    queries_two = low(low_back(matmul32(act_two, attn_in[3])) + biases[3])
    text_keys = low(low_back(matmul32(enc32, attn_in[4])))
    text_values = low(low_back(matmul32(enc32, attn_in[5])) + biases[4])
    mixed_cross = low(low_back(attend(queries_two, text_keys, text_values, unit_seq, text_seq, False)))
    after_cross = after_self + low_back(matmul32(mixed_cross, attn_out[1])) + biases[5]
    act_three = low(layer_norm(after_cross, norm_gains[2], shifts[2]))
    before_act = low_back(matmul32(act_three, w_up)) + up_bias
    hidden = low(before_act * jax.nn.sigmoid(before_act))
    after_ffn = after_cross + low_back(matmul32(hidden, w_down)) + biases[6]
    return layer_norm(after_ffn, norm_gains[3], shifts[3])

def reference(tokens, encoded, unit_ids, text_ids, cotangent, attn_in, attn_out, w_up, w_down, norm_gains, shifts, biases, up_bias):

    def forward(inputs32, enc32, attn_in, attn_out, w_up, w_down, norm_gains, shifts, biases, up_bias):
        params = [low(member) for member in (attn_in, attn_out, w_up, w_down, norm_gains, shifts, biases, up_bias)]
        run_one = jax.checkpoint(sequence_layer)
        return lax.map(lambda pieces: run_one(params, pieces[0], pieces[1], pieces[2], pieces[3]), (inputs32, enc32, unit_ids, text_ids))
    layer_out, pullback = jax.vjp(forward, tokens.astype(jnp.float32), encoded.astype(jnp.float32), attn_in, attn_out, w_up, w_down, norm_gains, shifts, biases, up_bias)
    grads = pullback(cotangent.astype(jnp.float32))
    return (layer_out, grads[0], grads[1], grads[2], grads[3], grads[4], grads[5], grads[6], grads[7], grads[8], grads[9])
```

```python
import functools

import jax
import jax.numpy as jnp
from jax import lax
from jax.experimental import pallas as pl
from jax.experimental.pallas import tpu as pltpu
from jax.sharding import Mesh
from jax.sharding import PartitionSpec as P

D = 1024
FF = 4096
GROUPS = 8
LANES = 128
HALF = 64
BLOCK = 256
EPS = 1e-05
MASKED = -1e30

SEQ = ("yl", "z")
CHIPS = ("yh", "x", "yl", "z")
PLANE = ("yh", "yl", "x")
BF = jnp.bfloat16
F32 = jnp.float32


def dot(a, b):
    return jnp.dot(a, b, preferred_element_type=F32)


def dot_nt(a, b):
    return lax.dot_general(a, b, (((1,), (1,)), ((), ())), preferred_element_type=F32)


def dot_tn(a, b):
    return lax.dot_general(a, b, (((0,), (0,)), ((), ())), preferred_element_type=F32)


def stack_cols(xt):
    zero = jnp.zeros((HALF, xt.shape[1]), xt.dtype)
    return jnp.concatenate(
        [
            jnp.concatenate([xt[:HALF], zero], axis=0),
            jnp.concatenate([zero, xt[HALF:]], axis=0),
        ],
        axis=1,
    )


def stack_rows(x):
    lane = lax.broadcasted_iota(jnp.int32, x.shape, 1)
    zero = jnp.zeros_like(x)
    return jnp.concatenate(
        [jnp.where(lane < HALF, x, zero), jnp.where(lane < HALF, zero, x)], axis=0
    )


def unstack_cols(xt):
    n = xt.shape[1] // 2
    return jnp.concatenate([xt[:HALF, :n], xt[HALF:, n:]], axis=0)


def allowed_mask(j, start, length):
    pos = lax.broadcasted_iota(jnp.int32, (BLOCK, start.shape[1]), 0) + j * BLOCK
    off = pos - start
    return (off >= 0) & (off < length)


def attn_fwd_kernel(lo_ref, hi_ref, start_ref, len_ref, q_ref, k_ref, v_ref, o_ref, lse_ref,
                    vt_scr, s_scr, o_scr):
    i = pl.program_id(0)
    nk = vt_scr.shape[0]
    per = BLOCK // k_ref.shape[1]

    @pl.when(i == 0)
    def _():
        for j in range(nk):
            vt_scr[j] = v_ref[j * per:(j + 1) * per].reshape(BLOCK, LANES).astype(F32).T

    q = q_ref[0] * jnp.asarray(0.125, BF)
    qst = stack_cols(q.T)
    start = jnp.concatenate([start_ref[0], start_ref[0]], axis=1)
    length = jnp.concatenate([len_ref[0], len_ref[0]], axis=1)
    lo, hi = lo_ref[i], hi_ref[i]
    width = 2 * BLOCK

    def first(j, m8):
        k = k_ref[pl.ds(j * per, per)].reshape(BLOCK, LANES)
        s = dot(k, qst)
        s = jnp.where(allowed_mask(j, start, length), s, MASKED)
        s_scr[pl.ds(pl.multiple_of(j * BLOCK, BLOCK), BLOCK)] = s
        return jnp.maximum(m8, jnp.max(s.reshape(BLOCK // 8, 8, width), axis=0))

    m8 = lax.fori_loop(lo, hi, first, jnp.full((8, width), MASKED, F32))
    m = jnp.max(m8, axis=0, keepdims=True)
    o_scr[...] = jnp.zeros_like(o_scr)

    def second(j, l8):
        p = jnp.exp(s_scr[pl.ds(pl.multiple_of(j * BLOCK, BLOCK), BLOCK)] - m)
        o_scr[...] += dot(vt_scr[j].astype(BF), p.astype(BF))
        return l8 + jnp.sum(p.reshape(BLOCK // 8, 8, width), axis=0)

    l8 = lax.fori_loop(lo, hi, second, jnp.zeros((8, width), F32))
    l = jnp.sum(l8, axis=0, keepdims=True)
    lse_ref[0] = m + jnp.log(l)
    ot = unstack_cols(o_scr[...] * (1.0 / l))
    o_ref[0] = ot.T.astype(BF)


def attn_bwd_kernel(wide, lo_ref, hi_ref, start_ref, len_ref, lse_ref, q_ref, k_ref, v_ref, o_ref,
                    do_ref, out_ref, kt_scr, dq_scr, dk_scr, dv_scr):
    i = pl.program_id(0)
    nk = kt_scr.shape[0]
    kb = k_ref.shape[1]
    per = BLOCK // kb

    @pl.when(i == 0)
    def _():
        for j in range(nk):
            kt_scr[j] = k_ref[j * per:(j + 1) * per].reshape(BLOCK, LANES).astype(F32).T
        dk_scr[...] = jnp.zeros_like(dk_scr)
        dv_scr[...] = jnp.zeros_like(dv_scr)

    q = q_ref[0] * jnp.asarray(0.125, BF)
    do = do_ref[0]
    qs, qst = stack_rows(q), stack_cols(q.T)
    dot_t = do.T
    dos, dost = stack_rows(do), stack_cols(dot_t)
    prod = dot_t.astype(F32) * o_ref[0].T.astype(F32)
    delta = jnp.concatenate(
        [
            jnp.sum(prod[:HALF], axis=0, keepdims=True),
            jnp.sum(prod[HALF:], axis=0, keepdims=True),
        ],
        axis=1,
    )
    lse = lse_ref[0]
    start = jnp.concatenate([start_ref[0], start_ref[0]], axis=1)
    length = jnp.concatenate([len_ref[0], len_ref[0]], axis=1)
    dq_scr[...] = jnp.zeros_like(dq_scr)

    def body(j, carry):
        k = k_ref[pl.ds(j * per, per)].reshape(BLOCK, LANES)
        v = v_ref[pl.ds(j * per, per)].reshape(BLOCK, LANES)
        s = jnp.where(allowed_mask(j, start, length), dot(k, qst), MASKED)
        p = jnp.exp(s - lse)
        ds = (p * (dot(v, dost) - delta)).astype(BF)
        rows = pl.ds(pl.multiple_of(j * BLOCK, BLOCK), BLOCK)
        dv_scr[rows] += dot(p.astype(BF), dos)
        dk_scr[rows] += dot(ds, qs)
        dq_scr[...] += dot(kt_scr[j].astype(BF), ds)
        return carry

    lax.fori_loop(lo_ref[i], hi_ref[i], body, 0)
    dq = (unstack_cols(dq_scr[...]) * 0.125).T.astype(BF)
    if wide:
        out_ref[i, :, :LANES] = dq
    else:
        out_ref[i, :BLOCK] = dq

    @pl.when(i == pl.num_programs(0) - 1)
    def _():
        n = GROUPS
        dk = dk_scr[...].astype(BF).reshape(n, kb, LANES)
        dv = dv_scr[...].astype(BF).reshape(n, kb, LANES)
        if wide:
            out_ref[:, :, LANES:2 * LANES] = dk
            out_ref[:, :, 2 * LANES:] = dv
        else:
            out_ref[:, BLOCK:BLOCK + kb] = dk
            out_ref[:, BLOCK + kb:] = dv


def row_spec(n):
    return pl.BlockSpec((1, 1, n), lambda i, lo, hi: (i, 0, 0))


def block_rows():
    return pl.BlockSpec((1, BLOCK, LANES), lambda i, lo, hi: (i, 0, 0))


def key_specs(kshape, kblock, vblock):
    return [
        pl.BlockSpec(kshape, lambda i, lo, hi: kblock),
        pl.BlockSpec(kshape, lambda i, lo, hi: vblock),
    ]


def attend_fwd(plan, q, kv, keys_at):
    lo, hi, start, length = plan
    nq = lo.shape[0]
    keys = keys_at[0][0] * keys_at[0][1]
    return pl.pallas_call(
        attn_fwd_kernel,
        grid_spec=pltpu.PrefetchScalarGridSpec(
            num_scalar_prefetch=2,
            grid=(nq,),
            in_specs=[row_spec(BLOCK), row_spec(BLOCK), block_rows()] + key_specs(*keys_at),
            out_specs=[block_rows(), row_spec(2 * BLOCK)],
            scratch_shapes=[
                pltpu.VMEM((keys // BLOCK, LANES, BLOCK), F32),
                pltpu.VMEM((keys, 2 * BLOCK), F32),
                pltpu.VMEM((LANES, 2 * BLOCK), F32),
            ],
        ),
        out_shape=[
            jax.ShapeDtypeStruct((nq, BLOCK, LANES), BF),
            jax.ShapeDtypeStruct((nq, 1, 2 * BLOCK), F32),
        ],
        compiler_params=params(),
        cost_estimate=cost(8e9, 4e6),
    )(lo, hi, start, length, q, kv, kv)


def attend_bwd(plan, lse, q, kv, out, grad, keys_at, wide):
    lo, hi, start, length = plan
    nq = lo.shape[0]
    keys = keys_at[0][0] * keys_at[0][1]
    shape = (nq, BLOCK, 3 * LANES) if wide else (nq, BLOCK + 2 * keys_at[0][1], LANES)
    return pl.pallas_call(
        functools.partial(attn_bwd_kernel, wide),
        grid_spec=pltpu.PrefetchScalarGridSpec(
            num_scalar_prefetch=2,
            grid=(nq,),
            in_specs=[row_spec(BLOCK), row_spec(BLOCK), row_spec(2 * BLOCK), block_rows()]
            + key_specs(*keys_at)
            + [block_rows(), block_rows()],
            out_specs=pl.BlockSpec(shape, lambda i, lo, hi: (0, 0, 0)),
            scratch_shapes=[
                pltpu.VMEM((keys // BLOCK, LANES, BLOCK), F32),
                pltpu.VMEM((LANES, 2 * BLOCK), F32),
                pltpu.VMEM((keys, LANES), F32),
                pltpu.VMEM((keys, LANES), F32),
            ],
        ),
        out_shape=jax.ShapeDtypeStruct(shape, BF),
        compiler_params=params(),
        cost_estimate=cost(8e9, 6e6),
    )(lo, hi, start, length, lse, q, kv, kv, out, grad)


def key_plan(query_ids, key_ids, causal):
    start = jnp.sum((key_ids[None, :] < query_ids[:, None]).astype(jnp.int32), axis=1)
    if causal:
        end = jnp.arange(query_ids.shape[0], dtype=jnp.int32) + 1
    else:
        end = jnp.sum((key_ids[None, :] <= query_ids[:, None]).astype(jnp.int32), axis=1)
    start = start.reshape(-1, 1, BLOCK)
    end = end.reshape(-1, 1, BLOCK)
    lo = jnp.min(start, axis=(1, 2)) // BLOCK
    hi = (jnp.max(end, axis=(1, 2)) + BLOCK - 1) // BLOCK
    return lo, hi, start, end - start


def params():
    return pltpu.CompilerParams(vmem_limit_bytes=44 * 2**20)


def cost(flops, size):
    return pl.CostEstimate(flops=int(flops), bytes_accessed=int(size), transcendentals=0)


def norm_forward(values, gain, shift):
    centered = values - jnp.mean(values, axis=-1, keepdims=True)
    inverse = lax.rsqrt(jnp.mean(centered * centered, axis=-1, keepdims=True) + EPS)
    normed = centered * inverse
    return normed * gain + shift, normed, inverse


def column_sum(x):
    return jnp.sum(x, axis=0, keepdims=True)


def norm_backward(upstream, normed, inverse, gain):
    scaled = upstream * gain
    inner = (
        scaled
        - jnp.mean(scaled, axis=-1, keepdims=True)
        - normed * jnp.mean(scaled * normed, axis=-1, keepdims=True)
    )
    return inverse * inner, column_sum(upstream * normed), column_sum(upstream)


PLACES = tuple(yh * 8 + yl * 4 + x for yh in range(2) for x in range(4) for yl in range(2))


def rows_of(ref):
    return jnp.concatenate([ref[p, 0] for p in PLACES], axis=0)


def plane_rows(ref):
    return ref[:, 0].reshape(512, ref.shape[3])


def put_rows(ref, value, other=None):
    for i, p in enumerate(PLACES):
        piece = value[i * 32:(i + 1) * 32]
        if other is not None:
            piece = piece + other[p, 0].astype(F32)
        ref[p, 0] = piece.astype(ref.dtype)


def halves(core, x):
    n = x.shape[1] // 2
    a, b = x[:, :n], x[:, n:]
    first = core == 0
    return jnp.where(first, a, b), jnp.where(first, b, a)


def ordered(core, mine, theirs):
    first = core == 0
    return jnp.concatenate(
        [jnp.where(first, mine, theirs), jnp.where(first, theirs, mine)], axis=1
    )


def joined(ref, first=0, count=None):
    count = ref.shape[1] if count is None else count
    return jnp.concatenate([ref[g, first:first + count] for g in range(GROUPS)], axis=1)


def put_groups(ref, value):
    for g in range(GROUPS):
        ref[g] = value[:, g * LANES:(g + 1) * LANES].astype(ref.dtype)


def qkv_kernel(core_ref, x_ref, own_tile_ref, other_tile_ref, own_ref, other_ref,
               qkv_ref, a1_ref, vec_ref):
    g = pl.program_id(0)
    core = core_ref[0]

    @pl.when(g == 0)
    def _():
        own = own_tile_ref[...].astype(F32).T[:16]
        other = other_tile_ref[...].astype(F32).T[:16]
        vec = ordered(core, own, other)
        vec_ref[...] = vec
        a, _, _ = norm_forward(x_ref[...].astype(F32), vec[0:1], vec[4:5])
        mine, theirs = halves(core, a)
        a1_ref[0] = mine.astype(BF)
        a1_ref[1] = theirs.astype(BF)

    y = dot(a1_ref[0], own_ref[...]) + dot(a1_ref[1], other_ref[...])
    at = pl.ds(pl.multiple_of(g * LANES, LANES), LANES)
    bias = jnp.concatenate(
        [vec_ref[8:9, at], jnp.zeros((1, LANES), F32), vec_ref[9:10, at]], axis=1
    )
    qkv_ref[0] = (y + bias).astype(BF)


def text_kernel(core_ref, enc_ref, vec_ref, own_ref, other_ref, out_ref):
    m = pl.program_id(0)
    mine, theirs = halves(core_ref[0], enc_ref[...])
    y = dot(mine, rows_of(own_ref)) + dot(theirs, rows_of(other_ref))
    put_groups(out_ref, y + vec_ref[12:13] * m.astype(F32))


def middle_kernel(core_ref, o1_ref, x_ref, vec_ref, wo_own, wo_other, wq_own, wq_other,
                  x1_ref, a2_ref, q2_ref):
    core = core_ref[0]
    mine, theirs = halves(core, joined(o1_ref))
    x1 = (
        x_ref[...].astype(F32)
        + dot(mine, rows_of(wo_own))
        + dot(theirs, rows_of(wo_other))
        + vec_ref[10:11]
    )
    x1_ref[...] = x1
    a, _, _ = norm_forward(x1, vec_ref[1:2], vec_ref[5:6])
    mine, theirs = halves(core, a)
    mine, theirs = mine.astype(BF), theirs.astype(BF)
    a2_ref[0] = mine
    a2_ref[1] = theirs
    q2 = dot(mine, rows_of(wq_own)) + dot(theirs, rows_of(wq_other)) + vec_ref[11:12]
    put_groups(q2_ref, q2)


def ffn_kernel(core_ref, o2_ref, x1_ref, vec_ref, upb_ref, cot_ref, wo_own, wo_other,
               up_own, up_other, dn_own, dn_other,
               out_ref, g2_ref, e2_ref, do2_ref, a3_ref, e3_ref, hid_ref, ep_ref, small_ref,
               dupb_ref, gup_ref, gdn_ref,
               x2_scr, acc_scr, pre_scr, hid_scr, da_scr, dh_scr, a3t_scr):
    s = pl.program_id(0)
    t = lax.rem(s, 8)
    core = core_ref[0]

    @pl.when(s == 0)
    def _():
        mine, theirs = halves(core, joined(o2_ref))
        x2 = (
            x1_ref[...]
            + dot(mine, rows_of(wo_own))
            + dot(theirs, rows_of(wo_other))
            + vec_ref[13:14]
        )
        x2_scr[...] = x2
        a, _, _ = norm_forward(x2, vec_ref[2:3], vec_ref[6:7])
        mine, theirs = halves(core, a)
        a3_ref[0] = mine.astype(BF)
        a3_ref[1] = theirs.astype(BF)
        acc_scr[...] = jnp.zeros_like(acc_scr)

    @pl.when(s < 8)
    def _():
        pre = dot(a3_ref[0], rows_of(up_own)) + dot(a3_ref[1], rows_of(up_other)) + upb_ref[...]
        pre_scr[t] = pre
        hidden = (pre * jax.nn.sigmoid(pre)).astype(BF)
        hid_scr[t] = hidden

        @pl.when(t < 4)
        def _():
            acc_scr[...] += dot(hidden, plane_rows(dn_own))

        @pl.when(t >= 4)
        def _():
            acc_scr[...] += dot(hidden, plane_rows(dn_other))

    @pl.when(s == 7)
    def _():
        x3 = x2_scr[...] + acc_scr[...] + vec_ref[14:15]
        y, n4, r4 = norm_forward(x3, vec_ref[3:4], vec_ref[7:8])
        out_ref[...] = y
        g3, dgain, dshift = norm_backward(cot_ref[...].astype(F32), n4, r4, vec_ref[3:4])
        acc_scr[...] = g3
        e3_ref[...] = g3.astype(BF)
        small_ref[0:1] = dgain
        small_ref[1:2] = dshift
        small_ref[2:3] = column_sum(g3)
        da_scr[...] = jnp.zeros_like(da_scr)
        a3t_scr[...] = a3_ref[1].astype(F32).T

    @pl.when(s >= 8)
    def _():
        e3 = e3_ref[...]

        @pl.when(t < 4)
        def _():
            dh_scr[...] = dot_nt(e3, plane_rows(dn_own))
            hid_ref[...] = hid_scr[t]

        @pl.when(t >= 4)
        def _():
            dh_scr[...] = dot_nt(e3, plane_rows(dn_other))
            gdn_ref[:, 0] = dot_tn(hid_scr[t], e3).astype(BF).reshape(16, 32, D)

        pre = pre_scr[t]
        sig = jax.nn.sigmoid(pre)
        dpre = dh_scr[...] * sig * (1.0 + pre * (1.0 - sig))
        ep = dpre.astype(BF)
        ep_ref[...] = ep
        dupb_ref[...] = column_sum(dpre)
        put_rows(gup_ref, dot(a3t_scr[...].astype(BF), ep))
        da_scr[0] += dot_nt(ep, rows_of(up_own))
        da_scr[1] += dot_nt(ep, rows_of(up_other))

    @pl.when(s == 15)
    def _():
        da3 = ordered(core, da_scr[0], da_scr[1])
        _, n3, r3 = norm_forward(x2_scr[...], vec_ref[2:3], vec_ref[6:7])
        back, dgain, dshift = norm_backward(da3, n3, r3, vec_ref[2:3])
        g2 = acc_scr[...] + back
        g2_ref[...] = g2
        small_ref[3:4] = dgain
        small_ref[4:5] = dshift
        small_ref[5:6] = column_sum(g2)
        e2 = g2.astype(BF)
        e2_ref[...] = e2
        put_groups(
            do2_ref, ordered(core, dot_nt(e2, rows_of(wo_own)), dot_nt(e2, rows_of(wo_other)))
        )


def ffn_grad_kernel(core_ref, a3_ref, ep_ref, hid_ref, e3_ref, up_ref, dn_ref, out_ref):
    m = pl.program_id(0)

    @pl.when(m < 4)
    def _():
        put_rows(out_ref, dot_tn(a3_ref[0], ep_ref[...]), up_ref)

    @pl.when(m >= 4)
    def _():
        g = dot_tn(hid_ref[...], e3_ref[...]).reshape(16, 32, D)
        out_ref[:, 0] = (g + dn_ref[:, 0].astype(F32)).astype(BF)


def cross_back_kernel(core_ref, b2_ref, x1_ref, g2_ref, vec_ref, wq_own, wq_other,
                      wo_own, wo_other, g1_ref, e1_ref, do1_ref, small_ref):
    core = core_ref[0]
    dq = joined(b2_ref, 0, BLOCK)
    da2 = ordered(core, dot_nt(dq, rows_of(wq_own)), dot_nt(dq, rows_of(wq_other)))
    _, n2, r2 = norm_forward(x1_ref[...], vec_ref[1:2], vec_ref[5:6])
    back, dgain, dshift = norm_backward(da2, n2, r2, vec_ref[1:2])
    g1 = g2_ref[...] + back
    g1_ref[...] = g1
    e1 = g1.astype(BF)
    e1_ref[...] = e1
    put_groups(
        do1_ref, ordered(core, dot_nt(e1, rows_of(wo_own)), dot_nt(e1, rows_of(wo_other)))
    )
    small_ref[0:1] = dgain
    small_ref[1:2] = dshift
    small_ref[2:3] = column_sum(g1)
    small_ref[3:4] = column_sum(dq.astype(F32))
    small_ref[4:5] = column_sum(joined(b2_ref, BLOCK + 128, 128).astype(F32))


def text_back_kernel(core_ref, b2_ref, wk_own, wk_other, wv_own, wv_other, out_ref):
    dk = joined(b2_ref, BLOCK, 128)
    dv = joined(b2_ref, BLOCK + 128, 128)
    mine = dot_nt(dk, rows_of(wk_own)) + dot_nt(dv, rows_of(wv_own))
    theirs = dot_nt(dk, rows_of(wk_other)) + dot_nt(dv, rows_of(wv_other))
    out_ref[...] = ordered(core_ref[0], mine, theirs)


def attn_grad_kernel(half, core_ref, a2_ref, enc_ref, o1_ref, o2_ref, b2_ref, e1_ref, e2_ref,
                     *rest):
    other = rest[0] if len(rest) == 2 else None
    out_ref = rest[-1]
    core = core_ref[0]
    m = pl.program_id(0)

    def emit(at, a, g):
        @pl.when(m == at)
        def _():
            put_rows(out_ref, dot_tn(a(), g()), other)

    emit(0, lambda: a2_ref[half], lambda: joined(b2_ref, 0, BLOCK))
    emit(1, lambda: halves(core, enc_ref[...])[half], lambda: joined(b2_ref, BLOCK, 128))
    emit(2, lambda: halves(core, enc_ref[...])[half], lambda: joined(b2_ref, BLOCK + 128, 128))
    emit(3, lambda: halves(core, joined(o1_ref))[half], lambda: e1_ref[...])
    emit(4, lambda: halves(core, joined(o2_ref))[half], lambda: e2_ref[...])


def self_grad_kernel(a1_ref, d_ref, out_ref):
    a = a1_ref[1]
    for g in range(GROUPS):
        out_ref[:, g * 384:(g + 1) * 384] = dot_tn(a, d_ref[g]).astype(BF)


def self_grad_own_kernel(a1_ref, d_ref, recv_ref, small_ref, small_recv_ref, out_ref):
    a = a1_ref[0]
    for g in range(GROUPS):
        at = slice(g * 384, (g + 1) * 384)
        out_ref[:, at] = (dot_tn(a, d_ref[g]) + recv_ref[:, at].astype(F32)).astype(BF)
    out_ref[:, 3 * D:] = (small_ref[...] + small_recv_ref[...].astype(F32)).astype(BF)


def self_back_kernel(core_ref, d_ref, own_ref, other_ref, x_ref, g1_ref, vec_ref,
                     out_ref, small_ref, sum_ref, da_scr):
    g = pl.program_id(0)

    @pl.when(g == 0)
    def _():
        da_scr[...] = jnp.zeros_like(da_scr)

    d = d_ref[0]
    sum_ref[0] = column_sum(d.astype(F32))
    da_scr[0] += dot_nt(d, own_ref[...])
    da_scr[1] += dot_nt(d, other_ref[...])

    @pl.when(g == pl.num_programs(0) - 1)
    def _():
        da1 = ordered(core_ref[0], da_scr[0], da_scr[1])
        _, n1, r1 = norm_forward(x_ref[...].astype(F32), vec_ref[0:1], vec_ref[4:5])
        back, dgain, dshift = norm_backward(da1, n1, r1, vec_ref[0:1])
        out_ref[...] = g1_ref[...] + back
        small_ref[0:1] = dgain
        small_ref[1:2] = dshift


def whole(shape):
    return pl.BlockSpec(shape, lambda *a: (0,) * len(shape))


def matrix(m):
    return pl.BlockSpec((16, 1, 32, D), lambda *a: (0, m, 0, 0))


def call(kernel, grid, in_specs, out_specs, out_shape, scratch, flops, size):
    return pl.pallas_call(
        kernel,
        grid_spec=pltpu.PrefetchScalarGridSpec(
            num_scalar_prefetch=1,
            grid=grid,
            in_specs=in_specs,
            out_specs=out_specs,
            scratch_shapes=scratch,
        ),
        out_shape=out_shape,
        compiler_params=params(),
        cost_estimate=cost(flops, size),
    )


def shape(dims, dtype=BF):
    return jax.ShapeDtypeStruct(dims, dtype)


def by_core(x):
    lead = x.shape[:-1]
    return x.reshape(*lead, 8, 2, HALF).swapaxes(-3, -2).reshape(*lead, D)


def by_place(x):
    lead = x.shape[:-1]
    return x.reshape(*lead, 2, 8, HALF).swapaxes(-3, -2).reshape(*lead, D)


def swap(x):
    return lax.ppermute(x, "c", [(0, 1), (1, 0)])


def local(
    tokens,
    encoded,
    unit_ids,
    text_ids,
    cotangent,
    attn_in,
    attn_out,
    w_up,
    w_down,
    norm_gains,
    shifts,
    biases,
    up_bias,
):
    core = lax.axis_index("c")
    first_core = core == 0
    core_arg = core.astype(jnp.int32).reshape(1)
    rows = tokens.shape[1]
    text_rows = encoded.shape[1]

    def mine(x):
        return lax.dynamic_slice_in_dim(x, core * (x.shape[0] // 2), x.shape[0] // 2, 0)

    def theirs(x):
        return lax.dynamic_slice_in_dim(x, (1 - core) * (x.shape[0] // 2), x.shape[0] // 2, 0)

    in_low = by_core(attn_in.astype(BF))
    out_low = by_core(attn_out.astype(BF))
    self_cols = (
        in_low[0:3].reshape(3, 8, GROUPS, LANES).transpose(1, 2, 0, 3).reshape(8, 3 * D)
    )
    vectors = jnp.concatenate([norm_gains, shifts, biases], axis=0).astype(BF)
    tile = jnp.concatenate(
        [
            vectors.T,
            up_bias.astype(BF).reshape(8, 4),
            jnp.zeros((8, 13), BF),
            unit_ids.reshape(8, 32).astype(BF),
            text_ids.reshape(8, 16).astype(BF),
            jnp.zeros((8, 48), BF),
        ],
        axis=1,
    )
    first_pack = jnp.concatenate([self_cols, tile], axis=1)
    width = 3 * D + LANES
    first_all = lax.all_to_all(
        jnp.broadcast_to(first_pack[None], (64, 8, width)), CHIPS, 0, 0, tiled=True
    )
    self_own = first_all.reshape(512, width)
    self_other = swap(self_own)

    up_low = w_up.astype(BF).reshape(8, 2, 4, 2, 2, 4, 32).transpose(0, 3, 5, 1, 4, 2, 6)
    up_low = up_low.reshape(8, 4, D).transpose(1, 0, 2).reshape(32, D)
    down_low = by_core(w_down.astype(BF))
    attn_low = jnp.concatenate([in_low[3:6], out_low], axis=0).reshape(40, D)
    z_pack = jnp.concatenate([up_low, down_low, attn_low], axis=0)
    z_all = lax.all_gather(z_pack, "z", axis=0, tiled=False)
    attn_z = z_all[:, 64:].reshape(4, 5, 8, D).transpose(1, 0, 2, 3).reshape(1, 5, 32, D)
    up_z = z_all[:, :32].reshape(4, 4, 8, D).transpose(1, 0, 2, 3).reshape(4, 32, D)
    ffn_z = jnp.concatenate([up_z, z_all[:, 32:64]], axis=0)[None]
    attn_own = lax.all_gather(attn_z, PLANE, axis=0, tiled=True)
    attn_other = swap(attn_own)
    ffn_own = lax.all_gather(ffn_z, PLANE, axis=0, tiled=True)
    ffn_other = swap(ffn_own)

    x = by_core(tokens[0])
    enc = by_core(encoded[0])
    cot = by_core(cotangent[0])

    tile_own, tile_other = self_own[:, 3 * D:], self_other[:, 3 * D:]

    def up_part(t):
        return t[:, 15:19].reshape(2, 4, 2, 4, 32).transpose(3, 0, 2, 1, 4).reshape(1, 2048)

    up_own, up_other = up_part(tile_own), up_part(tile_other)
    up_vec = jnp.concatenate(
        [jnp.where(first_core, up_own, up_other), jnp.where(first_core, up_other, up_own)], axis=1
    ).astype(F32)
    place = lax.axis_index(("yh", "x"))
    seq_tile = lax.dynamic_slice_in_dim(tile_own, place * 64, 64, 0)
    seq_tile = seq_tile.reshape(8, 8, LANES).astype(F32).astype(jnp.int32)
    units = seq_tile[:, :, 32:64].reshape(-1)
    texts = seq_tile[:, :, 64:80].reshape(-1)
    self_plan = key_plan(units, units, True)
    cross_plan = key_plan(units, texts, False)

    qkv, a1, vec = call(
        qkv_kernel,
        (GROUPS,),
        [
            whole((rows, D)),
            pl.BlockSpec((512, LANES), lambda g, c: (0, 24)),
            pl.BlockSpec((512, LANES), lambda g, c: (0, 24)),
            pl.BlockSpec((512, 384), lambda g, c: (0, g)),
            pl.BlockSpec((512, 384), lambda g, c: (0, g)),
        ],
        [
            pl.BlockSpec((1, rows, 384), lambda g, c: (g, 0, 0)),
            whole((2, rows, 512)),
            whole((16, D)),
        ],
        [shape((GROUPS, rows, 384)), shape((2, rows, 512)), shape((16, D), F32)],
        [],
        1.6e9,
        8e6,
    )(core_arg, x, self_own, self_other, self_own, self_other)
    qkv = lax.all_to_all(qkv, SEQ, 0, 0, tiled=True)
    self_keys = ((GROUPS, rows, LANES), (0, 0, 1), (0, 0, 2))
    o1_heads, lse1 = attend_fwd(self_plan, qkv, qkv, self_keys)
    o1 = lax.all_to_all(o1_heads, SEQ, 0, 0, tiled=True)

    kv2 = call(
        text_kernel,
        (2,),
        [
            whole((text_rows, D)),
            whole((16, D)),
            pl.BlockSpec((16, 1, 32, D), lambda m, c: (0, 1 + m, 0, 0)),
            pl.BlockSpec((16, 1, 32, D), lambda m, c: (0, 1 + m, 0, 0)),
        ],
        pl.BlockSpec((GROUPS, text_rows, LANES), lambda m, c: (0, m, 0)),
        shape((GROUPS, 2 * text_rows, LANES)),
        [],
        0.5e9,
        4e6,
    )(core_arg, enc, vec, attn_own, attn_other)
    kv2 = lax.all_to_all(kv2, SEQ, 0, 0, tiled=True)

    x1, a2, q2 = call(
        middle_kernel,
        (1,),
        [whole((GROUPS, rows, LANES)), whole((rows, D)), whole((16, D))]
        + [matrix(3), matrix(3), matrix(0), matrix(0)],
        [whole((rows, D)), whole((2, rows, 512)), whole((GROUPS, rows, LANES))],
        [shape((rows, D), F32), shape((2, rows, 512)), shape((GROUPS, rows, LANES))],
        [],
        1.1e9,
        8e6,
    )(core_arg, o1, x, vec, attn_own, attn_other, attn_own, attn_other)
    q2 = lax.all_to_all(q2, SEQ, 0, 0, tiled=True)
    cross_keys = ((GROUPS, text_rows, LANES), (0, 0, 0), (0, 1, 0))
    o2_heads, lse2 = attend_fwd(cross_plan, q2, kv2, cross_keys)
    o2 = lax.all_to_all(o2_heads, SEQ, 0, 0, tiled=True)

    def block_of(s, c):
        t = lax.rem(s, 8)
        return jnp.where(t < 4, c[0], 1 - c[0]) * 4 + lax.rem(t, 4)

    def back_block(s, c):
        return block_of(jnp.maximum(s, 8), c)

    up_spec = pl.BlockSpec(
        (16, 1, 32, 512), lambda s, c: (0, block_of(s, c) // 2, 0, lax.rem(block_of(s, c), 2))
    )
    gup_spec = pl.BlockSpec(
        (16, 1, 32, 512), lambda s, c: (0, back_block(s, c) // 2, 0, lax.rem(back_block(s, c), 2))
    )
    (layer_out, g2, e2, do2, a3, e3, hidden, ep, small_f, dup_bias, gup, gdn) = call(
        ffn_kernel,
        (16,),
        [
            whole((GROUPS, rows, LANES)),
            whole((rows, D)),
            whole((16, D)),
            pl.BlockSpec((1, 512), lambda s, c: (0, block_of(s, c))),
            whole((rows, D)),
            matrix(4),
            matrix(4),
            up_spec,
            up_spec,
            pl.BlockSpec(
                (16, 1, 32, D), lambda s, c: (0, 4 + jnp.minimum(lax.rem(s, 8), 3), 0, 0)
            ),
            pl.BlockSpec(
                (16, 1, 32, D), lambda s, c: (0, jnp.maximum(lax.rem(s, 8), 4), 0, 0)
            ),
        ],
        [
            whole((rows, D)),
            whole((rows, D)),
            whole((rows, D)),
            whole((GROUPS, rows, LANES)),
            whole((2, rows, 512)),
            whole((rows, D)),
            pl.BlockSpec((rows, 512), lambda s, c: (0, jnp.clip(s - 8, 0, 3))),
            pl.BlockSpec((rows, 512), lambda s, c: (0, back_block(s, c))),
            whole((8, D)),
            pl.BlockSpec((1, 512), lambda s, c: (0, back_block(s, c))),
            gup_spec,
            pl.BlockSpec((16, 1, 32, D), lambda s, c: (0, jnp.maximum(s - 12, 0), 0, 0)),
        ],
        [
            shape((rows, D), F32),
            shape((rows, D), F32),
            shape((rows, D)),
            shape((GROUPS, rows, LANES)),
            shape((2, rows, 512)),
            shape((rows, D)),
            shape((rows, FF // 2)),
            shape((rows, FF)),
            shape((8, D), F32),
            shape((1, FF), F32),
            shape((16, 4, 32, D)),
            shape((16, 4, 32, D)),
        ],
        [
            pltpu.VMEM((rows, D), F32),
            pltpu.VMEM((rows, D), F32),
            pltpu.VMEM((8, rows, 512), F32),
            pltpu.VMEM((8, rows, 512), BF),
            pltpu.VMEM((2, rows, 512), F32),
            pltpu.VMEM((rows, 512), F32),
            pltpu.VMEM((512, rows), F32),
        ],
        16e9,
        50e6,
    )(core_arg, o2, x1, vec, up_vec, cot, attn_own, attn_other, ffn_own, ffn_other,
      ffn_own, ffn_other)
    do2 = lax.all_to_all(do2, SEQ, 0, 0, tiled=True)
    gup_recv, gdn_recv = swap(gup), swap(gdn)

    back2 = attend_bwd(cross_plan, lse2, q2, kv2, o2_heads, do2, cross_keys, False)
    back2 = lax.all_to_all(back2, SEQ, 0, 0, tiled=True)
    ffn_grad = call(
        ffn_grad_kernel,
        (8,),
        [
            whole((2, rows, 512)),
            pl.BlockSpec((rows, D), lambda m, c: (0, jnp.minimum(m, 3))),
            pl.BlockSpec((rows, 512), lambda m, c: (0, jnp.maximum(m - 4, 0))),
            whole((rows, D)),
            pl.BlockSpec((16, 1, 32, D), lambda m, c: (0, jnp.minimum(m, 3), 0, 0)),
            pl.BlockSpec((16, 1, 32, D), lambda m, c: (0, jnp.maximum(m - 4, 0), 0, 0)),
        ],
        pl.BlockSpec((16, 1, 32, D), lambda m, c: (0, m, 0, 0)),
        shape((16, 8, 32, D)),
        [],
        2.2e9,
        20e6,
    )(core_arg, a3, ep, hidden, e3, gup_recv, gdn_recv)
    ffn_grad = lax.psum_scatter(
        ffn_grad.reshape(4096, D), PLANE, scatter_dimension=0, tiled=True
    ).reshape(1, 8, 32, D)

    g1, e1, do1, small_c = call(
        cross_back_kernel,
        (1,),
        [whole((GROUPS, rows + 2 * text_rows, LANES)), whole((rows, D)), whole((rows, D))]
        + [whole((16, D)), matrix(0), matrix(0), matrix(3), matrix(3)],
        [whole((rows, D)), whole((rows, D)), whole((GROUPS, rows, LANES)), whole((8, D))],
        [
            shape((rows, D), F32),
            shape((rows, D)),
            shape((GROUPS, rows, LANES)),
            shape((8, D), F32),
        ],
        [],
        1.1e9,
        10e6,
    )(core_arg, back2, x1, g2, vec, attn_own, attn_other, attn_own, attn_other)
    do1 = lax.all_to_all(do1, SEQ, 0, 0, tiled=True)
    d_enc = call(
        text_back_kernel,
        (1,),
        [whole((GROUPS, rows + 2 * text_rows, LANES))]
        + [matrix(1), matrix(1), matrix(2), matrix(2)],
        whole((text_rows, D)),
        shape((text_rows, D), F32),
        [],
        0.5e9,
        5e6,
    )(core_arg, back2, attn_own, attn_other, attn_own, attn_other)

    def attn_grads(half, recv):
        specs = [
            whole((2, rows, 512)),
            whole((text_rows, D)),
            whole((GROUPS, rows, LANES)),
            whole((GROUPS, rows, LANES)),
            whole((GROUPS, rows + 2 * text_rows, LANES)),
            whole((rows, D)),
            whole((rows, D)),
        ]
        block = pl.BlockSpec((16, 1, 32, D), lambda m, c: (0, m, 0, 0))
        return call(
            functools.partial(attn_grad_kernel, half),
            (5,),
            specs + [block] * len(recv),
            block,
            shape((16, 5, 32, D)),
            [],
            1.1e9,
            8e6,
        )(core_arg, a2, enc, o1, o2, back2, e1, e2, *recv)

    attn_grad = attn_grads(0, [swap(attn_grads(1, []))])
    attn_grad = lax.psum_scatter(
        attn_grad.reshape(2560, D), PLANE, scatter_dimension=0, tiled=True
    ).reshape(1, 5, 32, D)

    dqkv = attend_bwd(self_plan, lse1, qkv, qkv, o1_heads, do1, self_keys, True)
    dqkv = lax.all_to_all(dqkv, SEQ, 0, 0, tiled=True)

    def plain(kernel, out, *args):
        return pl.pallas_call(
            kernel, out_shape=out, compiler_params=params(), cost_estimate=cost(0.8e9, 6e6)
        )(*args)

    self_recv = swap(plain(self_grad_kernel, shape((512, 3 * D)), a1, dqkv))
    d_tokens, small_s, dsum = call(
        self_back_kernel,
        (GROUPS,),
        [
            pl.BlockSpec((1, rows, 384), lambda g, c: (g, 0, 0)),
            pl.BlockSpec((512, 384), lambda g, c: (0, g)),
            pl.BlockSpec((512, 384), lambda g, c: (0, g)),
            whole((rows, D)),
            whole((rows, D)),
            whole((16, D)),
        ],
        [
            whole((rows, D)),
            whole((8, D)),
            pl.BlockSpec((1, 1, 384), lambda g, c: (g, 0, 0)),
        ],
        [shape((rows, D), F32), shape((8, D), F32), shape((GROUPS, 1, 384), F32)],
        [pltpu.VMEM((2, rows, 512), F32)],
        1.6e9,
        9e6,
    )(core_arg, dqkv, self_own, self_other, x, g1, vec)

    dsum = dsum.reshape(GROUPS, 3, LANES)
    small = jnp.concatenate(
        [
            small_s[0:1],
            small_c[0:1],
            small_f[3:4],
            small_f[0:1],
            small_s[1:2],
            small_c[1:2],
            small_f[4:5],
            small_f[1:2],
            dsum[:, 0].reshape(1, D),
            dsum[:, 2].reshape(1, D),
            small_c[2:3],
            small_c[3:4],
            small_c[4:5],
            small_f[5:6],
            small_f[2:3],
        ],
        axis=0,
    )
    up_sums = dup_bias.reshape(2, 4, 2, 2, 4, 32).transpose(0, 2, 4, 3, 1, 5).reshape(D, 4)
    small = jnp.concatenate([small.T, up_sums, jnp.zeros((D, LANES - 19), F32)], axis=1)
    small_recv = swap(theirs(small).astype(BF))
    last = plain(
        self_grad_own_kernel, shape((512, width)), a1, dqkv, self_recv, mine(small), small_recv
    )
    last = lax.all_to_all(last.reshape(64, 8, width), CHIPS, 0, 0, tiled=True)
    last = jnp.sum(last.astype(F32), axis=0)

    ffn_grad, attn_grad = ffn_grad[0], attn_grad[0]
    z_grad = jnp.concatenate(
        [
            ffn_grad[:4].reshape(4, 4, 8, D).transpose(1, 0, 2, 3).reshape(4, 32, D),
            ffn_grad[4:],
            attn_grad.reshape(5, 4, 8, D).transpose(1, 0, 2, 3).reshape(4, 40, D),
        ],
        axis=1,
    )
    z_grad = lax.all_to_all(z_grad, "z", 0, 0, tiled=True)
    z_grad = jnp.sum(z_grad.astype(F32), axis=0)
    d_up = z_grad[:32].reshape(4, 8, D).transpose(1, 0, 2).reshape(8, 2, 4, 2, 2, 4, 32)
    d_up = d_up.transpose(0, 3, 5, 1, 4, 2, 6).reshape(8, FF)
    d_down = by_place(z_grad[32:64])
    attn_grad = z_grad[64:].reshape(5, 8, D)
    d_self = last[:, :3 * D].reshape(8, GROUPS, 3, LANES).transpose(2, 0, 1, 3).reshape(3, 8, D)
    d_in = by_place(jnp.concatenate([d_self, attn_grad[:3]], axis=0))
    d_out = by_place(attn_grad[3:])
    d_vec = last[:, 3 * D:3 * D + 15].T
    d_up_bias = last[:, 3 * D + 15:3 * D + 19].reshape(32)
    return (
        by_place(layer_out)[None],
        by_place(d_tokens)[None],
        by_place(d_enc)[None],
        d_in,
        d_out,
        d_up,
        d_down,
        d_vec[0:4],
        d_vec[4:8],
        d_vec[8:15],
        d_up_bias,
    )


def solution(mesh):
    fine = Mesh(mesh.devices.reshape(2, 4, 2, 2, 4), ("yh", "x", "c", "yl", "z"))
    fsdp = ("yh", "x", "c")
    every = fsdp + SEQ
    placed = (
        P(fsdp, SEQ, None),
        P(fsdp, SEQ, None),
        P(fsdp, SEQ),
        P(fsdp, SEQ),
        P(fsdp, SEQ, None),
        P(None, every, None),
        P(None, every, None),
        P(every, None),
        P(every, None),
        P(None, every),
        P(None, every),
        P(None, every),
        P(every),
    )
    return jax.shard_map(
        local,
        mesh=fine,
        in_specs=placed,
        out_specs=(
            P(fsdp, SEQ, None),
            P(fsdp, SEQ, None),
            P(fsdp, SEQ, None),
            P(None, every, None),
            P(None, every, None),
            P(every, None),
            P(every, None),
            P(None, every),
            P(None, every),
            P(None, every),
            P(every),
        ),
        check_vma=False,
    )
```

```python
import functools

import jax
import jax.numpy as jnp
from jax import lax
from jax.experimental import pallas as pl
from jax.experimental.pallas import tpu as pltpu
from jax.sharding import Mesh
from jax.sharding import PartitionSpec as P

D = 1024
FF = 4096
GROUPS = 8
LANES = 128
HALF = 64
BLOCK = 256
EPS = 1e-05
MASKED = -1e30

SEQ = ("yl", "z")
CHIPS = ("yh", "x", "yl", "z")
PLANE = ("yh", "yl", "x")
BF = jnp.bfloat16
F32 = jnp.float32


def dot(a, b):
    return jnp.dot(a, b, preferred_element_type=F32)


def dot_nt(a, b):
    return lax.dot_general(a, b, (((1,), (1,)), ((), ())), preferred_element_type=F32)


def dot_tn(a, b):
    return lax.dot_general(a, b, (((0,), (0,)), ((), ())), preferred_element_type=F32)


def stack_cols(xt):
    zero = jnp.zeros((HALF, xt.shape[1]), xt.dtype)
    return jnp.concatenate(
        [
            jnp.concatenate([xt[:HALF], zero], axis=0),
            jnp.concatenate([zero, xt[HALF:]], axis=0),
        ],
        axis=1,
    )


def stack_rows(x):
    lane = lax.broadcasted_iota(jnp.int32, x.shape, 1)
    zero = jnp.zeros_like(x)
    return jnp.concatenate(
        [jnp.where(lane < HALF, x, zero), jnp.where(lane < HALF, zero, x)], axis=0
    )


def unstack_cols(xt):
    n = xt.shape[1] // 2
    return jnp.concatenate([xt[:HALF, :n], xt[HALF:, n:]], axis=0)


def allowed_mask(j, start, length):
    pos = lax.broadcasted_iota(jnp.int32, (BLOCK, start.shape[1]), 0) + j * BLOCK
    off = pos - start
    return (off >= 0) & (off < length)


def attn_fwd_kernel(lo_ref, hi_ref, start_ref, len_ref, q_ref, k_ref, v_ref, o_ref, lse_ref,
                    vt_scr, s_scr, o_scr):
    i = pl.program_id(0)
    nk = vt_scr.shape[0]
    per = BLOCK // k_ref.shape[1]

    @pl.when(i == 0)
    def _():
        for j in range(nk):
            vt_scr[j] = v_ref[j * per:(j + 1) * per].reshape(BLOCK, LANES).astype(F32).T

    q = q_ref[0] * jnp.asarray(0.125, BF)
    qst = stack_cols(q.T)
    start = jnp.concatenate([start_ref[0], start_ref[0]], axis=1)
    length = jnp.concatenate([len_ref[0], len_ref[0]], axis=1)
    lo, hi = lo_ref[i], hi_ref[i]
    width = 2 * BLOCK

    def first(j, m8):
        k = k_ref[pl.ds(j * per, per)].reshape(BLOCK, LANES)
        s = dot(k, qst)
        s = jnp.where(allowed_mask(j, start, length), s, MASKED)
        s_scr[pl.ds(pl.multiple_of(j * BLOCK, BLOCK), BLOCK)] = s
        return jnp.maximum(m8, jnp.max(s.reshape(BLOCK // 8, 8, width), axis=0))

    m8 = lax.fori_loop(lo, hi, first, jnp.full((8, width), MASKED, F32))
    m = jnp.max(m8, axis=0, keepdims=True)
    o_scr[...] = jnp.zeros_like(o_scr)

    def second(j, l8):
        p = jnp.exp(s_scr[pl.ds(pl.multiple_of(j * BLOCK, BLOCK), BLOCK)] - m)
        o_scr[...] += dot(vt_scr[j].astype(BF), p.astype(BF))
        return l8 + jnp.sum(p.reshape(BLOCK // 8, 8, width), axis=0)

    l8 = lax.fori_loop(lo, hi, second, jnp.zeros((8, width), F32))
    l = jnp.sum(l8, axis=0, keepdims=True)
    lse_ref[0] = m + jnp.log(l)
    ot = unstack_cols(o_scr[...] * (1.0 / l))
    o_ref[0] = ot.T.astype(BF)


def attn_bwd_kernel(wide, lo_ref, hi_ref, start_ref, len_ref, lse_ref, q_ref, k_ref, v_ref, o_ref,
                    do_ref, out_ref, kt_scr, dq_scr, dk_scr, dv_scr):
    i = pl.program_id(0)
    nk = kt_scr.shape[0]
    kb = k_ref.shape[1]
    per = BLOCK // kb

    @pl.when(i == 0)
    def _():
        for j in range(nk):
            kt_scr[j] = k_ref[j * per:(j + 1) * per].reshape(BLOCK, LANES).astype(F32).T
        dk_scr[...] = jnp.zeros_like(dk_scr)
        dv_scr[...] = jnp.zeros_like(dv_scr)

    q = q_ref[0] * jnp.asarray(0.125, BF)
    do = do_ref[0]
    qs, qst = stack_rows(q), stack_cols(q.T)
    dot_t = do.T
    dos, dost = stack_rows(do), stack_cols(dot_t)
    prod = dot_t.astype(F32) * o_ref[0].T.astype(F32)
    delta = jnp.concatenate(
        [
            jnp.sum(prod[:HALF], axis=0, keepdims=True),
            jnp.sum(prod[HALF:], axis=0, keepdims=True),
        ],
        axis=1,
    )
    lse = lse_ref[0]
    start = jnp.concatenate([start_ref[0], start_ref[0]], axis=1)
    length = jnp.concatenate([len_ref[0], len_ref[0]], axis=1)
    dq_scr[...] = jnp.zeros_like(dq_scr)

    def body(j, carry):
        k = k_ref[pl.ds(j * per, per)].reshape(BLOCK, LANES)
        v = v_ref[pl.ds(j * per, per)].reshape(BLOCK, LANES)
        s = jnp.where(allowed_mask(j, start, length), dot(k, qst), MASKED)
        p = jnp.exp(s - lse)
        ds = (p * (dot(v, dost) - delta)).astype(BF)
        rows = pl.ds(pl.multiple_of(j * BLOCK, BLOCK), BLOCK)
        dv_scr[rows] += dot(p.astype(BF), dos)
        dk_scr[rows] += dot(ds, qs)
        dq_scr[...] += dot(kt_scr[j].astype(BF), ds)
        return carry

    lax.fori_loop(lo_ref[i], hi_ref[i], body, 0)
    dq = (unstack_cols(dq_scr[...]) * 0.125).T.astype(BF)
    if wide:
        out_ref[i, :, :LANES] = dq
    else:
        out_ref[i, :BLOCK] = dq

    @pl.when(i == pl.num_programs(0) - 1)
    def _():
        n = GROUPS
        dk = dk_scr[...].astype(BF).reshape(n, kb, LANES)
        dv = dv_scr[...].astype(BF).reshape(n, kb, LANES)
        if wide:
            out_ref[:, :, LANES:2 * LANES] = dk
            out_ref[:, :, 2 * LANES:] = dv
        else:
            out_ref[:, BLOCK:BLOCK + kb] = dk
            out_ref[:, BLOCK + kb:] = dv


def row_spec(n):
    return pl.BlockSpec((1, 1, n), lambda i, lo, hi: (i, 0, 0))


def block_rows():
    return pl.BlockSpec((1, BLOCK, LANES), lambda i, lo, hi: (i, 0, 0))


def key_specs(kshape, kblock, vblock):
    return [
        pl.BlockSpec(kshape, lambda i, lo, hi: kblock),
        pl.BlockSpec(kshape, lambda i, lo, hi: vblock),
    ]


def attend_fwd(plan, q, kv, keys_at, after=()):
    lo, hi, start, length = plan
    nq = lo.shape[0]
    keys = keys_at[0][0] * keys_at[0][1]
    return pl.pallas_call(
        without(attn_fwd_kernel, 7, len(after)),
        grid_spec=pltpu.PrefetchScalarGridSpec(
            num_scalar_prefetch=2,
            grid=(nq,),
            in_specs=[row_spec(BLOCK), row_spec(BLOCK), block_rows()]
            + key_specs(*keys_at)
            + [pl.BlockSpec(memory_space=pl.ANY)] * len(after),
            out_specs=[block_rows(), row_spec(2 * BLOCK)],
            scratch_shapes=[
                pltpu.VMEM((keys // BLOCK, LANES, BLOCK), F32),
                pltpu.VMEM((keys, 2 * BLOCK), F32),
                pltpu.VMEM((LANES, 2 * BLOCK), F32),
            ],
        ),
        out_shape=[
            jax.ShapeDtypeStruct((nq, BLOCK, LANES), BF),
            jax.ShapeDtypeStruct((nq, 1, 2 * BLOCK), F32),
        ],
        compiler_params=params(),
        cost_estimate=cost(8e9, 4e6),
    )(lo, hi, start, length, q, kv, kv, *after)


def attend_bwd(plan, lse, q, kv, out, grad, keys_at, wide, after=()):
    lo, hi, start, length = plan
    nq = lo.shape[0]
    keys = keys_at[0][0] * keys_at[0][1]
    shape = (nq, BLOCK, 3 * LANES) if wide else (nq, BLOCK + 2 * keys_at[0][1], LANES)
    return pl.pallas_call(
        without(functools.partial(attn_bwd_kernel, wide), 10, len(after)),
        grid_spec=pltpu.PrefetchScalarGridSpec(
            num_scalar_prefetch=2,
            grid=(nq,),
            in_specs=[row_spec(BLOCK), row_spec(BLOCK), row_spec(2 * BLOCK), block_rows()]
            + key_specs(*keys_at)
            + [block_rows(), block_rows()]
            + [pl.BlockSpec(memory_space=pl.ANY)] * len(after),
            out_specs=pl.BlockSpec(shape, lambda i, lo, hi: (0, 0, 0)),
            scratch_shapes=[
                pltpu.VMEM((keys // BLOCK, LANES, BLOCK), F32),
                pltpu.VMEM((LANES, 2 * BLOCK), F32),
                pltpu.VMEM((keys, LANES), F32),
                pltpu.VMEM((keys, LANES), F32),
            ],
        ),
        out_shape=jax.ShapeDtypeStruct(shape, BF),
        compiler_params=params(),
        cost_estimate=cost(8e9, 6e6),
    )(lo, hi, start, length, lse, q, kv, kv, out, grad, *after)


def key_plan(query_ids, key_ids, causal):
    start = jnp.sum((key_ids[None, :] < query_ids[:, None]).astype(jnp.int32), axis=1)
    if causal:
        end = jnp.arange(query_ids.shape[0], dtype=jnp.int32) + 1
    else:
        end = jnp.sum((key_ids[None, :] <= query_ids[:, None]).astype(jnp.int32), axis=1)
    start = start.reshape(-1, 1, BLOCK)
    end = end.reshape(-1, 1, BLOCK)
    lo = jnp.min(start, axis=(1, 2)) // BLOCK
    hi = (jnp.max(end, axis=(1, 2)) + BLOCK - 1) // BLOCK
    return lo, hi, start, end - start


def params():
    return pltpu.CompilerParams(vmem_limit_bytes=44 * 2**20)


def cost(flops, size):
    return pl.CostEstimate(flops=int(flops), bytes_accessed=int(size), transcendentals=0)


def norm_forward(values, gain, shift):
    centered = values - jnp.mean(values, axis=-1, keepdims=True)
    inverse = lax.rsqrt(jnp.mean(centered * centered, axis=-1, keepdims=True) + EPS)
    normed = centered * inverse
    return normed * gain + shift, normed, inverse


def column_sum(x):
    return jnp.sum(x, axis=0, keepdims=True)


def norm_backward(upstream, normed, inverse, gain):
    scaled = upstream * gain
    inner = (
        scaled
        - jnp.mean(scaled, axis=-1, keepdims=True)
        - normed * jnp.mean(scaled * normed, axis=-1, keepdims=True)
    )
    return inverse * inner, column_sum(upstream * normed), column_sum(upstream)


PLACES = tuple(yh * 8 + yl * 4 + x for yh in range(2) for x in range(4) for yl in range(2))


def rows_of(ref):
    return jnp.concatenate([ref[p, 0] for p in PLACES], axis=0)


def plane_rows(ref):
    return ref[:, 0].reshape(512, ref.shape[3])


def put_rows(ref, value, other=None):
    for i, p in enumerate(PLACES):
        piece = value[i * 32:(i + 1) * 32]
        if other is not None:
            piece = piece + other[p, 0].astype(F32)
        ref[p, 0] = piece.astype(ref.dtype)


def halves(core, x):
    n = x.shape[1] // 2
    a, b = x[:, :n], x[:, n:]
    first = core == 0
    return jnp.where(first, a, b), jnp.where(first, b, a)


def ordered(core, mine, theirs):
    first = core == 0
    return jnp.concatenate(
        [jnp.where(first, mine, theirs), jnp.where(first, theirs, mine)], axis=1
    )


def joined(ref, first=0, count=None):
    count = ref.shape[1] if count is None else count
    return jnp.concatenate([ref[g, first:first + count] for g in range(GROUPS)], axis=1)


def put_groups(ref, value):
    for g in range(GROUPS):
        ref[g] = value[:, g * LANES:(g + 1) * LANES].astype(ref.dtype)


def qkv_kernel(core_ref, x_ref, own_tile_ref, other_tile_ref, own_ref, other_ref,
               qkv_ref, a1_ref, vec_ref, rows_ref):
    g = pl.program_id(0)
    core = core_ref[0]

    @pl.when(g == 0)
    def _():
        own = own_tile_ref[...].astype(F32).T[:16]
        other = other_tile_ref[...].astype(F32).T[:16]
        vec = ordered(core, own, other)
        vec_ref[...] = vec
        a, _, _ = norm_forward(x_ref[...].astype(F32), vec[0:1], vec[4:5])
        rows_ref[...] = a.astype(BF)
        mine, theirs = halves(core, a)
        a1_ref[0] = mine.astype(BF)
        a1_ref[1] = theirs.astype(BF)

    y = dot(a1_ref[0], own_ref[...]) + dot(a1_ref[1], other_ref[...])
    at = pl.ds(pl.multiple_of(g * LANES, LANES), LANES)
    bias = jnp.concatenate(
        [vec_ref[8:9, at], jnp.zeros((1, LANES), F32), vec_ref[9:10, at]], axis=1
    )
    qkv_ref[0] = (y + bias).astype(BF)


def text_kernel(core_ref, enc_ref, vec_ref, own_ref, other_ref, out_ref):
    m = pl.program_id(0)
    mine, theirs = halves(core_ref[0], enc_ref[...])
    y = dot(mine, rows_of(own_ref)) + dot(theirs, rows_of(other_ref))
    put_groups(out_ref, y + vec_ref[12:13] * m.astype(F32))


def middle_kernel(core_ref, o1_ref, x_ref, vec_ref, wo_own, wo_other, wq_own, wq_other, kv_ref,
                  x1_ref, a2_ref, q2_ref):
    core = core_ref[0]
    mine, theirs = halves(core, joined(o1_ref))
    x1 = (
        x_ref[...].astype(F32)
        + dot(mine, rows_of(wo_own))
        + dot(theirs, rows_of(wo_other))
        + vec_ref[10:11]
    )
    x1_ref[...] = x1
    a, _, _ = norm_forward(x1, vec_ref[1:2], vec_ref[5:6])
    mine, theirs = halves(core, a)
    mine, theirs = mine.astype(BF), theirs.astype(BF)
    a2_ref[0] = mine
    a2_ref[1] = theirs
    q2 = dot(mine, rows_of(wq_own)) + dot(theirs, rows_of(wq_other)) + vec_ref[11:12]
    for g in range(GROUPS):
        q2_ref[g, :BLOCK] = q2[:, g * LANES:(g + 1) * LANES].astype(BF)
        q2_ref[g, BLOCK:] = kv_ref[g]


def ffn_kernel(core_ref, o2_ref, x1_ref, vec_ref, upb_ref, cot_ref, wo_own, wo_other,
               up_own, up_other, dn_own, dn_other,
               out_ref, g2_ref, e2_ref, do2_ref, a3_ref, e3_ref, hid_ref, ep_ref, small_ref,
               dupb_ref, gup_ref, gdn_ref, go_ref,
               x2_scr, acc_scr, pre_scr, hid_scr, da_scr, dh_scr, a3t_scr):
    s = pl.program_id(0)
    t = lax.rem(s, 8)
    core = core_ref[0]

    @pl.when(s == 0)
    def _():
        mine, theirs = halves(core, joined(o2_ref))
        x2 = (
            x1_ref[...]
            + dot(mine, rows_of(wo_own))
            + dot(theirs, rows_of(wo_other))
            + vec_ref[13:14]
        )
        x2_scr[...] = x2
        a, _, _ = norm_forward(x2, vec_ref[2:3], vec_ref[6:7])
        mine, theirs = halves(core, a)
        a3_ref[0] = mine.astype(BF)
        a3_ref[1] = theirs.astype(BF)
        acc_scr[...] = jnp.zeros_like(acc_scr)

    @pl.when(s < 8)
    def _():
        pre = dot(a3_ref[0], rows_of(up_own)) + dot(a3_ref[1], rows_of(up_other)) + upb_ref[...]
        pre_scr[t] = pre
        hidden = (pre * jax.nn.sigmoid(pre)).astype(BF)
        hid_scr[t] = hidden

        @pl.when(t < 4)
        def _():
            acc_scr[...] += dot(hidden, plane_rows(dn_own))

        @pl.when(t >= 4)
        def _():
            acc_scr[...] += dot(hidden, plane_rows(dn_other))

    @pl.when(s == 7)
    def _():
        x3 = x2_scr[...] + acc_scr[...] + vec_ref[14:15]
        y, n4, r4 = norm_forward(x3, vec_ref[3:4], vec_ref[7:8])
        out_ref[...] = y
        g3, dgain, dshift = norm_backward(cot_ref[...].astype(F32), n4, r4, vec_ref[3:4])
        acc_scr[...] = g3
        e3_ref[...] = g3.astype(BF)
        small_ref[0:1] = dgain
        small_ref[1:2] = dshift
        small_ref[2:3] = column_sum(g3)
        da_scr[...] = jnp.zeros_like(da_scr)
        a3t_scr[...] = a3_ref[1].astype(F32).T

    @pl.when(s >= 8)
    def _():
        e3 = e3_ref[...]

        @pl.when(t < 4)
        def _():
            dh_scr[...] = dot_nt(e3, plane_rows(dn_own))
            hid_ref[...] = hid_scr[t]

        @pl.when(t >= 4)
        def _():
            dh_scr[...] = dot_nt(e3, plane_rows(dn_other))
            gdn_ref[:, 0] = dot_tn(hid_scr[t], e3).astype(BF).reshape(16, 32, D)

        pre = pre_scr[t]
        sig = jax.nn.sigmoid(pre)
        dpre = dh_scr[...] * sig * (1.0 + pre * (1.0 - sig))
        ep = dpre.astype(BF)
        ep_ref[...] = ep
        dupb_ref[...] = column_sum(dpre)
        put_rows(gup_ref, dot(a3t_scr[...].astype(BF), ep))
        da_scr[0] += dot_nt(ep, rows_of(up_own))
        da_scr[1] += dot_nt(ep, rows_of(up_other))

    @pl.when(s == 15)
    def _():
        da3 = ordered(core, da_scr[0], da_scr[1])
        _, n3, r3 = norm_forward(x2_scr[...], vec_ref[2:3], vec_ref[6:7])
        back, dgain, dshift = norm_backward(da3, n3, r3, vec_ref[2:3])
        g2 = acc_scr[...] + back
        g2_ref[...] = g2
        small_ref[3:4] = dgain
        small_ref[4:5] = dshift
        small_ref[5:6] = column_sum(g2)
        e2 = g2.astype(BF)
        e2_ref[...] = e2
        put_groups(
            do2_ref, ordered(core, dot_nt(e2, rows_of(wo_own)), dot_nt(e2, rows_of(wo_other)))
        )
        put_rows(go_ref, dot_tn(halves(core, joined(o2_ref))[1], e2))


def ffn_grad_kernel(core_ref, a3_ref, ep_ref, hid_ref, e3_ref, up_ref, dn_ref, o2_ref, e2_ref,
                    go_ref, out_ref):
    m = pl.program_id(0)

    @pl.when(m < 4)
    def _():
        put_rows(out_ref, dot_tn(a3_ref[0], ep_ref[...]), up_ref)

    @pl.when(m == 8)
    def _():
        o2 = halves(core_ref[0], joined(o2_ref))[0]
        put_rows(out_ref, dot_tn(o2, e2_ref[...]), go_ref)

    @pl.when((m >= 4) & (m < 8))
    def _():
        g = dot_tn(hid_ref[...], e3_ref[...]).reshape(16, 32, D)
        out_ref[:, 0] = (g + dn_ref[:, 0].astype(F32)).astype(BF)


def cross_back_kernel(core_ref, b2_ref, x1_ref, g2_ref, vec_ref, wq_own, wq_other,
                      wo_own, wo_other, g1_ref, e1_ref, do1_ref, small_ref):
    core = core_ref[0]
    dq = joined(b2_ref, 0, BLOCK)
    da2 = ordered(core, dot_nt(dq, rows_of(wq_own)), dot_nt(dq, rows_of(wq_other)))
    _, n2, r2 = norm_forward(x1_ref[...], vec_ref[1:2], vec_ref[5:6])
    back, dgain, dshift = norm_backward(da2, n2, r2, vec_ref[1:2])
    g1 = g2_ref[...] + back
    g1_ref[...] = g1
    e1 = g1.astype(BF)
    e1_ref[...] = e1
    put_groups(
        do1_ref, ordered(core, dot_nt(e1, rows_of(wo_own)), dot_nt(e1, rows_of(wo_other)))
    )
    small_ref[0:1] = dgain
    small_ref[1:2] = dshift
    small_ref[2:3] = column_sum(g1)
    small_ref[3:4] = column_sum(dq.astype(F32))
    small_ref[4:5] = column_sum(joined(b2_ref, BLOCK + 128, 128).astype(F32))


def text_back_kernel(core_ref, b2_ref, wk_own, wk_other, wv_own, wv_other, out_ref):
    dk = joined(b2_ref, BLOCK, 128)
    dv = joined(b2_ref, BLOCK + 128, 128)
    mine = dot_nt(dk, rows_of(wk_own)) + dot_nt(dv, rows_of(wv_own))
    theirs = dot_nt(dk, rows_of(wk_other)) + dot_nt(dv, rows_of(wv_other))
    out_ref[...] = ordered(core_ref[0], mine, theirs)


def cross_grad_kernel(half, core_ref, a2_ref, enc_ref, b2_ref, *rest):
    other = rest[0] if len(rest) == 2 else None
    out_ref = rest[-1]
    core = core_ref[0]
    m = pl.program_id(0)

    def emit(at, a, g):
        @pl.when(m == at)
        def _():
            put_rows(out_ref, dot_tn(a(), g()), other)

    emit(0, lambda: a2_ref[half], lambda: joined(b2_ref, 0, BLOCK))
    emit(1, lambda: halves(core, enc_ref[...])[half], lambda: joined(b2_ref, BLOCK, 128))
    emit(2, lambda: halves(core, enc_ref[...])[half], lambda: joined(b2_ref, BLOCK + 128, 128))


def self_grad_kernel(half, core_ref, a_ref, d_ref, o1_ref, e1_ref, *rest):
    other = rest[0] if len(rest) == 2 else None
    out_ref = rest[-1]
    n = 3 * LANES
    a = a_ref[...].reshape(GROUPS * BLOCK, a_ref.shape[2])
    g = dot_tn(a, d_ref[...].reshape(GROUPS * BLOCK, n))
    go = dot_tn(halves(core_ref[0], joined(o1_ref))[half], e1_ref[...])
    if other is not None:
        g = g + other[:, :n].astype(F32)
        go = go + other[:, n:].astype(F32)
    out_ref[:, :n] = g.astype(BF)
    out_ref[:, n:n + D] = go.astype(BF)


def small_kernel(core_ref, small_ref, recv_ref, big_ref, out_ref):
    out_ref[...] = (small_ref[...] + recv_ref[...].astype(F32)).astype(BF)


def self_back_kernel(core_ref, d_ref, own_ref, other_ref, x_ref, g1_ref, vec_ref,
                     out_ref, small_ref, sum_ref, da_scr):
    g = pl.program_id(0)

    @pl.when(g == 0)
    def _():
        da_scr[...] = jnp.zeros_like(da_scr)

    d = d_ref[0]
    sum_ref[0] = column_sum(d.astype(F32))
    da_scr[0] += dot_nt(d, own_ref[...])
    da_scr[1] += dot_nt(d, other_ref[...])

    @pl.when(g == pl.num_programs(0) - 1)
    def _():
        da1 = ordered(core_ref[0], da_scr[0], da_scr[1])
        _, n1, r1 = norm_forward(x_ref[...].astype(F32), vec_ref[0:1], vec_ref[4:5])
        back, dgain, dshift = norm_backward(da1, n1, r1, vec_ref[0:1])
        out_ref[...] = g1_ref[...] + back
        small_ref[0:1] = dgain
        small_ref[1:2] = dshift


def whole(shape):
    return pl.BlockSpec(shape, lambda *a: (0,) * len(shape))


def matrix(m):
    return pl.BlockSpec((16, 1, 32, D), lambda *a: (0, m, 0, 0))


def without(kernel, first, count):
    def run(*refs):
        return kernel(*refs[:first], *refs[first + count:])

    return run


def call(kernel, grid, in_specs, out_specs, out_shape, scratch, flops, size, after=()):
    def start(*args):
        return ordered_call(
            kernel, grid, in_specs, out_specs, out_shape, scratch, flops, size, args, after
        )

    return start


def ordered_call(
    kernel, grid, in_specs, out_specs, out_shape, scratch, flops, size, args, after
):
    return pl.pallas_call(
        without(kernel, len(args), len(after)),
        grid_spec=pltpu.PrefetchScalarGridSpec(
            num_scalar_prefetch=1,
            grid=grid,
            in_specs=list(in_specs) + [pl.BlockSpec(memory_space=pl.ANY)] * len(after),
            out_specs=out_specs,
            scratch_shapes=scratch,
        ),
        out_shape=out_shape,
        compiler_params=params(),
        cost_estimate=cost(flops, size),
    )(*args, *after)


def shape(dims, dtype=BF):
    return jax.ShapeDtypeStruct(dims, dtype)


def by_core(x):
    lead = x.shape[:-1]
    return x.reshape(*lead, 8, 2, HALF).swapaxes(-3, -2).reshape(*lead, D)


def by_place(x):
    lead = x.shape[:-1]
    return x.reshape(*lead, 2, 8, HALF).swapaxes(-3, -2).reshape(*lead, D)


def swap(x):
    return lax.ppermute(x, "c", [(0, 1), (1, 0)])


def local(
    tokens,
    encoded,
    unit_ids,
    text_ids,
    cotangent,
    attn_in,
    attn_out,
    w_up,
    w_down,
    norm_gains,
    shifts,
    biases,
    up_bias,
):
    core = lax.axis_index("c")
    first_core = core == 0
    core_arg = core.astype(jnp.int32).reshape(1)
    rows = tokens.shape[1]
    text_rows = encoded.shape[1]

    def mine(x):
        return lax.dynamic_slice_in_dim(x, core * (x.shape[0] // 2), x.shape[0] // 2, 0)

    def theirs(x):
        return lax.dynamic_slice_in_dim(x, (1 - core) * (x.shape[0] // 2), x.shape[0] // 2, 0)

    in_low = by_core(attn_in.astype(BF))
    out_low = by_core(attn_out.astype(BF))
    self_cols = (
        in_low[0:3].reshape(3, 8, GROUPS, LANES).transpose(1, 2, 0, 3).reshape(8, 3 * D)
    )
    vectors = jnp.concatenate([norm_gains, shifts, biases], axis=0).astype(BF)
    tile = jnp.concatenate(
        [
            vectors.T,
            up_bias.astype(BF).reshape(8, 4),
            jnp.zeros((8, 13), BF),
            unit_ids.reshape(8, 32).astype(BF),
            text_ids.reshape(8, 16).astype(BF),
            jnp.zeros((8, 48), BF),
        ],
        axis=1,
    )
    first_pack = jnp.concatenate([self_cols, tile], axis=1)
    width = 3 * D + LANES
    first_all = lax.all_to_all(
        jnp.broadcast_to(first_pack[None], (64, 8, width)), CHIPS, 0, 0, tiled=True
    )
    self_own = first_all.reshape(512, width)
    self_other = swap(self_own)

    up_low = w_up.astype(BF).reshape(8, 2, 4, 2, 2, 4, 32).transpose(0, 3, 5, 1, 4, 2, 6)
    up_low = up_low.reshape(8, 4, D).transpose(1, 0, 2).reshape(32, D)
    down_low = by_core(w_down.astype(BF))
    attn_low = jnp.concatenate([in_low[3:6], out_low], axis=0).reshape(40, D)
    z_pack = jnp.concatenate([up_low, down_low, attn_low], axis=0)
    z_at = lax.axis_index("z")
    z_all = jnp.zeros((4,) + z_pack.shape, BF)
    for k in range(4):
        part = z_pack if k == 0 else lax.ppermute(z_pack, "z", [(i, (i + k) % 4) for i in range(4)])
        z_all = lax.dynamic_update_slice(z_all, part[None], (lax.rem(z_at + 4 - k, 4), 0, 0))
    attn_z = z_all[:, 64:].reshape(4, 5, 8, D).transpose(1, 0, 2, 3).reshape(1, 5, 32, D)
    up_z = z_all[:, :32].reshape(4, 4, 8, D).transpose(1, 0, 2, 3).reshape(4, 32, D)
    ffn_z = jnp.concatenate([up_z, z_all[:, 32:64]], axis=0)[None]
    attn_own = lax.all_gather(attn_z, PLANE, axis=0, tiled=True)
    ffn_own = lax.all_gather(ffn_z, PLANE, axis=0, tiled=True)

    x = by_core(tokens[0])
    enc = by_core(encoded[0])
    cot = by_core(cotangent[0])

    tile_own, tile_other = self_own[:, 3 * D:], self_other[:, 3 * D:]

    def up_part(t):
        return t[:, 15:19].reshape(2, 4, 2, 4, 32).transpose(3, 0, 2, 1, 4).reshape(1, 2048)

    up_own, up_other = up_part(tile_own), up_part(tile_other)
    up_vec = jnp.concatenate(
        [jnp.where(first_core, up_own, up_other), jnp.where(first_core, up_other, up_own)], axis=1
    ).astype(F32)
    place = lax.axis_index(("yh", "x"))
    seq_tile = lax.dynamic_slice_in_dim(tile_own, place * 64, 64, 0)
    seq_tile = seq_tile.reshape(8, 8, LANES).astype(F32).astype(jnp.int32)
    units = seq_tile[:, :, 32:64].reshape(-1)
    texts = seq_tile[:, :, 64:80].reshape(-1)
    self_plan = key_plan(units, units, True)
    cross_plan = key_plan(units, texts, False)

    qkv, _, vec, a1 = call(
        qkv_kernel,
        (GROUPS,),
        [
            whole((rows, D)),
            pl.BlockSpec((512, LANES), lambda g, c: (0, 24)),
            pl.BlockSpec((512, LANES), lambda g, c: (0, 24)),
            pl.BlockSpec((512, 384), lambda g, c: (0, g)),
            pl.BlockSpec((512, 384), lambda g, c: (0, g)),
        ],
        [
            pl.BlockSpec((1, rows, 384), lambda g, c: (g, 0, 0)),
            whole((2, rows, 512)),
            whole((16, D)),
            whole((rows, D)),
        ],
        [
            shape((GROUPS, rows, 384)),
            shape((2, rows, 512)),
            shape((16, D), F32),
            shape((rows, D)),
        ],
        [],
        1.6e9,
        8e6,
    )(core_arg, x, self_own, self_other, self_own, self_other)
    (attn_own, _) = lax.optimization_barrier((attn_own, qkv))
    attn_other = swap(attn_own)
    qkv = lax.all_to_all(qkv, SEQ, 0, 0, tiled=True)
    self_keys = ((GROUPS, rows, LANES), (0, 0, 1), (0, 0, 2))
    o1_heads, lse1 = attend_fwd(self_plan, qkv, qkv, self_keys)
    o1 = lax.all_to_all(o1_heads, SEQ, 0, 0, tiled=True)

    kv2 = call(
        text_kernel,
        (2,),
        [
            whole((text_rows, D)),
            whole((16, D)),
            pl.BlockSpec((16, 1, 32, D), lambda m, c: (0, 1 + m, 0, 0)),
            pl.BlockSpec((16, 1, 32, D), lambda m, c: (0, 1 + m, 0, 0)),
        ],
        pl.BlockSpec((GROUPS, text_rows, LANES), lambda m, c: (0, m, 0)),
        shape((GROUPS, 2 * text_rows, LANES)),
        [],
        0.5e9,
        4e6,
        after=(o1_heads,),
    )(core_arg, enc, vec, attn_own, attn_other)

    x1, a2, q2 = call(
        middle_kernel,
        (1,),
        [whole((GROUPS, rows, LANES)), whole((rows, D)), whole((16, D))]
        + [matrix(3), matrix(3), matrix(0), matrix(0), whole((GROUPS, 2 * text_rows, LANES))],
        [whole((rows, D)), whole((2, rows, 512)), whole((GROUPS, 2 * rows, LANES))],
        [shape((rows, D), F32), shape((2, rows, 512)), shape((GROUPS, 2 * rows, LANES))],
        [],
        1.1e9,
        8e6,
    )(core_arg, o1, x, vec, attn_own, attn_other, attn_own, attn_other, kv2)
    (a1, _) = lax.optimization_barrier((a1, q2))
    a1_all = lax.all_gather(a1, SEQ, axis=0, tiled=False)
    (ffn_own, _) = lax.optimization_barrier((ffn_own, q2))
    ffn_other = swap(ffn_own)
    q2 = lax.all_to_all(q2, SEQ, 0, 0, tiled=True)
    cross_keys = ((GROUPS, text_rows, LANES), (0, 2, 0), (0, 3, 0))
    o2_heads, lse2 = attend_fwd(cross_plan, q2, q2, cross_keys)
    o2 = lax.all_to_all(o2_heads, SEQ, 0, 0, tiled=True)

    def block_of(s, c):
        t = lax.rem(s, 8)
        return jnp.where(t < 4, c[0], 1 - c[0]) * 4 + lax.rem(t, 4)

    def back_block(s, c):
        return block_of(jnp.maximum(s, 8), c)

    up_spec = pl.BlockSpec(
        (16, 1, 32, 512), lambda s, c: (0, block_of(s, c) // 2, 0, lax.rem(block_of(s, c), 2))
    )
    gup_spec = pl.BlockSpec(
        (16, 1, 32, 512), lambda s, c: (0, back_block(s, c) // 2, 0, lax.rem(back_block(s, c), 2))
    )
    (layer_out, g2, e2, do2, a3, e3, hidden, ep, small_f, dup_bias, gup, gdn, go) = call(
        ffn_kernel,
        (16,),
        [
            whole((GROUPS, rows, LANES)),
            whole((rows, D)),
            whole((16, D)),
            pl.BlockSpec((1, 512), lambda s, c: (0, block_of(s, c))),
            whole((rows, D)),
            matrix(4),
            matrix(4),
            up_spec,
            up_spec,
            pl.BlockSpec(
                (16, 1, 32, D), lambda s, c: (0, 4 + jnp.minimum(lax.rem(s, 8), 3), 0, 0)
            ),
            pl.BlockSpec(
                (16, 1, 32, D), lambda s, c: (0, jnp.maximum(lax.rem(s, 8), 4), 0, 0)
            ),
        ],
        [
            whole((rows, D)),
            whole((rows, D)),
            whole((rows, D)),
            whole((GROUPS, rows, LANES)),
            whole((2, rows, 512)),
            whole((rows, D)),
            pl.BlockSpec((rows, 512), lambda s, c: (0, jnp.clip(s - 8, 0, 3))),
            pl.BlockSpec((rows, 512), lambda s, c: (0, back_block(s, c))),
            whole((8, D)),
            pl.BlockSpec((1, 512), lambda s, c: (0, back_block(s, c))),
            gup_spec,
            pl.BlockSpec((16, 1, 32, D), lambda s, c: (0, jnp.maximum(s - 12, 0), 0, 0)),
            matrix(0),
        ],
        [
            shape((rows, D), F32),
            shape((rows, D), F32),
            shape((rows, D)),
            shape((GROUPS, rows, LANES)),
            shape((2, rows, 512)),
            shape((rows, D)),
            shape((rows, FF // 2)),
            shape((rows, FF)),
            shape((8, D), F32),
            shape((1, FF), F32),
            shape((16, 4, 32, D)),
            shape((16, 4, 32, D)),
            shape((16, 1, 32, D)),
        ],
        [
            pltpu.VMEM((rows, D), F32),
            pltpu.VMEM((rows, D), F32),
            pltpu.VMEM((8, rows, 512), F32),
            pltpu.VMEM((8, rows, 512), BF),
            pltpu.VMEM((2, rows, 512), F32),
            pltpu.VMEM((rows, 512), F32),
            pltpu.VMEM((512, rows), F32),
        ],
        16e9,
        50e6,
    )(core_arg, o2, x1, vec, up_vec, cot, attn_own, attn_other, ffn_own, ffn_other,
      ffn_own, ffn_other)
    do2 = lax.all_to_all(do2, SEQ, 0, 0, tiled=True)
    gup_recv, gdn_recv, go_recv = swap(gup), swap(gdn), swap(go)

    back2_heads = attend_bwd(cross_plan, lse2, q2, q2, o2_heads, do2, cross_keys, False)
    back2 = lax.all_to_all(back2_heads, SEQ, 0, 0, tiled=True)
    ffn_grad = call(
        ffn_grad_kernel,
        (9,),
        [
            whole((2, rows, 512)),
            pl.BlockSpec((rows, D), lambda m, c: (0, jnp.minimum(m, 3))),
            pl.BlockSpec((rows, 512), lambda m, c: (0, jnp.clip(m - 4, 0, 3))),
            whole((rows, D)),
            pl.BlockSpec((16, 1, 32, D), lambda m, c: (0, jnp.minimum(m, 3), 0, 0)),
            pl.BlockSpec((16, 1, 32, D), lambda m, c: (0, jnp.clip(m - 4, 0, 3), 0, 0)),
            whole((GROUPS, rows, LANES)),
            whole((rows, D)),
            matrix(0),
        ],
        pl.BlockSpec((16, 1, 32, D), lambda m, c: (0, m, 0, 0)),
        shape((16, 12, 32, D)),
        [],
        2.4e9,
        20e6,
        after=(back2_heads,),
    )(core_arg, a3, ep, hidden, e3, gup_recv, gdn_recv, o2, e2, go_recv)

    def cross_grads(half, recv, into, after=()):
        args = (core_arg, a2, enc, back2) + tuple(recv)
        later = after if into is None else (into,)
        first, blocks = (0, 3) if into is None else (9, 12)
        block = pl.BlockSpec((16, 1, 32, D), lambda m, c: (0, m, 0, 0))
        return pl.pallas_call(
            without(functools.partial(cross_grad_kernel, half), len(args), len(later)),
            grid_spec=pltpu.PrefetchScalarGridSpec(
                num_scalar_prefetch=1,
                grid=(3,),
                in_specs=[
                    whole((2, rows, 512)),
                    whole((text_rows, D)),
                    whole((GROUPS, rows + 2 * text_rows, LANES)),
                ]
                + [block] * len(recv)
                + [pl.BlockSpec(memory_space=pl.ANY)] * len(later),
                out_specs=pl.BlockSpec((16, 1, 32, D), lambda m, c: (0, first + m, 0, 0)),
            ),
            out_shape=shape((16, blocks, 32, D)),
            input_output_aliases={} if into is None else {len(args): 0},
            compiler_params=params(),
            cost_estimate=cost(0.6e9, 5e6),
        )(*args, *later)

    cross_theirs = cross_grads(1, [], None, (ffn_grad,))
    cross_recv = swap(cross_theirs)

    g1, e1, do1, small_c = call(
        cross_back_kernel,
        (1,),
        [whole((GROUPS, rows + 2 * text_rows, LANES)), whole((rows, D)), whole((rows, D))]
        + [whole((16, D)), matrix(0), matrix(0), matrix(3), matrix(3)],
        [whole((rows, D)), whole((rows, D)), whole((GROUPS, rows, LANES)), whole((8, D))],
        [
            shape((rows, D), F32),
            shape((rows, D)),
            shape((GROUPS, rows, LANES)),
            shape((8, D), F32),
        ],
        [],
        1.1e9,
        10e6,
        after=(ffn_grad, cross_theirs),
    )(core_arg, back2, x1, g2, vec, attn_own, attn_other, attn_own, attn_other)
    do1_rows = do1
    do1 = lax.all_to_all(do1, SEQ, 0, 0, tiled=True)
    (cross_recv, _) = lax.optimization_barrier((cross_recv, do1_rows))
    all_grads = cross_grads(0, [cross_recv], ffn_grad)
    grads = lax.psum_scatter(
        all_grads.reshape(16 * 12 * 32, D), PLANE, scatter_dimension=0, tiled=True
    ).reshape(12, 32, D)

    dqkv_heads = attend_bwd(
        self_plan, lse1, qkv, qkv, o1_heads, do1, self_keys, True, after=(all_grads,)
    )
    dqkv = lax.all_to_all(dqkv_heads, SEQ, 0, 0, tiled=True)
    width = 3 * LANES + D + LANES

    def self_grads(half, recv, n, later):
        at = (lambda m, c: (0, 0, c[0])) if half == 0 else (lambda m, c: (0, 0, 1 - c[0]))
        return call(
            functools.partial(self_grad_kernel, half),
            (1,),
            [
                pl.BlockSpec((GROUPS, rows, 512), at),
                whole((GROUPS, rows, 3 * LANES)),
                whole((GROUPS, rows, LANES)),
                whole((rows, D)),
            ]
            + [whole((512, 3 * LANES + D))] * len(recv),
            whole((512, n)),
            shape((512, n)),
            [],
            1.1e9,
            8e6,
            after=later,
        )(core_arg, a1_all, dqkv_heads, o1, e1, *recv)

    self_theirs = self_grads(1, [], 3 * LANES + D, ())
    self_recv = swap(self_theirs)
    d_enc = call(
        text_back_kernel,
        (1,),
        [whole((GROUPS, rows + 2 * text_rows, LANES))]
        + [matrix(1), matrix(1), matrix(2), matrix(2)],
        whole((text_rows, D)),
        shape((text_rows, D), F32),
        [],
        0.5e9,
        5e6,
        after=(self_theirs,),
    )(core_arg, back2, attn_own, attn_other, attn_own, attn_other)
    own = self_grads(0, [self_recv], width, (d_enc,))

    d_tokens, small_s, dsum = call(
        self_back_kernel,
        (GROUPS,),
        [
            pl.BlockSpec((1, rows, 384), lambda g, c: (g, 0, 0)),
            pl.BlockSpec((512, 384), lambda g, c: (0, g)),
            pl.BlockSpec((512, 384), lambda g, c: (0, g)),
            whole((rows, D)),
            whole((rows, D)),
            whole((16, D)),
        ],
        [
            whole((rows, D)),
            whole((8, D)),
            pl.BlockSpec((1, 1, 384), lambda g, c: (g, 0, 0)),
        ],
        [shape((rows, D), F32), shape((8, D), F32), shape((GROUPS, 1, 384), F32)],
        [pltpu.VMEM((2, rows, 512), F32)],
        1.6e9,
        9e6,
        after=(own,),
    )(core_arg, dqkv, self_own, self_other, x, g1, vec)

    dsum = dsum.reshape(GROUPS, 3, LANES)
    small = jnp.concatenate(
        [
            small_s[0:1],
            small_c[0:1],
            small_f[3:4],
            small_f[0:1],
            small_s[1:2],
            small_c[1:2],
            small_f[4:5],
            small_f[1:2],
            dsum[:, 0].reshape(1, D),
            dsum[:, 2].reshape(1, D),
            small_c[2:3],
            small_c[3:4],
            small_c[4:5],
            small_f[5:6],
            small_f[2:3],
        ],
        axis=0,
    )
    up_sums = dup_bias.reshape(2, 4, 2, 2, 4, 32).transpose(0, 2, 4, 3, 1, 5).reshape(D, 4)
    small = jnp.concatenate([small.T, up_sums, jnp.zeros((D, LANES - 19), F32)], axis=1)
    small_recv = swap(theirs(small).astype(BF))
    last = pl.pallas_call(
        small_kernel,
        grid_spec=pltpu.PrefetchScalarGridSpec(
            num_scalar_prefetch=1,
            grid=(1,),
            in_specs=[whole((512, LANES)), whole((512, LANES)), pl.BlockSpec(memory_space=pl.ANY)],
            out_specs=pl.BlockSpec((512, LANES), lambda m, c: (0, 3 + D // LANES)),
        ),
        out_shape=shape((512, width)),
        input_output_aliases={3: 0},
        compiler_params=params(),
        cost_estimate=cost(1e5, 5e5),
    )(core_arg, mine(small), small_recv, own)
    last = lax.all_to_all(last.reshape(64, 8, width), CHIPS, 0, 0, tiled=True)
    heads = jnp.sum(last[:, :, :3 * LANES].astype(F32).reshape(8, 8, 8, 3 * LANES), axis=0)
    last = jnp.sum(last[:, :, 3 * LANES:].astype(F32), axis=0)

    z_grad = jnp.concatenate(
        [
            grads[:4].reshape(4, 4, 8, D).transpose(1, 0, 2, 3).reshape(4, 32, D),
            grads[4:8],
            grads[8:].reshape(4, 4, 8, D).transpose(1, 0, 2, 3).reshape(4, 32, D),
        ],
        axis=1,
    )
    z_grad = lax.all_to_all(z_grad, "z", 0, 0, tiled=True)
    z_grad = jnp.sum(z_grad.astype(F32), axis=0)
    d_up = z_grad[:32].reshape(4, 8, D).transpose(1, 0, 2).reshape(8, 2, 4, 2, 2, 4, 32)
    d_up = d_up.transpose(0, 3, 5, 1, 4, 2, 6).reshape(8, FF)
    d_down = by_place(z_grad[32:64])
    heads = heads.reshape(GROUPS, 8, 3, LANES).transpose(2, 1, 0, 3).reshape(3, 8, D)
    attn_grad = z_grad[64:].reshape(4, 8, D)
    d_in = by_place(jnp.concatenate([heads, attn_grad[1:]], axis=0))
    d_out = by_place(jnp.stack([last[:, :D], attn_grad[0]]))
    d_vec = last[:, D:D + 15].T
    d_up_bias = last[:, D + 15:D + 19].reshape(32)
    return (
        by_place(layer_out)[None],
        by_place(d_tokens)[None],
        by_place(d_enc)[None],
        d_in,
        d_out,
        d_up,
        d_down,
        d_vec[0:4],
        d_vec[4:8],
        d_vec[8:15],
        d_up_bias,
    )


def solution(mesh):
    fine = Mesh(mesh.devices.reshape(2, 4, 2, 2, 4), ("yh", "x", "c", "yl", "z"))
    fsdp = ("yh", "x", "c")
    every = fsdp + SEQ
    placed = (
        P(fsdp, SEQ, None),
        P(fsdp, SEQ, None),
        P(fsdp, SEQ),
        P(fsdp, SEQ),
        P(fsdp, SEQ, None),
        P(None, every, None),
        P(None, every, None),
        P(every, None),
        P(every, None),
        P(None, every),
        P(None, every),
        P(None, every),
        P(every),
    )
    return jax.shard_map(
        local,
        mesh=fine,
        in_specs=placed,
        out_specs=(
            P(fsdp, SEQ, None),
            P(fsdp, SEQ, None),
            P(fsdp, SEQ, None),
            P(None, every, None),
            P(None, every, None),
            P(every, None),
            P(every, None),
            P(None, every),
            P(None, every),
            P(None, every),
            P(every),
        ),
        check_vma=False,
    )
```

```python
import functools

import jax
import jax.numpy as jnp
from jax import lax
from jax.experimental import pallas as pl
from jax.experimental.pallas import tpu as pltpu
from jax.sharding import Mesh
from jax.sharding import PartitionSpec as P

D = 1024
FF = 4096
GROUPS = 8
LANES = 128
HALF = 64
BLOCK = 256
EPS = 1e-05
MASKED = -1e30

SEQ = ("yl", "z")
CHIPS = ("yh", "x", "yl", "z")
PLANE = ("yh", "yl", "x")
BF = jnp.bfloat16
F32 = jnp.float32


def dot(a, b):
    return jnp.dot(a, b, preferred_element_type=F32)


def dot_nt(a, b):
    return lax.dot_general(a, b, (((1,), (1,)), ((), ())), preferred_element_type=F32)


def dot_tn(a, b):
    return lax.dot_general(a, b, (((0,), (0,)), ((), ())), preferred_element_type=F32)


def stack_cols(xt):
    zero = jnp.zeros((HALF, xt.shape[1]), xt.dtype)
    return jnp.concatenate(
        [
            jnp.concatenate([xt[:HALF], zero], axis=0),
            jnp.concatenate([zero, xt[HALF:]], axis=0),
        ],
        axis=1,
    )


def stack_rows(x):
    lane = lax.broadcasted_iota(jnp.int32, x.shape, 1)
    zero = jnp.zeros_like(x)
    return jnp.concatenate(
        [jnp.where(lane < HALF, x, zero), jnp.where(lane < HALF, zero, x)], axis=0
    )


def unstack_cols(xt):
    n = xt.shape[1] // 2
    return jnp.concatenate([xt[:HALF, :n], xt[HALF:, n:]], axis=0)


def allowed_mask(j, start, length):
    pos = lax.broadcasted_iota(jnp.int32, (BLOCK, start.shape[1]), 0) + j * BLOCK
    off = pos - start
    return (off >= 0) & (off < length)


def attn_fwd_kernel(lo_ref, hi_ref, start_ref, len_ref, q_ref, k_ref, v_ref, o_ref, lse_ref,
                    vt_scr, s_scr, o_scr):
    i = pl.program_id(0)
    nk = vt_scr.shape[0]
    per = BLOCK // k_ref.shape[1]

    @pl.when(i == 0)
    def _():
        for j in range(nk):
            vt_scr[j] = v_ref[j * per:(j + 1) * per].reshape(BLOCK, LANES).astype(F32).T

    q = q_ref[0] * jnp.asarray(0.125, BF)
    qst = stack_cols(q.T)
    start = jnp.concatenate([start_ref[0], start_ref[0]], axis=1)
    length = jnp.concatenate([len_ref[0], len_ref[0]], axis=1)
    lo, hi = lo_ref[i], hi_ref[i]
    width = 2 * BLOCK

    def first(j, m8):
        k = k_ref[pl.ds(j * per, per)].reshape(BLOCK, LANES)
        s = dot(k, qst)
        s = jnp.where(allowed_mask(j, start, length), s, MASKED)
        s_scr[pl.ds(pl.multiple_of(j * BLOCK, BLOCK), BLOCK)] = s
        return jnp.maximum(m8, jnp.max(s.reshape(BLOCK // 8, 8, width), axis=0))

    m8 = lax.fori_loop(lo, hi, first, jnp.full((8, width), MASKED, F32))
    m = jnp.max(m8, axis=0, keepdims=True)
    o_scr[...] = jnp.zeros_like(o_scr)

    def second(j, l8):
        p = jnp.exp(s_scr[pl.ds(pl.multiple_of(j * BLOCK, BLOCK), BLOCK)] - m)
        o_scr[...] += dot(vt_scr[j].astype(BF), p.astype(BF))
        return l8 + jnp.sum(p.reshape(BLOCK // 8, 8, width), axis=0)

    l8 = lax.fori_loop(lo, hi, second, jnp.zeros((8, width), F32))
    l = jnp.sum(l8, axis=0, keepdims=True)
    lse_ref[0] = m + jnp.log(l)
    ot = unstack_cols(o_scr[...] * (1.0 / l))
    o_ref[0] = ot.T.astype(BF)


def attn_bwd_kernel(wide, lo_ref, hi_ref, start_ref, len_ref, lse_ref, q_ref, k_ref, v_ref, o_ref,
                    do_ref, out_ref, kt_scr, dq_scr, dk_scr, dv_scr):
    i = pl.program_id(0)
    nk = kt_scr.shape[0]
    kb = k_ref.shape[1]
    per = BLOCK // kb

    @pl.when(i == 0)
    def _():
        for j in range(nk):
            kt_scr[j] = k_ref[j * per:(j + 1) * per].reshape(BLOCK, LANES).astype(F32).T
        dk_scr[...] = jnp.zeros_like(dk_scr)
        dv_scr[...] = jnp.zeros_like(dv_scr)

    q = q_ref[0] * jnp.asarray(0.125, BF)
    do = do_ref[0]
    qs, qst = stack_rows(q), stack_cols(q.T)
    dot_t = do.T
    dos, dost = stack_rows(do), stack_cols(dot_t)
    prod = dot_t.astype(F32) * o_ref[0].T.astype(F32)
    delta = jnp.concatenate(
        [
            jnp.sum(prod[:HALF], axis=0, keepdims=True),
            jnp.sum(prod[HALF:], axis=0, keepdims=True),
        ],
        axis=1,
    )
    lse = lse_ref[0]
    start = jnp.concatenate([start_ref[0], start_ref[0]], axis=1)
    length = jnp.concatenate([len_ref[0], len_ref[0]], axis=1)
    dq_scr[...] = jnp.zeros_like(dq_scr)

    def body(j, carry):
        k = k_ref[pl.ds(j * per, per)].reshape(BLOCK, LANES)
        v = v_ref[pl.ds(j * per, per)].reshape(BLOCK, LANES)
        s = jnp.where(allowed_mask(j, start, length), dot(k, qst), MASKED)
        p = jnp.exp(s - lse)
        ds = (p * (dot(v, dost) - delta)).astype(BF)
        rows = pl.ds(pl.multiple_of(j * BLOCK, BLOCK), BLOCK)
        dv_scr[rows] += dot(p.astype(BF), dos)
        dk_scr[rows] += dot(ds, qs)
        dq_scr[...] += dot(kt_scr[j].astype(BF), ds)
        return carry

    lax.fori_loop(lo_ref[i], hi_ref[i], body, 0)
    dq = (unstack_cols(dq_scr[...]) * 0.125).T.astype(BF)
    if wide:
        out_ref[i, :, :LANES] = dq
    else:
        out_ref[i, :BLOCK] = dq

    @pl.when(i == pl.num_programs(0) - 1)
    def _():
        n = GROUPS
        dk = dk_scr[...].astype(BF).reshape(n, kb, LANES)
        dv = dv_scr[...].astype(BF).reshape(n, kb, LANES)
        if wide:
            out_ref[:, :, LANES:2 * LANES] = dk
            out_ref[:, :, 2 * LANES:] = dv
        else:
            out_ref[:, BLOCK:BLOCK + kb] = dk
            out_ref[:, BLOCK + kb:] = dv


def row_spec(n):
    return pl.BlockSpec((1, 1, n), lambda i, lo, hi: (i, 0, 0))


def block_rows():
    return pl.BlockSpec((1, BLOCK, LANES), lambda i, lo, hi: (i, 0, 0))


def key_specs(kshape, kblock, vblock):
    return [
        pl.BlockSpec(kshape, lambda i, lo, hi: kblock),
        pl.BlockSpec(kshape, lambda i, lo, hi: vblock),
    ]


def attend_fwd(plan, q, kv, keys_at, after=()):
    lo, hi, start, length = plan
    nq = lo.shape[0]
    keys = keys_at[0][0] * keys_at[0][1]
    return pl.pallas_call(
        without(attn_fwd_kernel, 7, len(after)),
        grid_spec=pltpu.PrefetchScalarGridSpec(
            num_scalar_prefetch=2,
            grid=(nq,),
            in_specs=[row_spec(BLOCK), row_spec(BLOCK), block_rows()]
            + key_specs(*keys_at)
            + [pl.BlockSpec(memory_space=pl.ANY)] * len(after),
            out_specs=[block_rows(), row_spec(2 * BLOCK)],
            scratch_shapes=[
                pltpu.VMEM((keys // BLOCK, LANES, BLOCK), F32),
                pltpu.VMEM((keys, 2 * BLOCK), F32),
                pltpu.VMEM((LANES, 2 * BLOCK), F32),
            ],
        ),
        out_shape=[
            jax.ShapeDtypeStruct((nq, BLOCK, LANES), BF),
            jax.ShapeDtypeStruct((nq, 1, 2 * BLOCK), F32),
        ],
        compiler_params=params(),
        cost_estimate=cost(8e9, 4e6),
    )(lo, hi, start, length, q, kv, kv, *after)


def attend_bwd(plan, lse, q, kv, out, grad, keys_at, wide, after=()):
    lo, hi, start, length = plan
    nq = lo.shape[0]
    keys = keys_at[0][0] * keys_at[0][1]
    shape = (nq, BLOCK, 3 * LANES) if wide else (nq, BLOCK + 2 * keys_at[0][1], LANES)
    return pl.pallas_call(
        without(functools.partial(attn_bwd_kernel, wide), 10, len(after)),
        grid_spec=pltpu.PrefetchScalarGridSpec(
            num_scalar_prefetch=2,
            grid=(nq,),
            in_specs=[row_spec(BLOCK), row_spec(BLOCK), row_spec(2 * BLOCK), block_rows()]
            + key_specs(*keys_at)
            + [block_rows(), block_rows()]
            + [pl.BlockSpec(memory_space=pl.ANY)] * len(after),
            out_specs=pl.BlockSpec(shape, lambda i, lo, hi: (0, 0, 0)),
            scratch_shapes=[
                pltpu.VMEM((keys // BLOCK, LANES, BLOCK), F32),
                pltpu.VMEM((LANES, 2 * BLOCK), F32),
                pltpu.VMEM((keys, LANES), F32),
                pltpu.VMEM((keys, LANES), F32),
            ],
        ),
        out_shape=jax.ShapeDtypeStruct(shape, BF),
        compiler_params=params(),
        cost_estimate=cost(8e9, 6e6),
    )(lo, hi, start, length, lse, q, kv, kv, out, grad, *after)


def key_plan(query_ids, key_ids, causal):
    start = jnp.sum((key_ids[None, :] < query_ids[:, None]).astype(jnp.int32), axis=1)
    if causal:
        end = jnp.arange(query_ids.shape[0], dtype=jnp.int32) + 1
    else:
        end = jnp.sum((key_ids[None, :] <= query_ids[:, None]).astype(jnp.int32), axis=1)
    start = start.reshape(-1, 1, BLOCK)
    end = end.reshape(-1, 1, BLOCK)
    lo = jnp.min(start, axis=(1, 2)) // BLOCK
    hi = (jnp.max(end, axis=(1, 2)) + BLOCK - 1) // BLOCK
    return lo, hi, start, end - start


def params():
    return pltpu.CompilerParams(vmem_limit_bytes=58 * 2**20)


def cost(flops, size):
    return pl.CostEstimate(flops=int(flops), bytes_accessed=int(size), transcendentals=0)


def norm_forward(values, gain, shift):
    centered = values - jnp.mean(values, axis=-1, keepdims=True)
    inverse = lax.rsqrt(jnp.mean(centered * centered, axis=-1, keepdims=True) + EPS)
    normed = centered * inverse
    return normed * gain + shift, normed, inverse


def column_sum(x):
    return jnp.sum(x, axis=0, keepdims=True)


def norm_backward(upstream, normed, inverse, gain):
    scaled = upstream * gain
    inner = (
        scaled
        - jnp.mean(scaled, axis=-1, keepdims=True)
        - normed * jnp.mean(scaled * normed, axis=-1, keepdims=True)
    )
    return inverse * inner, column_sum(upstream * normed), column_sum(upstream)


PLACES = tuple(yh * 8 + yl * 4 + x for yh in range(2) for x in range(4) for yl in range(2))


def rows_of(ref):
    return jnp.concatenate([ref[p, 0] for p in PLACES], axis=0)


def plane_rows(ref):
    return ref[:, 0].reshape(512, ref.shape[3])


def put_rows(ref, value, other=None):
    for i, p in enumerate(PLACES):
        piece = value[i * 32:(i + 1) * 32]
        if other is not None:
            piece = piece + other[p, 0].astype(F32)
        ref[p, 0] = piece.astype(ref.dtype)


def halves(core, x):
    n = x.shape[1] // 2
    a, b = x[:, :n], x[:, n:]
    first = core == 0
    return jnp.where(first, a, b), jnp.where(first, b, a)


def ordered(core, mine, theirs):
    first = core == 0
    return jnp.concatenate(
        [jnp.where(first, mine, theirs), jnp.where(first, theirs, mine)], axis=1
    )


def joined(ref, first=0, count=None):
    count = ref.shape[1] if count is None else count
    return jnp.concatenate([ref[g, first:first + count] for g in range(GROUPS)], axis=1)


def put_groups(ref, value):
    for g in range(GROUPS):
        ref[g] = value[:, g * LANES:(g + 1) * LANES].astype(ref.dtype)


def qkv_kernel(core_ref, x_ref, own_tile_ref, other_tile_ref, own_ref, other_ref,
               qkv_ref, a1_ref, vec_ref, rows_ref):
    m = pl.program_id(0)
    core = core_ref[0]

    @pl.when(m == 0)
    def _():
        own = rows_of(own_tile_ref).astype(F32).T[:16]
        other = rows_of(other_tile_ref).astype(F32).T[:16]
        vec = ordered(core, own, other)
        vec_ref[...] = vec
        a, _, _ = norm_forward(x_ref[...].astype(F32), vec[0:1], vec[4:5])
        rows_ref[...] = a.astype(BF)
        mine, theirs = halves(core, a)
        a1_ref[0] = mine.astype(BF)
        a1_ref[1] = theirs.astype(BF)

    y = dot(a1_ref[0], rows_of(own_ref)) + dot(a1_ref[1], rows_of(other_ref))
    bias = vec_ref[8:9] * (m == 0).astype(F32) + vec_ref[9:10] * (m == 2).astype(F32)
    put_groups(qkv_ref, y + bias)


def text_kernel(core_ref, enc_ref, vec_ref, own_ref, other_ref, out_ref):
    m = pl.program_id(0)
    mine, theirs = halves(core_ref[0], enc_ref[...])
    y = dot(mine, rows_of(own_ref)) + dot(theirs, rows_of(other_ref))
    put_groups(out_ref, y + vec_ref[12:13] * m.astype(F32))


def middle_kernel(core_ref, o1_ref, x_ref, vec_ref, wo_own, wo_other, wq_own, wq_other, kv_ref,
                  x1_ref, a2_ref, q2_ref):
    core = core_ref[0]
    mine, theirs = halves(core, joined(o1_ref))
    x1 = (
        x_ref[...].astype(F32)
        + dot(mine, rows_of(wo_own))
        + dot(theirs, rows_of(wo_other))
        + vec_ref[10:11]
    )
    x1_ref[...] = x1
    a, _, _ = norm_forward(x1, vec_ref[1:2], vec_ref[5:6])
    mine, theirs = halves(core, a)
    mine, theirs = mine.astype(BF), theirs.astype(BF)
    a2_ref[0] = mine
    a2_ref[1] = theirs
    q2 = dot(mine, rows_of(wq_own)) + dot(theirs, rows_of(wq_other)) + vec_ref[11:12]
    for g in range(GROUPS):
        q2_ref[g, :BLOCK] = q2[:, g * LANES:(g + 1) * LANES].astype(BF)
        q2_ref[g, BLOCK:] = kv_ref[g]


def ffn_kernel(core_ref, o2_ref, x1_ref, vec_ref, upb_ref, cot_ref, wo_own, wo_other,
               up_own, up_other, dn_own, dn_other,
               out_ref, g2_ref, e2_ref, do2_ref, a3_ref, e3_ref, hid_ref, ep_ref, small_ref,
               dupb_ref, gup_ref, gdn_ref, go_ref,
               x2_scr, acc_scr, pre_scr, hid_scr, da_scr, dh_scr, a3t_scr):
    s = pl.program_id(0)
    t = lax.rem(s, 8)
    core = core_ref[0]

    @pl.when(s == 0)
    def _():
        mine, theirs = halves(core, joined(o2_ref))
        x2 = (
            x1_ref[...]
            + dot(mine, rows_of(wo_own))
            + dot(theirs, rows_of(wo_other))
            + vec_ref[13:14]
        )
        x2_scr[...] = x2
        a, _, _ = norm_forward(x2, vec_ref[2:3], vec_ref[6:7])
        mine, theirs = halves(core, a)
        a3_ref[0] = mine.astype(BF)
        a3_ref[1] = theirs.astype(BF)
        acc_scr[...] = jnp.zeros_like(acc_scr)

    @pl.when(s < 8)
    def _():
        pre = dot(a3_ref[0], rows_of(up_own)) + dot(a3_ref[1], rows_of(up_other)) + upb_ref[...]
        pre_scr[t] = pre
        hidden = (pre * jax.nn.sigmoid(pre)).astype(BF)
        hid_scr[t] = hidden

        @pl.when(t < 4)
        def _():
            acc_scr[...] += dot(hidden, plane_rows(dn_own))

        @pl.when(t >= 4)
        def _():
            acc_scr[...] += dot(hidden, plane_rows(dn_other))

    @pl.when(s == 7)
    def _():
        x3 = x2_scr[...] + acc_scr[...] + vec_ref[14:15]
        y, n4, r4 = norm_forward(x3, vec_ref[3:4], vec_ref[7:8])
        out_ref[...] = y
        g3, dgain, dshift = norm_backward(cot_ref[...].astype(F32), n4, r4, vec_ref[3:4])
        acc_scr[...] = g3
        e3_ref[...] = g3.astype(BF)
        small_ref[0:1] = dgain
        small_ref[1:2] = dshift
        small_ref[2:3] = column_sum(g3)
        da_scr[...] = jnp.zeros_like(da_scr)
        a3t_scr[...] = a3_ref[1].astype(F32).T

    @pl.when(s >= 8)
    def _():
        e3 = e3_ref[...]

        @pl.when(t < 4)
        def _():
            dh_scr[...] = dot_nt(e3, plane_rows(dn_own))
            hid_ref[...] = hid_scr[t]

        @pl.when(t >= 4)
        def _():
            dh_scr[...] = dot_nt(e3, plane_rows(dn_other))
            gdn_ref[:, 0] = dot_tn(hid_scr[t], e3).astype(BF).reshape(16, 32, D)

        pre = pre_scr[t]
        sig = jax.nn.sigmoid(pre)
        dpre = dh_scr[...] * sig * (1.0 + pre * (1.0 - sig))
        ep = dpre.astype(BF)
        ep_ref[...] = ep
        dupb_ref[...] = column_sum(dpre)
        put_rows(gup_ref, dot(a3t_scr[...].astype(BF), ep))
        da_scr[0] += dot_nt(ep, rows_of(up_own))
        da_scr[1] += dot_nt(ep, rows_of(up_other))

    @pl.when(s == 15)
    def _():
        da3 = ordered(core, da_scr[0], da_scr[1])
        _, n3, r3 = norm_forward(x2_scr[...], vec_ref[2:3], vec_ref[6:7])
        back, dgain, dshift = norm_backward(da3, n3, r3, vec_ref[2:3])
        g2 = acc_scr[...] + back
        g2_ref[...] = g2
        small_ref[3:4] = dgain
        small_ref[4:5] = dshift
        small_ref[5:6] = column_sum(g2)
        e2 = g2.astype(BF)
        e2_ref[...] = e2
        put_groups(
            do2_ref, ordered(core, dot_nt(e2, rows_of(wo_own)), dot_nt(e2, rows_of(wo_other)))
        )
        put_rows(go_ref, dot_tn(halves(core, joined(o2_ref))[1], e2))


def ffn_grad_kernel(core_ref, a3_ref, ep_ref, hid_ref, e3_ref, up_ref, dn_ref, o2_ref, e2_ref,
                    go_ref, out_ref):
    m = pl.program_id(0)

    @pl.when(m < 4)
    def _():
        put_rows(out_ref, dot_tn(a3_ref[0], ep_ref[...]), up_ref)

    @pl.when(m == 8)
    def _():
        o2 = halves(core_ref[0], joined(o2_ref))[0]
        put_rows(out_ref, dot_tn(o2, e2_ref[...]), go_ref)

    @pl.when((m >= 4) & (m < 8))
    def _():
        g = dot_tn(hid_ref[...], e3_ref[...]).reshape(16, 32, D)
        out_ref[:, 0] = (g + dn_ref[:, 0].astype(F32)).astype(BF)


def cross_back_kernel(core_ref, b2_ref, x1_ref, g2_ref, vec_ref, wq_own, wq_other,
                      wo_own, wo_other, g1_ref, e1_ref, do1_ref, small_ref):
    core = core_ref[0]
    dq = joined(b2_ref, 0, BLOCK)
    da2 = ordered(core, dot_nt(dq, rows_of(wq_own)), dot_nt(dq, rows_of(wq_other)))
    _, n2, r2 = norm_forward(x1_ref[...], vec_ref[1:2], vec_ref[5:6])
    back, dgain, dshift = norm_backward(da2, n2, r2, vec_ref[1:2])
    g1 = g2_ref[...] + back
    g1_ref[...] = g1
    e1 = g1.astype(BF)
    e1_ref[...] = e1
    put_groups(
        do1_ref, ordered(core, dot_nt(e1, rows_of(wo_own)), dot_nt(e1, rows_of(wo_other)))
    )
    small_ref[0:1] = dgain
    small_ref[1:2] = dshift
    small_ref[2:3] = column_sum(g1)
    small_ref[3:4] = column_sum(dq.astype(F32))
    small_ref[4:5] = column_sum(joined(b2_ref, BLOCK + 128, 128).astype(F32))


def text_back_kernel(core_ref, b2_ref, wk_own, wk_other, wv_own, wv_other, out_ref):
    dk = joined(b2_ref, BLOCK, 128)
    dv = joined(b2_ref, BLOCK + 128, 128)
    mine = dot_nt(dk, rows_of(wk_own)) + dot_nt(dv, rows_of(wv_own))
    theirs = dot_nt(dk, rows_of(wk_other)) + dot_nt(dv, rows_of(wv_other))
    out_ref[...] = ordered(core_ref[0], mine, theirs)


def cross_grad_kernel(half, core_ref, a2_ref, enc_ref, b2_ref, *rest):
    other = rest[0] if len(rest) == 2 else None
    out_ref = rest[-1]
    core = core_ref[0]
    m = pl.program_id(0)

    def emit(at, a, g):
        @pl.when(m == at)
        def _():
            put_rows(out_ref, dot_tn(a(), g()), other)

    emit(0, lambda: a2_ref[half], lambda: joined(b2_ref, 0, BLOCK))
    emit(1, lambda: halves(core, enc_ref[...])[half], lambda: joined(b2_ref, BLOCK, 128))
    emit(2, lambda: halves(core, enc_ref[...])[half], lambda: joined(b2_ref, BLOCK + 128, 128))


def self_grad_kernel(half, core_ref, a_ref, d_ref, o1_ref, e1_ref, *rest):
    other = rest[0] if len(rest) == 2 else None
    out_ref = rest[-1]
    n = 3 * LANES
    a = a_ref[...].reshape(GROUPS * BLOCK, a_ref.shape[2])
    g = dot_tn(a, d_ref[...].reshape(GROUPS * BLOCK, n))
    go = dot_tn(halves(core_ref[0], joined(o1_ref))[half], e1_ref[...])
    if other is not None:
        g = g + other[:, :n].astype(F32)
        go = go + other[:, n:].astype(F32)
    out_ref[:, :n] = g.astype(BF)
    out_ref[:, n:n + D] = go.astype(BF)


def small_kernel(core_ref, small_ref, recv_ref, big_ref, out_ref):
    out_ref[...] = (small_ref[...] + recv_ref[...].astype(F32)).astype(BF)


def self_back_kernel(core_ref, d_ref, own_ref, other_ref, x_ref, g1_ref, vec_ref,
                     out_ref, small_ref, sum_ref, da_scr):
    g = pl.program_id(0)

    @pl.when(g == 0)
    def _():
        da_scr[...] = jnp.zeros_like(da_scr)

    d = joined(d_ref)
    sum_ref[0] = column_sum(d.astype(F32))
    da_scr[0] += dot_nt(d, rows_of(own_ref))
    da_scr[1] += dot_nt(d, rows_of(other_ref))

    @pl.when(g == pl.num_programs(0) - 1)
    def _():
        da1 = ordered(core_ref[0], da_scr[0], da_scr[1])
        _, n1, r1 = norm_forward(x_ref[...].astype(F32), vec_ref[0:1], vec_ref[4:5])
        back, dgain, dshift = norm_backward(da1, n1, r1, vec_ref[0:1])
        out_ref[...] = g1_ref[...] + back
        small_ref[0:1] = dgain
        small_ref[1:2] = dshift


def whole(shape):
    return pl.BlockSpec(shape, lambda *a: (0,) * len(shape))


def matrix(m):
    return pl.BlockSpec((16, 1, 32, D), lambda *a: (0, m, 0, 0))


def without(kernel, first, count):
    def run(*refs):
        return kernel(*refs[:first], *refs[first + count:])

    return run


def call(kernel, grid, in_specs, out_specs, out_shape, scratch, flops, size, after=()):
    def start(*args):
        return ordered_call(
            kernel, grid, in_specs, out_specs, out_shape, scratch, flops, size, args, after
        )

    return start


def ordered_call(
    kernel, grid, in_specs, out_specs, out_shape, scratch, flops, size, args, after
):
    return pl.pallas_call(
        without(kernel, len(args), len(after)),
        grid_spec=pltpu.PrefetchScalarGridSpec(
            num_scalar_prefetch=1,
            grid=grid,
            in_specs=list(in_specs) + [pl.BlockSpec(memory_space=pl.ANY)] * len(after),
            out_specs=out_specs,
            scratch_shapes=scratch,
        ),
        out_shape=out_shape,
        compiler_params=params(),
        cost_estimate=cost(flops, size),
    )(*args, *after)


def shape(dims, dtype=BF):
    return jax.ShapeDtypeStruct(dims, dtype)


def by_core(x):
    lead = x.shape[:-1]
    return x.reshape(*lead, 8, 2, HALF).swapaxes(-3, -2).reshape(*lead, D)


def by_place(x):
    lead = x.shape[:-1]
    return x.reshape(*lead, 2, 8, HALF).swapaxes(-3, -2).reshape(*lead, D)


def swap(x):
    return lax.ppermute(x, "c", [(0, 1), (1, 0)])


def local(
    tokens,
    encoded,
    unit_ids,
    text_ids,
    cotangent,
    attn_in,
    attn_out,
    w_up,
    w_down,
    norm_gains,
    shifts,
    biases,
    up_bias,
):
    core = lax.axis_index("c")
    first_core = core == 0
    core_arg = core.astype(jnp.int32).reshape(1)
    rows = tokens.shape[1]
    text_rows = encoded.shape[1]

    def mine(x):
        return lax.dynamic_slice_in_dim(x, core * (x.shape[0] // 2), x.shape[0] // 2, 0)

    def theirs(x):
        return lax.dynamic_slice_in_dim(x, (1 - core) * (x.shape[0] // 2), x.shape[0] // 2, 0)

    in_low = by_core(attn_in.astype(BF))
    out_low = by_core(attn_out.astype(BF))
    vectors = jnp.concatenate([norm_gains, shifts, biases], axis=0).astype(BF)
    tile = jnp.concatenate(
        [
            vectors.T,
            up_bias.astype(BF).reshape(8, 4),
            jnp.zeros((8, 13), BF),
            unit_ids.reshape(8, 32).astype(BF),
            text_ids.reshape(8, 16).astype(BF),
            jnp.zeros((8, 48), BF),
        ],
        axis=1,
    )
    up_low = w_up.astype(BF).reshape(8, 2, 4, 2, 2, 4, 32).transpose(0, 3, 5, 1, 4, 2, 6)
    up_low = up_low.reshape(8, 4, D).transpose(1, 0, 2).reshape(32, D)
    down_low = by_core(w_down.astype(BF))
    attn_low = jnp.concatenate([in_low[3:6], out_low], axis=0).reshape(40, D)
    self_low = jnp.concatenate(
        [in_low[0:3].reshape(24, D), jnp.pad(tile, ((0, 0), (0, D - LANES)))], axis=0
    )
    z_pack = jnp.concatenate([up_low, down_low, attn_low, self_low], axis=0)
    z_at = lax.axis_index("z")
    z_all = jnp.zeros((4,) + z_pack.shape, BF)
    for k in range(4):
        part = z_pack if k == 0 else lax.ppermute(z_pack, "z", [(i, (i + k) % 4) for i in range(4)])
        z_all = lax.dynamic_update_slice(z_all, part[None], (lax.rem(z_at + 4 - k, 4), 0, 0))
    self_z = z_all[:, 104:].reshape(4, 4, 8, D).transpose(1, 0, 2, 3).reshape(1, 4, 32, D)
    attn_z = z_all[:, 64:104].reshape(4, 5, 8, D).transpose(1, 0, 2, 3).reshape(1, 5, 32, D)
    up_z = z_all[:, :32].reshape(4, 4, 8, D).transpose(1, 0, 2, 3).reshape(4, 32, D)
    ffn_z = jnp.concatenate([up_z, z_all[:, 32:64]], axis=0)[None]

    def over_plane(x):
        n = x.shape[1]
        y = lax.all_gather(x.reshape(n * 32, D), PLANE, axis=0, tiled=True)
        return y.reshape(16, n, 32, D)

    self_own = over_plane(self_z)
    self_other = swap(self_own)
    attn_own = over_plane(attn_z)
    ffn_own = over_plane(ffn_z)

    x = by_core(tokens[0])
    enc = by_core(encoded[0])
    cot = by_core(cotangent[0])

    tile_own, tile_other = self_own[:, 3, :, :LANES], self_other[:, 3, :, :LANES]

    def up_part(t):
        return t[:, :, 15:19].reshape(16, 4, 32).transpose(1, 0, 2).reshape(1, 2048)

    up_own, up_other = up_part(tile_own), up_part(tile_other)
    up_vec = jnp.concatenate(
        [jnp.where(first_core, up_own, up_other), jnp.where(first_core, up_other, up_own)], axis=1
    ).astype(F32)
    at = (lax.axis_index("yh"), 0, lax.axis_index("x"), 0, 0, 0)
    seq_tile = lax.dynamic_slice(
        tile_own.reshape(2, 2, 4, 4, 8, LANES), at, (1, 2, 1, 4, 8, LANES)
    )
    seq_tile = seq_tile.reshape(8, 8, LANES).astype(F32).astype(jnp.int32)
    units = seq_tile[:, :, 32:64].reshape(-1)
    texts = seq_tile[:, :, 64:80].reshape(-1)
    self_plan = key_plan(units, units, True)
    cross_plan = key_plan(units, texts, False)

    qkv, _, vec, a1 = call(
        qkv_kernel,
        (3,),
        [
            whole((rows, D)),
            pl.BlockSpec((16, 1, 32, LANES), lambda m, c: (0, 3, 0, 0)),
            pl.BlockSpec((16, 1, 32, LANES), lambda m, c: (0, 3, 0, 0)),
            pl.BlockSpec((16, 1, 32, D), lambda m, c: (0, m, 0, 0)),
            pl.BlockSpec((16, 1, 32, D), lambda m, c: (0, m, 0, 0)),
        ],
        [
            pl.BlockSpec((GROUPS, rows, LANES), lambda m, c: (0, 0, m)),
            whole((2, rows, 512)),
            whole((16, D)),
            whole((rows, D)),
        ],
        [
            shape((GROUPS, rows, 384)),
            shape((2, rows, 512)),
            shape((16, D), F32),
            shape((rows, D)),
        ],
        [],
        1.6e9,
        8e6,
    )(core_arg, x, self_own, self_other, self_own, self_other)
    qkv = lax.all_to_all(qkv, SEQ, 0, 0, tiled=True)
    self_keys = ((GROUPS, rows, LANES), (0, 0, 1), (0, 0, 2))
    o1_heads, lse1 = attend_fwd(self_plan, qkv, qkv, self_keys)
    (attn_own, a1, _) = lax.optimization_barrier((attn_own, a1, o1_heads))
    attn_other = swap(attn_own)
    a1_all = lax.all_gather(a1, SEQ, axis=0, tiled=False)
    o1 = lax.all_to_all(o1_heads, SEQ, 0, 0, tiled=True)

    kv2 = call(
        text_kernel,
        (2,),
        [
            whole((text_rows, D)),
            whole((16, D)),
            pl.BlockSpec((16, 1, 32, D), lambda m, c: (0, 1 + m, 0, 0)),
            pl.BlockSpec((16, 1, 32, D), lambda m, c: (0, 1 + m, 0, 0)),
        ],
        pl.BlockSpec((GROUPS, text_rows, LANES), lambda m, c: (0, m, 0)),
        shape((GROUPS, 2 * text_rows, LANES)),
        [],
        0.5e9,
        4e6,
        after=(o1_heads,),
    )(core_arg, enc, vec, attn_own, attn_other)

    x1, a2, q2 = call(
        middle_kernel,
        (1,),
        [whole((GROUPS, rows, LANES)), whole((rows, D)), whole((16, D))]
        + [matrix(3), matrix(3), matrix(0), matrix(0), whole((GROUPS, 2 * text_rows, LANES))],
        [whole((rows, D)), whole((2, rows, 512)), whole((GROUPS, 2 * rows, LANES))],
        [shape((rows, D), F32), shape((2, rows, 512)), shape((GROUPS, 2 * rows, LANES))],
        [],
        1.1e9,
        8e6,
    )(core_arg, o1, x, vec, attn_own, attn_other, attn_own, attn_other, kv2)
    q2 = lax.all_to_all(q2, SEQ, 0, 0, tiled=True)
    cross_keys = ((GROUPS, text_rows, LANES), (0, 2, 0), (0, 3, 0))
    o2_heads, lse2 = attend_fwd(cross_plan, q2, q2, cross_keys)
    o2 = lax.all_to_all(o2_heads, SEQ, 0, 0, tiled=True)
    (ffn_own, _) = lax.optimization_barrier((ffn_own, o2))
    ffn_other = swap(ffn_own)

    def block_of(s, c):
        t = lax.rem(s, 8)
        return jnp.where(t < 4, c[0], 1 - c[0]) * 4 + lax.rem(t, 4)

    def back_block(s, c):
        return block_of(jnp.maximum(s, 8), c)

    up_spec = pl.BlockSpec(
        (16, 1, 32, 512), lambda s, c: (0, block_of(s, c) // 2, 0, lax.rem(block_of(s, c), 2))
    )
    gup_spec = pl.BlockSpec(
        (16, 1, 32, 512), lambda s, c: (0, back_block(s, c) // 2, 0, lax.rem(back_block(s, c), 2))
    )
    (layer_out, g2, e2, do2, a3, e3, hidden, ep, small_f, dup_bias, gup, gdn, go) = call(
        ffn_kernel,
        (16,),
        [
            whole((GROUPS, rows, LANES)),
            whole((rows, D)),
            whole((16, D)),
            pl.BlockSpec((1, 512), lambda s, c: (0, block_of(s, c))),
            whole((rows, D)),
            matrix(4),
            matrix(4),
            up_spec,
            up_spec,
            pl.BlockSpec(
                (16, 1, 32, D), lambda s, c: (0, 4 + jnp.minimum(lax.rem(s, 8), 3), 0, 0)
            ),
            pl.BlockSpec(
                (16, 1, 32, D), lambda s, c: (0, jnp.maximum(lax.rem(s, 8), 4), 0, 0)
            ),
        ],
        [
            whole((rows, D)),
            whole((rows, D)),
            whole((rows, D)),
            whole((GROUPS, rows, LANES)),
            whole((2, rows, 512)),
            whole((rows, D)),
            pl.BlockSpec((rows, 512), lambda s, c: (0, jnp.clip(s - 8, 0, 3))),
            pl.BlockSpec((rows, 512), lambda s, c: (0, back_block(s, c))),
            whole((8, D)),
            pl.BlockSpec((1, 512), lambda s, c: (0, back_block(s, c))),
            gup_spec,
            pl.BlockSpec((16, 1, 32, D), lambda s, c: (0, jnp.maximum(s - 12, 0), 0, 0)),
            matrix(0),
        ],
        [
            shape((rows, D), F32),
            shape((rows, D), F32),
            shape((rows, D)),
            shape((GROUPS, rows, LANES)),
            shape((2, rows, 512)),
            shape((rows, D)),
            shape((rows, FF // 2)),
            shape((rows, FF)),
            shape((8, D), F32),
            shape((1, FF), F32),
            shape((16, 4, 32, D)),
            shape((16, 4, 32, D)),
            shape((16, 1, 32, D)),
        ],
        [
            pltpu.VMEM((rows, D), F32),
            pltpu.VMEM((rows, D), F32),
            pltpu.VMEM((8, rows, 512), F32),
            pltpu.VMEM((8, rows, 512), BF),
            pltpu.VMEM((2, rows, 512), F32),
            pltpu.VMEM((rows, 512), F32),
            pltpu.VMEM((512, rows), F32),
        ],
        16e9,
        50e6,
    )(core_arg, o2, x1, vec, up_vec, cot, attn_own, attn_other, ffn_own, ffn_other,
      ffn_own, ffn_other)
    do2 = lax.all_to_all(do2, SEQ, 0, 0, tiled=True)
    gup_recv, gdn_recv, go_recv = swap(gup), swap(gdn), swap(go)

    back2_heads = attend_bwd(
        cross_plan, lse2, q2, q2, o2_heads, do2, cross_keys, False, after=(a1_all,)
    )
    back2 = lax.all_to_all(back2_heads, SEQ, 0, 0, tiled=True)
    ffn_grad = call(
        ffn_grad_kernel,
        (9,),
        [
            whole((2, rows, 512)),
            pl.BlockSpec((rows, D), lambda m, c: (0, jnp.minimum(m, 3))),
            pl.BlockSpec((rows, 512), lambda m, c: (0, jnp.clip(m - 4, 0, 3))),
            whole((rows, D)),
            pl.BlockSpec((16, 1, 32, D), lambda m, c: (0, jnp.minimum(m, 3), 0, 0)),
            pl.BlockSpec((16, 1, 32, D), lambda m, c: (0, jnp.clip(m - 4, 0, 3), 0, 0)),
            whole((GROUPS, rows, LANES)),
            whole((rows, D)),
            matrix(0),
        ],
        pl.BlockSpec((16, 1, 32, D), lambda m, c: (0, m, 0, 0)),
        shape((16, 12, 32, D)),
        [],
        2.4e9,
        20e6,
        after=(back2_heads,),
    )(core_arg, a3, ep, hidden, e3, gup_recv, gdn_recv, o2, e2, go_recv)

    def cross_grads(half, recv, into, after=()):
        args = (core_arg, a2, enc, back2) + tuple(recv)
        later = after if into is None else (into,)
        first, blocks = (0, 3) if into is None else (9, 12)
        block = pl.BlockSpec((16, 1, 32, D), lambda m, c: (0, m, 0, 0))
        return pl.pallas_call(
            without(functools.partial(cross_grad_kernel, half), len(args), len(later)),
            grid_spec=pltpu.PrefetchScalarGridSpec(
                num_scalar_prefetch=1,
                grid=(3,),
                in_specs=[
                    whole((2, rows, 512)),
                    whole((text_rows, D)),
                    whole((GROUPS, rows + 2 * text_rows, LANES)),
                ]
                + [block] * len(recv)
                + [pl.BlockSpec(memory_space=pl.ANY)] * len(later),
                out_specs=pl.BlockSpec((16, 1, 32, D), lambda m, c: (0, first + m, 0, 0)),
            ),
            out_shape=shape((16, blocks, 32, D)),
            input_output_aliases={} if into is None else {len(args): 0},
            compiler_params=params(),
            cost_estimate=cost(0.6e9, 5e6),
        )(*args, *later)

    cross_theirs = cross_grads(1, [], None, (ffn_grad,))
    cross_recv = swap(cross_theirs)

    g1, e1, do1, small_c = call(
        cross_back_kernel,
        (1,),
        [whole((GROUPS, rows + 2 * text_rows, LANES)), whole((rows, D)), whole((rows, D))]
        + [whole((16, D)), matrix(0), matrix(0), matrix(3), matrix(3)],
        [whole((rows, D)), whole((rows, D)), whole((GROUPS, rows, LANES)), whole((8, D))],
        [
            shape((rows, D), F32),
            shape((rows, D)),
            shape((GROUPS, rows, LANES)),
            shape((8, D), F32),
        ],
        [],
        1.1e9,
        10e6,
        after=(ffn_grad, cross_theirs),
    )(core_arg, back2, x1, g2, vec, attn_own, attn_other, attn_own, attn_other)
    do1_rows = do1
    do1 = lax.all_to_all(do1, SEQ, 0, 0, tiled=True)
    (cross_recv, _) = lax.optimization_barrier((cross_recv, do1_rows))
    all_grads = cross_grads(0, [cross_recv], ffn_grad)
    grads = lax.psum_scatter(
        all_grads.reshape(16 * 12 * 32, D), PLANE, scatter_dimension=0, tiled=True
    ).reshape(12, 32, D)

    dqkv_heads = attend_bwd(
        self_plan, lse1, qkv, qkv, o1_heads, do1, self_keys, True, after=(all_grads,)
    )
    dqkv = lax.all_to_all(dqkv_heads, SEQ, 0, 0, tiled=True)
    width = 3 * LANES + D + LANES

    def self_grads(half, recv, n, later):
        at = (lambda m, c: (0, 0, c[0])) if half == 0 else (lambda m, c: (0, 0, 1 - c[0]))
        return call(
            functools.partial(self_grad_kernel, half),
            (1,),
            [
                pl.BlockSpec((GROUPS, rows, 512), at),
                whole((GROUPS, rows, 3 * LANES)),
                whole((GROUPS, rows, LANES)),
                whole((rows, D)),
            ]
            + [whole((512, 3 * LANES + D))] * len(recv),
            whole((512, n)),
            shape((512, n)),
            [],
            1.1e9,
            8e6,
            after=later,
        )(core_arg, a1_all, dqkv_heads, o1, e1, *recv)

    self_theirs = self_grads(1, [], 3 * LANES + D, ())
    self_recv = swap(self_theirs)
    d_enc = call(
        text_back_kernel,
        (1,),
        [whole((GROUPS, rows + 2 * text_rows, LANES))]
        + [matrix(1), matrix(1), matrix(2), matrix(2)],
        whole((text_rows, D)),
        shape((text_rows, D), F32),
        [],
        0.5e9,
        5e6,
        after=(self_theirs,),
    )(core_arg, back2, attn_own, attn_other, attn_own, attn_other)
    own = self_grads(0, [self_recv], width, (d_enc,))

    d_tokens, small_s, dsum = call(
        self_back_kernel,
        (3,),
        [
            pl.BlockSpec((GROUPS, rows, LANES), lambda m, c: (0, 0, m)),
            pl.BlockSpec((16, 1, 32, D), lambda m, c: (0, m, 0, 0)),
            pl.BlockSpec((16, 1, 32, D), lambda m, c: (0, m, 0, 0)),
            whole((rows, D)),
            whole((rows, D)),
            whole((16, D)),
        ],
        [
            whole((rows, D)),
            whole((8, D)),
            pl.BlockSpec((1, 1, D), lambda m, c: (m, 0, 0)),
        ],
        [shape((rows, D), F32), shape((8, D), F32), shape((3, 1, D), F32)],
        [pltpu.VMEM((2, rows, 512), F32)],
        1.6e9,
        9e6,
        after=(own,),
    )(core_arg, dqkv, self_own, self_other, x, g1, vec)

    small = jnp.concatenate(
        [
            small_s[0:1],
            small_c[0:1],
            small_f[3:4],
            small_f[0:1],
            small_s[1:2],
            small_c[1:2],
            small_f[4:5],
            small_f[1:2],
            dsum[0],
            dsum[2],
            small_c[2:3],
            small_c[3:4],
            small_c[4:5],
            small_f[5:6],
            small_f[2:3],
        ],
        axis=0,
    )
    up_sums = dup_bias.reshape(2, 4, 2, 2, 4, 32).transpose(0, 2, 4, 3, 1, 5).reshape(D, 4)
    small = jnp.concatenate([small.T, up_sums, jnp.zeros((D, LANES - 19), F32)], axis=1)
    small_recv = swap(theirs(small).astype(BF))
    last = pl.pallas_call(
        small_kernel,
        grid_spec=pltpu.PrefetchScalarGridSpec(
            num_scalar_prefetch=1,
            grid=(1,),
            in_specs=[whole((512, LANES)), whole((512, LANES)), pl.BlockSpec(memory_space=pl.ANY)],
            out_specs=pl.BlockSpec((512, LANES), lambda m, c: (0, 3 + D // LANES)),
        ),
        out_shape=shape((512, width)),
        input_output_aliases={3: 0},
        compiler_params=params(),
        cost_estimate=cost(1e5, 5e5),
    )(core_arg, mine(small), small_recv, own)
    last = lax.all_to_all(last.reshape(64, 8, width), CHIPS, 0, 0, tiled=True)
    heads = jnp.sum(last[:, :, :3 * LANES].astype(F32).reshape(8, 8, 8, 3 * LANES), axis=0)
    last = jnp.sum(last[:, :, 3 * LANES:].astype(F32), axis=0)

    z_grad = jnp.concatenate(
        [
            grads[:4].reshape(4, 4, 8, D).transpose(1, 0, 2, 3).reshape(4, 32, D),
            grads[4:8],
            grads[8:].reshape(4, 4, 8, D).transpose(1, 0, 2, 3).reshape(4, 32, D),
        ],
        axis=1,
    )
    z_grad = lax.all_to_all(z_grad, "z", 0, 0, tiled=True)
    z_grad = jnp.sum(z_grad.astype(F32), axis=0)
    d_up = z_grad[:32].reshape(4, 8, D).transpose(1, 0, 2).reshape(8, 2, 4, 2, 2, 4, 32)
    d_up = d_up.transpose(0, 3, 5, 1, 4, 2, 6).reshape(8, FF)
    d_down = by_place(z_grad[32:64])
    heads = heads.reshape(GROUPS, 8, 3, LANES).transpose(2, 1, 0, 3).reshape(3, 8, D)
    attn_grad = z_grad[64:].reshape(4, 8, D)
    d_in = by_place(jnp.concatenate([heads, attn_grad[1:]], axis=0))
    d_out = by_place(jnp.stack([last[:, :D], attn_grad[0]]))
    d_vec = last[:, D:D + 15].T
    d_up_bias = last[:, D + 15:D + 19].reshape(32)
    return (
        by_place(layer_out)[None],
        by_place(d_tokens)[None],
        by_place(d_enc)[None],
        d_in,
        d_out,
        d_up,
        d_down,
        d_vec[0:4],
        d_vec[4:8],
        d_vec[8:15],
        d_up_bias,
    )


def solution(mesh):
    fine = Mesh(mesh.devices.reshape(2, 4, 2, 2, 4), ("yh", "x", "c", "yl", "z"))
    fsdp = ("yh", "x", "c")
    every = fsdp + SEQ
    placed = (
        P(fsdp, SEQ, None),
        P(fsdp, SEQ, None),
        P(fsdp, SEQ),
        P(fsdp, SEQ),
        P(fsdp, SEQ, None),
        P(None, every, None),
        P(None, every, None),
        P(every, None),
        P(every, None),
        P(None, every),
        P(None, every),
        P(None, every),
        P(every),
    )
    return jax.shard_map(
        local,
        mesh=fine,
        in_specs=placed,
        out_specs=(
            P(fsdp, SEQ, None),
            P(fsdp, SEQ, None),
            P(fsdp, SEQ, None),
            P(None, every, None),
            P(None, every, None),
            P(every, None),
            P(every, None),
            P(None, every),
            P(None, every),
            P(None, every),
            P(every),
        ),
        check_vma=False,
    )
```

```python
import functools

import jax
import jax.numpy as jnp
from jax import lax
from jax.experimental import pallas as pl
from jax.experimental.pallas import tpu as pltpu
from jax.sharding import Mesh
from jax.sharding import PartitionSpec as P

D = 1024
FF = 4096
GROUPS = 8
LANES = 128
HALF = 64
BLOCK = 256
EPS = 1e-05
MASKED = -1e30

SEQ = ("yl", "z")
CHIPS = ("yh", "x", "yl", "z")
PLANE = ("yh", "yl", "x")
BF = jnp.bfloat16
F32 = jnp.float32


def dot(a, b):
    return jnp.dot(a, b, preferred_element_type=F32)


def dot_nt(a, b):
    return lax.dot_general(a, b, (((1,), (1,)), ((), ())), preferred_element_type=F32)


def dot_tn(a, b):
    return lax.dot_general(a, b, (((0,), (0,)), ((), ())), preferred_element_type=F32)


def stack_cols(xt):
    zero = jnp.zeros((HALF, xt.shape[1]), xt.dtype)
    return jnp.concatenate(
        [
            jnp.concatenate([xt[:HALF], zero], axis=0),
            jnp.concatenate([zero, xt[HALF:]], axis=0),
        ],
        axis=1,
    )


def stack_rows(x):
    lane = lax.broadcasted_iota(jnp.int32, x.shape, 1)
    zero = jnp.zeros_like(x)
    return jnp.concatenate(
        [jnp.where(lane < HALF, x, zero), jnp.where(lane < HALF, zero, x)], axis=0
    )


def unstack_cols(xt):
    n = xt.shape[1] // 2
    return jnp.concatenate([xt[:HALF, :n], xt[HALF:, n:]], axis=0)


def allowed_mask(j, start, length):
    pos = lax.broadcasted_iota(jnp.int32, (BLOCK, start.shape[1]), 0)
    off = pos - (start - j * BLOCK)
    return off.astype(jnp.uint32) < length.astype(jnp.uint32)


def attn_fwd_kernel(lo_ref, hi_ref, start_ref, len_ref, q_ref, k_ref, v_ref, o_ref, lse_ref,
                    vt_scr, s_scr, o_scr):
    i = pl.program_id(0)
    nk = vt_scr.shape[0]
    per = BLOCK // k_ref.shape[1]

    @pl.when(i == 0)
    def _():
        for j in range(nk):
            vt_scr[j] = v_ref[j * per:(j + 1) * per].reshape(BLOCK, LANES).astype(F32).T

    q = q_ref[0] * jnp.asarray(0.125, BF)
    qst = stack_cols(q.T)
    start = jnp.concatenate([start_ref[0], start_ref[0]], axis=1)
    length = jnp.concatenate([len_ref[0], len_ref[0]], axis=1)
    lo, hi = lo_ref[i], hi_ref[i]
    width = 2 * BLOCK

    def first(j, m8):
        k = k_ref[pl.ds(j * per, per)].reshape(BLOCK, LANES)
        s = dot(k, qst)
        s = jnp.where(allowed_mask(j, start, length), s, MASKED)
        s_scr[pl.ds(pl.multiple_of(j * BLOCK, BLOCK), BLOCK)] = s
        return jnp.maximum(m8, jnp.max(s.reshape(BLOCK // 8, 8, width), axis=0))

    m8 = lax.fori_loop(lo, hi, first, jnp.full((8, width), MASKED, F32))
    m = jnp.max(m8, axis=0, keepdims=True)
    o_scr[...] = jnp.zeros_like(o_scr)

    def second(j, l8):
        p = jnp.exp(s_scr[pl.ds(pl.multiple_of(j * BLOCK, BLOCK), BLOCK)] - m)
        o_scr[...] += dot(vt_scr[j].astype(BF), p.astype(BF))
        return l8 + jnp.sum(p.reshape(BLOCK // 8, 8, width), axis=0)

    l8 = lax.fori_loop(lo, hi, second, jnp.zeros((8, width), F32))
    l = jnp.sum(l8, axis=0, keepdims=True)
    lse_ref[0] = m + jnp.log(l)
    ot = unstack_cols(o_scr[...] * (1.0 / l))
    o_ref[0] = ot.T.astype(BF)


def attn_bwd_kernel(wide, lo_ref, hi_ref, start_ref, len_ref, lse_ref, q_ref, k_ref, v_ref, o_ref,
                    do_ref, out_ref, kt_scr, dq_scr, dk_scr, dv_scr):
    i = pl.program_id(0)
    nk = kt_scr.shape[0]
    kb = k_ref.shape[1]
    per = BLOCK // kb

    @pl.when(i == 0)
    def _():
        for j in range(nk):
            kt_scr[j] = k_ref[j * per:(j + 1) * per].reshape(BLOCK, LANES).astype(F32).T
        dk_scr[...] = jnp.zeros_like(dk_scr)
        dv_scr[...] = jnp.zeros_like(dv_scr)

    q = q_ref[0] * jnp.asarray(0.125, BF)
    do = do_ref[0]
    qs, qst = stack_rows(q), stack_cols(q.T)
    dot_t = do.T
    dos, dost = stack_rows(do), stack_cols(dot_t)
    prod = dot_t.astype(F32) * o_ref[0].T.astype(F32)
    delta = jnp.concatenate(
        [
            jnp.sum(prod[:HALF], axis=0, keepdims=True),
            jnp.sum(prod[HALF:], axis=0, keepdims=True),
        ],
        axis=1,
    )
    lse = lse_ref[0]
    start = jnp.concatenate([start_ref[0], start_ref[0]], axis=1)
    length = jnp.concatenate([len_ref[0], len_ref[0]], axis=1)
    dq_scr[...] = jnp.zeros_like(dq_scr)

    def body(j, carry):
        k = k_ref[pl.ds(j * per, per)].reshape(BLOCK, LANES)
        v = v_ref[pl.ds(j * per, per)].reshape(BLOCK, LANES)
        s = jnp.where(allowed_mask(j, start, length), dot(k, qst), MASKED)
        p = jnp.exp(s - lse)
        ds = (p * (dot(v, dost) - delta)).astype(BF)
        rows = pl.ds(pl.multiple_of(j * BLOCK, BLOCK), BLOCK)
        dv_scr[rows] += dot(p.astype(BF), dos)
        dk_scr[rows] += dot(ds, qs)
        dq_scr[...] += dot(kt_scr[j].astype(BF), ds)
        return carry

    lax.fori_loop(lo_ref[i], hi_ref[i], body, 0)
    dq = (unstack_cols(dq_scr[...]) * 0.125).T.astype(BF)
    if wide:
        out_ref[i, :, :LANES] = dq
    else:
        out_ref[i, :BLOCK] = dq

    @pl.when(i == pl.num_programs(0) - 1)
    def _():
        n = GROUPS
        dk = dk_scr[...].astype(BF).reshape(n, kb, LANES)
        dv = dv_scr[...].astype(BF).reshape(n, kb, LANES)
        if wide:
            out_ref[:, :, LANES:2 * LANES] = dk
            out_ref[:, :, 2 * LANES:] = dv
        else:
            out_ref[:, BLOCK:BLOCK + kb] = dk
            out_ref[:, BLOCK + kb:] = dv


def row_spec(n):
    return pl.BlockSpec((1, 1, n), lambda i, lo, hi: (i, 0, 0))


def block_rows():
    return pl.BlockSpec((1, BLOCK, LANES), lambda i, lo, hi: (i, 0, 0))


def key_specs(kshape, kblock, vblock):
    return [
        pl.BlockSpec(kshape, lambda i, lo, hi: kblock),
        pl.BlockSpec(kshape, lambda i, lo, hi: vblock),
    ]


def attend_fwd(plan, q, kv, keys_at, after=()):
    lo, hi, start, length = plan
    nq = lo.shape[0]
    keys = keys_at[0][0] * keys_at[0][1]
    return pl.pallas_call(
        without(attn_fwd_kernel, 7, len(after)),
        grid_spec=pltpu.PrefetchScalarGridSpec(
            num_scalar_prefetch=2,
            grid=(nq,),
            in_specs=[row_spec(BLOCK), row_spec(BLOCK), block_rows()]
            + key_specs(*keys_at)
            + [pl.BlockSpec(memory_space=pl.ANY)] * len(after),
            out_specs=[block_rows(), row_spec(2 * BLOCK)],
            scratch_shapes=[
                pltpu.VMEM((keys // BLOCK, LANES, BLOCK), F32),
                pltpu.VMEM((keys, 2 * BLOCK), F32),
                pltpu.VMEM((LANES, 2 * BLOCK), F32),
            ],
        ),
        out_shape=[
            jax.ShapeDtypeStruct((nq, BLOCK, LANES), BF),
            jax.ShapeDtypeStruct((nq, 1, 2 * BLOCK), F32),
        ],
        compiler_params=params(),
        cost_estimate=cost(8e9, 4e6),
    )(lo, hi, start, length, q, kv, kv, *after)


def attend_bwd(plan, lse, q, kv, out, grad, keys_at, wide, after=()):
    lo, hi, start, length = plan
    nq = lo.shape[0]
    keys = keys_at[0][0] * keys_at[0][1]
    shape = (nq, BLOCK, 3 * LANES) if wide else (nq, BLOCK + 2 * keys_at[0][1], LANES)
    return pl.pallas_call(
        without(functools.partial(attn_bwd_kernel, wide), 10, len(after)),
        grid_spec=pltpu.PrefetchScalarGridSpec(
            num_scalar_prefetch=2,
            grid=(nq,),
            in_specs=[row_spec(BLOCK), row_spec(BLOCK), row_spec(2 * BLOCK), block_rows()]
            + key_specs(*keys_at)
            + [block_rows(), block_rows()]
            + [pl.BlockSpec(memory_space=pl.ANY)] * len(after),
            out_specs=pl.BlockSpec(shape, lambda i, lo, hi: (0, 0, 0)),
            scratch_shapes=[
                pltpu.VMEM((keys // BLOCK, LANES, BLOCK), F32),
                pltpu.VMEM((LANES, 2 * BLOCK), F32),
                pltpu.VMEM((keys, LANES), F32),
                pltpu.VMEM((keys, LANES), F32),
            ],
        ),
        out_shape=jax.ShapeDtypeStruct(shape, BF),
        compiler_params=params(),
        cost_estimate=cost(8e9, 6e6),
    )(lo, hi, start, length, lse, q, kv, kv, out, grad, *after)


def key_plan(query_ids, key_ids, causal):
    start = jnp.sum((key_ids[None, :] < query_ids[:, None]).astype(jnp.int32), axis=1)
    if causal:
        end = jnp.arange(query_ids.shape[0], dtype=jnp.int32) + 1
    else:
        end = jnp.sum((key_ids[None, :] <= query_ids[:, None]).astype(jnp.int32), axis=1)
    start = start.reshape(-1, 1, BLOCK)
    end = end.reshape(-1, 1, BLOCK)
    lo = jnp.min(start, axis=(1, 2)) // BLOCK
    hi = (jnp.max(end, axis=(1, 2)) + BLOCK - 1) // BLOCK
    return lo, hi, start, end - start


def params():
    return pltpu.CompilerParams(vmem_limit_bytes=58 * 2**20)


def cost(flops, size):
    return pl.CostEstimate(flops=int(flops), bytes_accessed=int(size), transcendentals=0)


def norm_forward(values, gain, shift):
    centered = values - jnp.mean(values, axis=-1, keepdims=True)
    inverse = lax.rsqrt(jnp.mean(centered * centered, axis=-1, keepdims=True) + EPS)
    normed = centered * inverse
    return normed * gain + shift, normed, inverse


def column_sum(x):
    return jnp.sum(x, axis=0, keepdims=True)


def norm_backward(upstream, normed, inverse, gain):
    scaled = upstream * gain
    inner = (
        scaled
        - jnp.mean(scaled, axis=-1, keepdims=True)
        - normed * jnp.mean(scaled * normed, axis=-1, keepdims=True)
    )
    return inverse * inner, column_sum(upstream * normed), column_sum(upstream)


PLACES = tuple(yh * 8 + yl * 4 + x for yh in range(2) for x in range(4) for yl in range(2))


def rows_of(ref):
    return jnp.concatenate([ref[p, 0] for p in PLACES], axis=0)


def plane_rows(ref):
    return ref[:, 0].reshape(512, ref.shape[3])


def put_rows(ref, value, other=None):
    for i, p in enumerate(PLACES):
        piece = value[i * 32:(i + 1) * 32]
        if other is not None:
            piece = piece + other[p, 0].astype(F32)
        ref[p, 0] = piece.astype(ref.dtype)


def halves(core, x):
    n = x.shape[1] // 2
    a, b = x[:, :n], x[:, n:]
    first = core == 0
    return jnp.where(first, a, b), jnp.where(first, b, a)


def ordered(core, mine, theirs):
    first = core == 0
    return jnp.concatenate(
        [jnp.where(first, mine, theirs), jnp.where(first, theirs, mine)], axis=1
    )


def to_place(x):
    pieces = [x[:, c * 512 + i * HALF:c * 512 + (i + 1) * HALF] for i in range(8) for c in range(2)]
    return jnp.concatenate(pieces, axis=1)


def joined(ref, first=0, count=None):
    count = ref.shape[1] if count is None else count
    return jnp.concatenate([ref[g, first:first + count] for g in range(GROUPS)], axis=1)


def put_groups(ref, value):
    for g in range(GROUPS):
        ref[g] = value[:, g * LANES:(g + 1) * LANES].astype(ref.dtype)


def qkv_kernel(core_ref, x_ref, own_tile_ref, other_tile_ref, own_ref, other_ref,
               qkv_ref, a1_ref, vec_ref, rows_ref):
    m = pl.program_id(0)
    core = core_ref[0]

    @pl.when(m == 0)
    def _():
        own = rows_of(own_tile_ref).astype(F32).T[:16]
        other = rows_of(other_tile_ref).astype(F32).T[:16]
        vec = ordered(core, own, other)
        vec_ref[...] = vec
        a, _, _ = norm_forward(x_ref[...].astype(F32), vec[0:1], vec[4:5])
        rows_ref[...] = a.astype(BF)
        mine, theirs = halves(core, a)
        a1_ref[0] = mine.astype(BF)
        a1_ref[1] = theirs.astype(BF)

    y = dot(a1_ref[0], rows_of(own_ref)) + dot(a1_ref[1], rows_of(other_ref))
    bias = vec_ref[8:9] * (m == 0).astype(F32) + vec_ref[9:10] * (m == 2).astype(F32)
    put_groups(qkv_ref, y + bias)


def text_kernel(core_ref, enc_ref, vec_ref, own_ref, other_ref, out_ref):
    m = pl.program_id(0)
    mine, theirs = halves(core_ref[0], enc_ref[...])
    y = dot(mine, rows_of(own_ref)) + dot(theirs, rows_of(other_ref))
    put_groups(out_ref, y + vec_ref[12:13] * m.astype(F32))


def middle_kernel(core_ref, o1_ref, x_ref, vec_ref, wo_own, wo_other, wq_own, wq_other, kv_ref,
                  x1_ref, a2_ref, q2_ref):
    core = core_ref[0]
    mine, theirs = halves(core, joined(o1_ref))
    x1 = (
        x_ref[...].astype(F32)
        + dot(mine, rows_of(wo_own))
        + dot(theirs, rows_of(wo_other))
        + vec_ref[10:11]
    )
    x1_ref[...] = x1
    a, _, _ = norm_forward(x1, vec_ref[1:2], vec_ref[5:6])
    mine, theirs = halves(core, a)
    mine, theirs = mine.astype(BF), theirs.astype(BF)
    a2_ref[0] = mine
    a2_ref[1] = theirs
    q2 = dot(mine, rows_of(wq_own)) + dot(theirs, rows_of(wq_other)) + vec_ref[11:12]
    for g in range(GROUPS):
        q2_ref[g, :BLOCK] = q2[:, g * LANES:(g + 1) * LANES].astype(BF)
        q2_ref[g, BLOCK:] = kv_ref[g]


def ffn_kernel(core_ref, o2_ref, x1_ref, vec_ref, upb_ref, cot_ref, wo_own, wo_other,
               up_own, up_other, dn_own, dn_other,
               out_ref, g2_ref, e2_ref, do2_ref, a3_ref, e3_ref, hid_ref, ep_ref, small_ref,
               dupb_ref, gup_ref, gdn_ref, go_ref,
               x2_scr, acc_scr, slope_scr, hid_scr, da_scr, dh_scr, a3t_scr):
    s = pl.program_id(0)
    t = lax.rem(s, 8)
    core = core_ref[0]

    @pl.when(s == 0)
    def _():
        mine, theirs = halves(core, joined(o2_ref))
        x2 = (
            x1_ref[...]
            + dot(mine, rows_of(wo_own))
            + dot(theirs, rows_of(wo_other))
            + vec_ref[13:14]
        )
        x2_scr[...] = x2
        a, _, _ = norm_forward(x2, vec_ref[2:3], vec_ref[6:7])
        mine, theirs = halves(core, a)
        a3_ref[0] = mine.astype(BF)
        a3_ref[1] = theirs.astype(BF)
        acc_scr[...] = jnp.zeros_like(acc_scr)

    @pl.when(s < 8)
    def _():
        pre = dot(a3_ref[0], rows_of(up_own)) + dot(a3_ref[1], rows_of(up_other)) + upb_ref[...]
        sig = jax.nn.sigmoid(pre)
        slope_scr[t] = sig * (1.0 + pre * (1.0 - sig))
        hidden = (pre * sig).astype(BF)
        hid_scr[t] = hidden

        @pl.when(t < 4)
        def _():
            acc_scr[...] += dot(hidden, plane_rows(dn_own))

        @pl.when(t >= 4)
        def _():
            acc_scr[...] += dot(hidden, plane_rows(dn_other))

    @pl.when(s == 7)
    def _():
        x3 = x2_scr[...] + acc_scr[...] + vec_ref[14:15]
        y, n4, r4 = norm_forward(x3, vec_ref[3:4], vec_ref[7:8])
        out_ref[...] = to_place(y)
        g3, dgain, dshift = norm_backward(cot_ref[...].astype(F32), n4, r4, vec_ref[3:4])
        acc_scr[...] = g3
        e3_ref[...] = g3.astype(BF)
        small_ref[0:1] = dgain
        small_ref[1:2] = dshift
        small_ref[2:3] = column_sum(g3)
        da_scr[...] = jnp.zeros_like(da_scr)
        a3t_scr[...] = a3_ref[1].astype(F32).T

    @pl.when(s >= 8)
    def _():
        e3 = e3_ref[...]

        @pl.when(t < 4)
        def _():
            dh_scr[...] = dot_nt(e3, plane_rows(dn_own))
            hid_ref[...] = hid_scr[t]

        @pl.when(t >= 4)
        def _():
            dh_scr[...] = dot_nt(e3, plane_rows(dn_other))
            gdn_ref[:, 0] = dot_tn(hid_scr[t], e3).astype(BF).reshape(16, 32, D)

        dpre = dh_scr[...] * slope_scr[t]
        ep = dpre.astype(BF)
        ep_ref[...] = ep
        dupb_ref[...] = column_sum(dpre)
        put_rows(gup_ref, dot(a3t_scr[...].astype(BF), ep))
        da_scr[0] += dot_nt(ep, rows_of(up_own))
        da_scr[1] += dot_nt(ep, rows_of(up_other))

    @pl.when(s == 15)
    def _():
        da3 = ordered(core, da_scr[0], da_scr[1])
        _, n3, r3 = norm_forward(x2_scr[...], vec_ref[2:3], vec_ref[6:7])
        back, dgain, dshift = norm_backward(da3, n3, r3, vec_ref[2:3])
        g2 = acc_scr[...] + back
        g2_ref[...] = g2
        small_ref[3:4] = dgain
        small_ref[4:5] = dshift
        small_ref[5:6] = column_sum(g2)
        e2 = g2.astype(BF)
        e2_ref[...] = e2
        put_groups(
            do2_ref, ordered(core, dot_nt(e2, rows_of(wo_own)), dot_nt(e2, rows_of(wo_other)))
        )
        put_rows(go_ref, dot_tn(halves(core, joined(o2_ref))[1], e2))


def ffn_grad_kernel(core_ref, a3_ref, ep_ref, hid_ref, e3_ref, up_ref, dn_ref, o2_ref, e2_ref,
                    go_ref, out_ref):
    m = pl.program_id(0)

    @pl.when(m < 4)
    def _():
        put_rows(out_ref, dot_tn(a3_ref[0], ep_ref[...]), up_ref)

    @pl.when(m == 8)
    def _():
        o2 = halves(core_ref[0], joined(o2_ref))[0]
        put_rows(out_ref, dot_tn(o2, e2_ref[...]), go_ref)

    @pl.when((m >= 4) & (m < 8))
    def _():
        g = dot_tn(hid_ref[...], e3_ref[...]).reshape(16, 32, D)
        out_ref[:, 0] = (g + dn_ref[:, 0].astype(F32)).astype(BF)


def cross_back_kernel(core_ref, b2_ref, x1_ref, g2_ref, vec_ref, wq_own, wq_other,
                      wo_own, wo_other, g1_ref, e1_ref, do1_ref, small_ref):
    core = core_ref[0]
    dq = joined(b2_ref, 0, BLOCK)
    da2 = ordered(core, dot_nt(dq, rows_of(wq_own)), dot_nt(dq, rows_of(wq_other)))
    _, n2, r2 = norm_forward(x1_ref[...], vec_ref[1:2], vec_ref[5:6])
    back, dgain, dshift = norm_backward(da2, n2, r2, vec_ref[1:2])
    g1 = g2_ref[...] + back
    g1_ref[...] = g1
    e1 = g1.astype(BF)
    e1_ref[...] = e1
    put_groups(
        do1_ref, ordered(core, dot_nt(e1, rows_of(wo_own)), dot_nt(e1, rows_of(wo_other)))
    )
    small_ref[0:1] = dgain
    small_ref[1:2] = dshift
    small_ref[2:3] = column_sum(g1)
    small_ref[3:4] = column_sum(dq.astype(F32))
    small_ref[4:5] = column_sum(joined(b2_ref, BLOCK + 128, 128).astype(F32))


def text_back_kernel(core_ref, b2_ref, wk_own, wk_other, wv_own, wv_other, out_ref):
    dk = joined(b2_ref, BLOCK, 128)
    dv = joined(b2_ref, BLOCK + 128, 128)
    mine = dot_nt(dk, rows_of(wk_own)) + dot_nt(dv, rows_of(wv_own))
    theirs = dot_nt(dk, rows_of(wk_other)) + dot_nt(dv, rows_of(wv_other))
    out_ref[...] = to_place(ordered(core_ref[0], mine, theirs))


def cross_grad_kernel(half, core_ref, a2_ref, enc_ref, b2_ref, *rest):
    other = rest[0] if len(rest) == 2 else None
    out_ref = rest[-1]
    core = core_ref[0]
    m = pl.program_id(0)

    def emit(at, a, g):
        @pl.when(m == at)
        def _():
            put_rows(out_ref, dot_tn(a(), g()), other)

    emit(0, lambda: a2_ref[half], lambda: joined(b2_ref, 0, BLOCK))
    emit(1, lambda: halves(core, enc_ref[...])[half], lambda: joined(b2_ref, BLOCK, 128))
    emit(2, lambda: halves(core, enc_ref[...])[half], lambda: joined(b2_ref, BLOCK + 128, 128))


def self_grad_kernel(half, core_ref, a_ref, d_ref, o1_ref, e1_ref, *rest):
    other = rest[0] if len(rest) == 2 else None
    out_ref = rest[-1]
    n = 3 * LANES
    a = a_ref[...].reshape(GROUPS * BLOCK, a_ref.shape[2])
    g = dot_tn(a, d_ref[...].reshape(GROUPS * BLOCK, n))
    go = dot_tn(halves(core_ref[0], joined(o1_ref))[half], e1_ref[...])
    if other is not None:
        g = g + other[:, :n].astype(F32)
        go = go + other[:, n:].astype(F32)
    out_ref[:, :n] = g.astype(BF)
    out_ref[:, n:n + D] = go.astype(BF)


def small_kernel(core_ref, small_ref, recv_ref, big_ref, out_ref):
    out_ref[...] = (small_ref[...] + recv_ref[...].astype(F32)).astype(BF)


def self_back_kernel(core_ref, d_ref, own_ref, other_ref, x_ref, g1_ref, vec_ref,
                     out_ref, small_ref, sum_ref, da_scr):
    g = pl.program_id(0)

    @pl.when(g == 0)
    def _():
        da_scr[...] = jnp.zeros_like(da_scr)

    d = joined(d_ref)
    sum_ref[0] = column_sum(d.astype(F32))
    da_scr[0] += dot_nt(d, rows_of(own_ref))
    da_scr[1] += dot_nt(d, rows_of(other_ref))

    @pl.when(g == pl.num_programs(0) - 1)
    def _():
        da1 = ordered(core_ref[0], da_scr[0], da_scr[1])
        _, n1, r1 = norm_forward(x_ref[...].astype(F32), vec_ref[0:1], vec_ref[4:5])
        back, dgain, dshift = norm_backward(da1, n1, r1, vec_ref[0:1])
        out_ref[...] = to_place(g1_ref[...] + back)
        small_ref[0:1] = dgain
        small_ref[1:2] = dshift


def whole(shape):
    return pl.BlockSpec(shape, lambda *a: (0,) * len(shape))


def matrix(m):
    return pl.BlockSpec((16, 1, 32, D), lambda *a: (0, m, 0, 0))


def without(kernel, first, count):
    def run(*refs):
        return kernel(*refs[:first], *refs[first + count:])

    return run


def call(kernel, grid, in_specs, out_specs, out_shape, scratch, flops, size, after=()):
    def start(*args):
        return ordered_call(
            kernel, grid, in_specs, out_specs, out_shape, scratch, flops, size, args, after
        )

    return start


def ordered_call(
    kernel, grid, in_specs, out_specs, out_shape, scratch, flops, size, args, after
):
    return pl.pallas_call(
        without(kernel, len(args), len(after)),
        grid_spec=pltpu.PrefetchScalarGridSpec(
            num_scalar_prefetch=1,
            grid=grid,
            in_specs=list(in_specs) + [pl.BlockSpec(memory_space=pl.ANY)] * len(after),
            out_specs=out_specs,
            scratch_shapes=scratch,
        ),
        out_shape=out_shape,
        compiler_params=params(),
        cost_estimate=cost(flops, size),
    )(*args, *after)


def shape(dims, dtype=BF):
    return jax.ShapeDtypeStruct(dims, dtype)


def by_core(x):
    lead = x.shape[:-1]
    return x.reshape(*lead, 8, 2, HALF).swapaxes(-3, -2).reshape(*lead, D)


def by_place(x):
    lead = x.shape[:-1]
    return x.reshape(*lead, 2, 8, HALF).swapaxes(-3, -2).reshape(*lead, D)


def swap(x):
    return lax.ppermute(x, "c", [(0, 1), (1, 0)])


def local(
    tokens,
    encoded,
    unit_ids,
    text_ids,
    cotangent,
    attn_in,
    attn_out,
    w_up,
    w_down,
    norm_gains,
    shifts,
    biases,
    up_bias,
):
    core = lax.axis_index("c")
    first_core = core == 0
    core_arg = core.astype(jnp.int32).reshape(1)
    rows = tokens.shape[1]
    text_rows = encoded.shape[1]

    def mine(x):
        return lax.dynamic_slice_in_dim(x, core * (x.shape[0] // 2), x.shape[0] // 2, 0)

    def theirs(x):
        return lax.dynamic_slice_in_dim(x, (1 - core) * (x.shape[0] // 2), x.shape[0] // 2, 0)

    in_low = by_core(attn_in.astype(BF))
    out_low = by_core(attn_out.astype(BF))
    vectors = jnp.concatenate([norm_gains, shifts, biases], axis=0).astype(BF)
    tile = jnp.concatenate(
        [
            vectors.T,
            up_bias.astype(BF).reshape(8, 4),
            jnp.zeros((8, 13), BF),
            unit_ids.reshape(8, 32).astype(BF),
            text_ids.reshape(8, 16).astype(BF),
            jnp.zeros((8, 48), BF),
        ],
        axis=1,
    )
    up_low = w_up.astype(BF).reshape(8, 2, 4, 2, 2, 4, 32).transpose(0, 3, 5, 1, 4, 2, 6)
    up_low = up_low.reshape(8, 4, D).transpose(1, 0, 2).reshape(32, D)
    down_low = by_core(w_down.astype(BF))
    attn_low = jnp.concatenate([in_low[3:6], out_low], axis=0).reshape(40, D)
    self_low = jnp.concatenate(
        [in_low[0:3].reshape(24, D), jnp.pad(tile, ((0, 0), (0, D - LANES)))], axis=0
    )
    z_at = lax.axis_index("z")

    def over_z(pack):
        out = jnp.zeros((4,) + pack.shape, BF)
        for k in range(4):
            steps = [(i, (i + k) % 4) for i in range(4)]
            part = pack if k == 0 else lax.ppermute(pack, "z", steps)
            out = lax.dynamic_update_slice(out, part[None], (lax.rem(z_at + 4 - k, 4), 0, 0))
        return out

    self_z = over_z(self_low).reshape(4, 4, 8, D).transpose(1, 0, 2, 3).reshape(1, 4, 32, D)
    z_pack = jnp.concatenate([up_low, down_low, attn_low], axis=0)
    (z_pack, self_z) = lax.optimization_barrier((z_pack, self_z))
    z_all = over_z(z_pack)
    attn_z = z_all[:, 64:104].reshape(4, 5, 8, D).transpose(1, 0, 2, 3).reshape(1, 5, 32, D)
    up_z = z_all[:, :32].reshape(4, 4, 8, D).transpose(1, 0, 2, 3).reshape(4, 32, D)
    ffn_z = jnp.concatenate([up_z, z_all[:, 32:64]], axis=0)[None]

    def over_plane(x):
        n = x.shape[1]
        y = lax.all_gather(x.reshape(n * 32, D), PLANE, axis=0, tiled=True)
        return y.reshape(16, n, 32, D)

    self_own = over_plane(self_z)
    self_other = swap(self_own)
    attn_own = over_plane(attn_z)
    ffn_own = over_plane(ffn_z)

    x = by_core(tokens[0])
    enc = by_core(encoded[0])
    cot = by_core(cotangent[0])

    tile_own, tile_other = self_own[:, 3, :, :LANES], self_other[:, 3, :, :LANES]

    def up_part(t):
        return t[:, :, 15:19].reshape(16, 4, 32).transpose(1, 0, 2).reshape(1, 2048)

    up_own, up_other = up_part(tile_own), up_part(tile_other)
    up_vec = jnp.concatenate(
        [jnp.where(first_core, up_own, up_other), jnp.where(first_core, up_other, up_own)], axis=1
    ).astype(F32)
    at = (lax.axis_index("yh"), 0, lax.axis_index("x"), 0, 0, 0)
    seq_tile = lax.dynamic_slice(
        tile_own.reshape(2, 2, 4, 4, 8, LANES), at, (1, 2, 1, 4, 8, LANES)
    )
    seq_tile = seq_tile.reshape(8, 8, LANES).astype(F32).astype(jnp.int32)
    units = seq_tile[:, :, 32:64].reshape(-1)
    texts = seq_tile[:, :, 64:80].reshape(-1)
    self_plan = key_plan(units, units, True)
    cross_plan = key_plan(units, texts, False)

    qkv, _, vec, a1 = call(
        qkv_kernel,
        (3,),
        [
            whole((rows, D)),
            pl.BlockSpec((16, 1, 32, LANES), lambda m, c: (0, 3, 0, 0)),
            pl.BlockSpec((16, 1, 32, LANES), lambda m, c: (0, 3, 0, 0)),
            pl.BlockSpec((16, 1, 32, D), lambda m, c: (0, m, 0, 0)),
            pl.BlockSpec((16, 1, 32, D), lambda m, c: (0, m, 0, 0)),
        ],
        [
            pl.BlockSpec((GROUPS, rows, LANES), lambda m, c: (0, 0, m)),
            whole((2, rows, 512)),
            whole((16, D)),
            whole((rows, D)),
        ],
        [
            shape((GROUPS, rows, 384)),
            shape((2, rows, 512)),
            shape((16, D), F32),
            shape((rows, D)),
        ],
        [],
        1.6e9,
        8e6,
    )(core_arg, x, self_own, self_other, self_own, self_other)
    qkv = lax.all_to_all(qkv, SEQ, 0, 0, tiled=True)
    self_keys = ((GROUPS, rows, LANES), (0, 0, 1), (0, 0, 2))
    o1_heads, lse1 = attend_fwd(self_plan, qkv, qkv, self_keys)
    (attn_own, a1, _) = lax.optimization_barrier((attn_own, a1, o1_heads))
    attn_other = swap(attn_own)
    a1_all = lax.all_gather(a1, SEQ, axis=0, tiled=False)
    o1 = lax.all_to_all(o1_heads, SEQ, 0, 0, tiled=True)

    kv2 = call(
        text_kernel,
        (2,),
        [
            whole((text_rows, D)),
            whole((16, D)),
            pl.BlockSpec((16, 1, 32, D), lambda m, c: (0, 1 + m, 0, 0)),
            pl.BlockSpec((16, 1, 32, D), lambda m, c: (0, 1 + m, 0, 0)),
        ],
        pl.BlockSpec((GROUPS, text_rows, LANES), lambda m, c: (0, m, 0)),
        shape((GROUPS, 2 * text_rows, LANES)),
        [],
        0.5e9,
        4e6,
        after=(o1_heads,),
    )(core_arg, enc, vec, attn_own, attn_other)

    x1, a2, q2 = call(
        middle_kernel,
        (1,),
        [whole((GROUPS, rows, LANES)), whole((rows, D)), whole((16, D))]
        + [matrix(3), matrix(3), matrix(0), matrix(0), whole((GROUPS, 2 * text_rows, LANES))],
        [whole((rows, D)), whole((2, rows, 512)), whole((GROUPS, 2 * rows, LANES))],
        [shape((rows, D), F32), shape((2, rows, 512)), shape((GROUPS, 2 * rows, LANES))],
        [],
        1.1e9,
        8e6,
    )(core_arg, o1, x, vec, attn_own, attn_other, attn_own, attn_other, kv2)
    q2 = lax.all_to_all(q2, SEQ, 0, 0, tiled=True)
    cross_keys = ((GROUPS, text_rows, LANES), (0, 2, 0), (0, 3, 0))
    o2_heads, lse2 = attend_fwd(cross_plan, q2, q2, cross_keys)
    o2 = lax.all_to_all(o2_heads, SEQ, 0, 0, tiled=True)
    (ffn_own, _) = lax.optimization_barrier((ffn_own, o2))
    ffn_other = swap(ffn_own)

    def block_of(s, c):
        t = lax.rem(s, 8)
        return jnp.where(t < 4, c[0], 1 - c[0]) * 4 + lax.rem(t, 4)

    def back_block(s, c):
        return block_of(jnp.maximum(s, 8), c)

    up_spec = pl.BlockSpec(
        (16, 1, 32, 512), lambda s, c: (0, block_of(s, c) // 2, 0, lax.rem(block_of(s, c), 2))
    )
    gup_spec = pl.BlockSpec(
        (16, 1, 32, 512), lambda s, c: (0, back_block(s, c) // 2, 0, lax.rem(back_block(s, c), 2))
    )
    (layer_out, g2, e2, do2, a3, e3, hidden, ep, small_f, dup_bias, gup, gdn, go) = call(
        ffn_kernel,
        (16,),
        [
            whole((GROUPS, rows, LANES)),
            whole((rows, D)),
            whole((16, D)),
            pl.BlockSpec((1, 512), lambda s, c: (0, block_of(s, c))),
            whole((rows, D)),
            matrix(4),
            matrix(4),
            up_spec,
            up_spec,
            pl.BlockSpec(
                (16, 1, 32, D), lambda s, c: (0, 4 + jnp.minimum(lax.rem(s, 8), 3), 0, 0)
            ),
            pl.BlockSpec(
                (16, 1, 32, D), lambda s, c: (0, jnp.maximum(lax.rem(s, 8), 4), 0, 0)
            ),
        ],
        [
            whole((rows, D)),
            whole((rows, D)),
            whole((rows, D)),
            whole((GROUPS, rows, LANES)),
            whole((2, rows, 512)),
            whole((rows, D)),
            pl.BlockSpec((rows, 512), lambda s, c: (0, jnp.clip(s - 8, 0, 3))),
            pl.BlockSpec((rows, 512), lambda s, c: (0, back_block(s, c))),
            whole((8, D)),
            pl.BlockSpec((1, 512), lambda s, c: (0, back_block(s, c))),
            gup_spec,
            pl.BlockSpec((16, 1, 32, D), lambda s, c: (0, jnp.maximum(s - 12, 0), 0, 0)),
            matrix(0),
        ],
        [
            shape((rows, D), F32),
            shape((rows, D), F32),
            shape((rows, D)),
            shape((GROUPS, rows, LANES)),
            shape((2, rows, 512)),
            shape((rows, D)),
            shape((rows, FF // 2)),
            shape((rows, FF)),
            shape((8, D), F32),
            shape((1, FF), F32),
            shape((16, 4, 32, D)),
            shape((16, 4, 32, D)),
            shape((16, 1, 32, D)),
        ],
        [
            pltpu.VMEM((rows, D), F32),
            pltpu.VMEM((rows, D), F32),
            pltpu.VMEM((8, rows, 512), F32),
            pltpu.VMEM((8, rows, 512), BF),
            pltpu.VMEM((2, rows, 512), F32),
            pltpu.VMEM((rows, 512), F32),
            pltpu.VMEM((512, rows), F32),
        ],
        16e9,
        50e6,
    )(core_arg, o2, x1, vec, up_vec, cot, attn_own, attn_other, ffn_own, ffn_other,
      ffn_own, ffn_other)
    do2 = lax.all_to_all(do2, SEQ, 0, 0, tiled=True)
    gup_recv, gdn_recv, go_recv = swap(gup), swap(gdn), swap(go)

    back2_heads = attend_bwd(
        cross_plan, lse2, q2, q2, o2_heads, do2, cross_keys, False, after=(a1_all,)
    )
    back2 = lax.all_to_all(back2_heads, SEQ, 0, 0, tiled=True)
    ffn_grad = call(
        ffn_grad_kernel,
        (9,),
        [
            whole((2, rows, 512)),
            pl.BlockSpec((rows, D), lambda m, c: (0, jnp.minimum(m, 3))),
            pl.BlockSpec((rows, 512), lambda m, c: (0, jnp.clip(m - 4, 0, 3))),
            whole((rows, D)),
            pl.BlockSpec((16, 1, 32, D), lambda m, c: (0, jnp.minimum(m, 3), 0, 0)),
            pl.BlockSpec((16, 1, 32, D), lambda m, c: (0, jnp.clip(m - 4, 0, 3), 0, 0)),
            whole((GROUPS, rows, LANES)),
            whole((rows, D)),
            matrix(0),
        ],
        pl.BlockSpec((16, 1, 32, D), lambda m, c: (0, m, 0, 0)),
        shape((16, 12, 32, D)),
        [],
        2.4e9,
        20e6,
        after=(back2_heads,),
    )(core_arg, a3, ep, hidden, e3, gup_recv, gdn_recv, o2, e2, go_recv)

    def cross_grads(half, recv, into, after=()):
        args = (core_arg, a2, enc, back2) + tuple(recv)
        later = after if into is None else (into,)
        first, blocks = (0, 3) if into is None else (9, 12)
        block = pl.BlockSpec((16, 1, 32, D), lambda m, c: (0, m, 0, 0))
        return pl.pallas_call(
            without(functools.partial(cross_grad_kernel, half), len(args), len(later)),
            grid_spec=pltpu.PrefetchScalarGridSpec(
                num_scalar_prefetch=1,
                grid=(3,),
                in_specs=[
                    whole((2, rows, 512)),
                    whole((text_rows, D)),
                    whole((GROUPS, rows + 2 * text_rows, LANES)),
                ]
                + [block] * len(recv)
                + [pl.BlockSpec(memory_space=pl.ANY)] * len(later),
                out_specs=pl.BlockSpec((16, 1, 32, D), lambda m, c: (0, first + m, 0, 0)),
            ),
            out_shape=shape((16, blocks, 32, D)),
            input_output_aliases={} if into is None else {len(args): 0},
            compiler_params=params(),
            cost_estimate=cost(0.6e9, 5e6),
        )(*args, *later)

    cross_theirs = cross_grads(1, [], None, (ffn_grad,))
    cross_recv = swap(cross_theirs)

    g1, e1, do1, small_c = call(
        cross_back_kernel,
        (1,),
        [whole((GROUPS, rows + 2 * text_rows, LANES)), whole((rows, D)), whole((rows, D))]
        + [whole((16, D)), matrix(0), matrix(0), matrix(3), matrix(3)],
        [whole((rows, D)), whole((rows, D)), whole((GROUPS, rows, LANES)), whole((8, D))],
        [
            shape((rows, D), F32),
            shape((rows, D)),
            shape((GROUPS, rows, LANES)),
            shape((8, D), F32),
        ],
        [],
        1.1e9,
        10e6,
        after=(ffn_grad, cross_theirs),
    )(core_arg, back2, x1, g2, vec, attn_own, attn_other, attn_own, attn_other)
    do1_rows = do1
    do1 = lax.all_to_all(do1, SEQ, 0, 0, tiled=True)
    (cross_recv, _) = lax.optimization_barrier((cross_recv, do1_rows))
    all_grads = cross_grads(0, [cross_recv], ffn_grad)
    grads = lax.psum_scatter(
        all_grads.reshape(16 * 12 * 32, D), PLANE, scatter_dimension=0, tiled=True
    ).reshape(12, 32, D)

    dqkv_heads = attend_bwd(
        self_plan, lse1, qkv, qkv, o1_heads, do1, self_keys, True, after=(all_grads,)
    )
    dqkv = lax.all_to_all(dqkv_heads, SEQ, 0, 0, tiled=True)
    width = 3 * LANES + D + LANES

    def self_grads(half, recv, n, later):
        at = (lambda m, c: (0, 0, c[0])) if half == 0 else (lambda m, c: (0, 0, 1 - c[0]))
        return call(
            functools.partial(self_grad_kernel, half),
            (1,),
            [
                pl.BlockSpec((GROUPS, rows, 512), at),
                whole((GROUPS, rows, 3 * LANES)),
                whole((GROUPS, rows, LANES)),
                whole((rows, D)),
            ]
            + [whole((512, 3 * LANES + D))] * len(recv),
            whole((512, n)),
            shape((512, n)),
            [],
            1.1e9,
            8e6,
            after=later,
        )(core_arg, a1_all, dqkv_heads, o1, e1, *recv)

    self_theirs = self_grads(1, [], 3 * LANES + D, ())
    self_recv = swap(self_theirs)
    d_enc = call(
        text_back_kernel,
        (1,),
        [whole((GROUPS, rows + 2 * text_rows, LANES))]
        + [matrix(1), matrix(1), matrix(2), matrix(2)],
        whole((text_rows, D)),
        shape((text_rows, D), F32),
        [],
        0.5e9,
        5e6,
        after=(self_theirs,),
    )(core_arg, back2, attn_own, attn_other, attn_own, attn_other)
    own = self_grads(0, [self_recv], width, (d_enc,))

    d_tokens, small_s, dsum = call(
        self_back_kernel,
        (3,),
        [
            pl.BlockSpec((GROUPS, rows, LANES), lambda m, c: (0, 0, m)),
            pl.BlockSpec((16, 1, 32, D), lambda m, c: (0, m, 0, 0)),
            pl.BlockSpec((16, 1, 32, D), lambda m, c: (0, m, 0, 0)),
            whole((rows, D)),
            whole((rows, D)),
            whole((16, D)),
        ],
        [
            whole((rows, D)),
            whole((8, D)),
            pl.BlockSpec((1, 1, D), lambda m, c: (m, 0, 0)),
        ],
        [shape((rows, D), F32), shape((8, D), F32), shape((3, 1, D), F32)],
        [pltpu.VMEM((2, rows, 512), F32)],
        1.6e9,
        9e6,
        after=(own,),
    )(core_arg, dqkv, self_own, self_other, x, g1, vec)

    small = jnp.concatenate(
        [
            small_s[0:1],
            small_c[0:1],
            small_f[3:4],
            small_f[0:1],
            small_s[1:2],
            small_c[1:2],
            small_f[4:5],
            small_f[1:2],
            dsum[0],
            dsum[2],
            small_c[2:3],
            small_c[3:4],
            small_c[4:5],
            small_f[5:6],
            small_f[2:3],
        ],
        axis=0,
    )
    up_sums = dup_bias.reshape(2, 4, 2, 2, 4, 32).transpose(0, 2, 4, 3, 1, 5).reshape(D, 4)
    small = jnp.concatenate([small.T, up_sums, jnp.zeros((D, LANES - 19), F32)], axis=1)
    small_recv = swap(theirs(small).astype(BF))
    last = pl.pallas_call(
        small_kernel,
        grid_spec=pltpu.PrefetchScalarGridSpec(
            num_scalar_prefetch=1,
            grid=(1,),
            in_specs=[whole((512, LANES)), whole((512, LANES)), pl.BlockSpec(memory_space=pl.ANY)],
            out_specs=pl.BlockSpec((512, LANES), lambda m, c: (0, 3 + D // LANES)),
        ),
        out_shape=shape((512, width)),
        input_output_aliases={3: 0},
        compiler_params=params(),
        cost_estimate=cost(1e5, 5e5),
    )(core_arg, mine(small), small_recv, own)
    last = lax.all_to_all(last.reshape(64, 8, width), CHIPS, 0, 0, tiled=True)
    z_grad = jnp.concatenate(
        [
            grads[:4].reshape(4, 4, 8, D).transpose(1, 0, 2, 3).reshape(4, 32, D),
            grads[4:8],
            grads[8:].reshape(4, 4, 8, D).transpose(1, 0, 2, 3).reshape(4, 32, D),
        ],
        axis=1,
    )
    parts = []
    for k in range(4):
        to = lax.rem(z_at + k, 4)
        part = lax.dynamic_slice_in_dim(z_grad, to, 1, 0)[0]
        if k:
            part = lax.ppermute(part, "z", [(i, (i + k) % 4) for i in range(4)])
        parts.append(part.astype(F32))
    z_grad = (parts[0] + parts[1]) + (parts[2] + parts[3])
    (last, _) = lax.optimization_barrier((last, z_grad))
    heads = jnp.sum(last[:, :, :3 * LANES].astype(F32).reshape(8, 8, 8, 3 * LANES), axis=0)
    last = jnp.sum(last[:, :, 3 * LANES:].astype(F32), axis=0)
    d_up = z_grad[:32].reshape(4, 8, D).transpose(1, 0, 2).reshape(8, 2, 4, 2, 2, 4, 32)
    d_up = d_up.transpose(0, 3, 5, 1, 4, 2, 6).reshape(8, FF)
    d_down = by_place(z_grad[32:64])
    heads = heads.reshape(GROUPS, 8, 3, LANES).transpose(2, 1, 0, 3).reshape(3, 8, D)
    attn_grad = z_grad[64:].reshape(4, 8, D)
    d_in = by_place(jnp.concatenate([heads, attn_grad[1:]], axis=0))
    d_out = by_place(jnp.stack([last[:, :D], attn_grad[0]]))
    d_vec = last[:, D:D + 15].T
    d_up_bias = last[:, D + 15:D + 19].reshape(32)
    return (
        layer_out[None],
        d_tokens[None],
        d_enc[None],
        d_in,
        d_out,
        d_up,
        d_down,
        d_vec[0:4],
        d_vec[4:8],
        d_vec[8:15],
        d_up_bias,
    )


def solution(mesh):
    fine = Mesh(mesh.devices.reshape(2, 4, 2, 2, 4), ("yh", "x", "c", "yl", "z"))
    fsdp = ("yh", "x", "c")
    every = fsdp + SEQ
    placed = (
        P(fsdp, SEQ, None),
        P(fsdp, SEQ, None),
        P(fsdp, SEQ),
        P(fsdp, SEQ),
        P(fsdp, SEQ, None),
        P(None, every, None),
        P(None, every, None),
        P(every, None),
        P(every, None),
        P(None, every),
        P(None, every),
        P(None, every),
        P(every),
    )
    return jax.shard_map(
        local,
        mesh=fine,
        in_specs=placed,
        out_specs=(
            P(fsdp, SEQ, None),
            P(fsdp, SEQ, None),
            P(fsdp, SEQ, None),
            P(None, every, None),
            P(None, every, None),
            P(every, None),
            P(every, None),
            P(None, every),
            P(None, every),
            P(None, every),
            P(every),
        ),
        check_vma=False,
    )
```

```python
import functools

import jax
import jax.numpy as jnp
from jax import lax
from jax.experimental import pallas as pl
from jax.experimental.pallas import tpu as pltpu
from jax.sharding import Mesh
from jax.sharding import PartitionSpec as P

D = 1024
FF = 4096
GROUPS = 8
LANES = 128
HALF = 64
BLOCK = 256
EPS = 1e-05
MASKED = -1e30

SEQ = ("yl", "z")
CHIPS = ("yh", "x", "yl", "z")
PLANE = ("yh", "yl", "x")
BF = jnp.bfloat16
F32 = jnp.float32


def dot(a, b):
    return jnp.dot(a, b, preferred_element_type=F32)


def dot_nt(a, b):
    return lax.dot_general(a, b, (((1,), (1,)), ((), ())), preferred_element_type=F32)


def dot_tn(a, b):
    return lax.dot_general(a, b, (((0,), (0,)), ((), ())), preferred_element_type=F32)


def stack_cols(xt):
    zero = jnp.zeros((HALF, xt.shape[1]), xt.dtype)
    return jnp.concatenate(
        [
            jnp.concatenate([xt[:HALF], zero], axis=0),
            jnp.concatenate([zero, xt[HALF:]], axis=0),
        ],
        axis=1,
    )


def stack_rows(x):
    lane = lax.broadcasted_iota(jnp.int32, x.shape, 1)
    zero = jnp.zeros_like(x)
    return jnp.concatenate(
        [jnp.where(lane < HALF, x, zero), jnp.where(lane < HALF, zero, x)], axis=0
    )


def unstack_cols(xt):
    n = xt.shape[1] // 2
    return jnp.concatenate([xt[:HALF, :n], xt[HALF:, n:]], axis=0)


def allowed_mask(j, start, length):
    pos = lax.broadcasted_iota(jnp.int32, (BLOCK, start.shape[1]), 0)
    off = pos - (start - j * BLOCK)
    return off.astype(jnp.uint32) < length.astype(jnp.uint32)


def attn_fwd_kernel(pair, lo_ref, hi_ref, start_ref, len_ref, q_ref, k_ref, v_ref, o_ref, lse_ref,
                    vt_scr, s_scr, o_scr):
    i = pl.program_id(0)
    nk = vt_scr.shape[0]
    per = BLOCK // k_ref.shape[1]

    @pl.when(i == 0)
    def _():
        for j in range(nk):
            vt_scr[j] = v_ref[j * per:(j + 1) * per].reshape(BLOCK, LANES).astype(F32).T

    q = q_ref[0] * jnp.asarray(0.125, BF)
    qst = stack_cols(q.T)
    start = jnp.concatenate([start_ref[0], start_ref[0]], axis=1)
    length = jnp.concatenate([len_ref[0], len_ref[0]], axis=1)
    lo, hi = lo_ref[i], hi_ref[i]
    width = 2 * BLOCK

    def first(j, m8):
        k = k_ref[pl.ds(j * per, per)].reshape(BLOCK, LANES)
        s = dot(k, qst)
        s = jnp.where(allowed_mask(j, start, length), s, MASKED)
        s_scr[pl.ds(pl.multiple_of(j * BLOCK, BLOCK), BLOCK)] = s
        return jnp.maximum(m8, jnp.max(s.reshape(BLOCK // 8, 8, width), axis=0))

    def first_step(j, m8):
        return first(2 * j + 1, first(2 * j, m8)) if pair else first(j, m8)

    if pair:
        lo, hi = lo // 2, (hi + 1) // 2
    m8 = lax.fori_loop(lo, hi, first_step, jnp.full((8, width), MASKED, F32))
    m = jnp.max(m8, axis=0, keepdims=True)
    o_scr[...] = jnp.zeros_like(o_scr)

    def second(j):
        p = jnp.exp(s_scr[pl.ds(pl.multiple_of(j * BLOCK, BLOCK), BLOCK)] - m)
        o = dot(vt_scr[j].astype(BF), p.astype(BF))
        return o, jnp.sum(p.reshape(BLOCK // 8, 8, width), axis=0)

    def second_step(j, l8):
        o, l = second(2 * j if pair else j)
        if pair:
            ob, lb = second(2 * j + 1)
            o, l = o + ob, l + lb
        o_scr[...] += o
        return l8 + l

    l8 = lax.fori_loop(lo, hi, second_step, jnp.zeros((8, width), F32))
    l = jnp.sum(l8, axis=0, keepdims=True)
    lse_ref[0] = m + jnp.log(l)
    ot = unstack_cols(o_scr[...] * (1.0 / l))
    o_ref[0] = ot.T.astype(BF)


def attn_bwd_kernel(wide, lo_ref, hi_ref, start_ref, len_ref, lse_ref, q_ref, k_ref, v_ref, o_ref,
                    do_ref, out_ref, kt_scr, dq_scr, dk_scr, dv_scr):
    i = pl.program_id(0)
    nk = kt_scr.shape[0]
    kb = k_ref.shape[1]
    per = BLOCK // kb

    @pl.when(i == 0)
    def _():
        for j in range(nk):
            kt_scr[j] = k_ref[j * per:(j + 1) * per].reshape(BLOCK, LANES).astype(F32).T
        dk_scr[...] = jnp.zeros_like(dk_scr)
        dv_scr[...] = jnp.zeros_like(dv_scr)

    q = q_ref[0] * jnp.asarray(0.125, BF)
    do = do_ref[0]
    qs, qst = stack_rows(q), stack_cols(q.T)
    dot_t = do.T
    dos, dost = stack_rows(do), stack_cols(dot_t)
    prod = dot_t.astype(F32) * o_ref[0].T.astype(F32)
    delta = jnp.concatenate(
        [
            jnp.sum(prod[:HALF], axis=0, keepdims=True),
            jnp.sum(prod[HALF:], axis=0, keepdims=True),
        ],
        axis=1,
    )
    lse = lse_ref[0]
    start = jnp.concatenate([start_ref[0], start_ref[0]], axis=1)
    length = jnp.concatenate([len_ref[0], len_ref[0]], axis=1)
    dq_scr[...] = jnp.zeros_like(dq_scr)

    def body(j, carry):
        k = k_ref[pl.ds(j * per, per)].reshape(BLOCK, LANES)
        v = v_ref[pl.ds(j * per, per)].reshape(BLOCK, LANES)
        s = jnp.where(allowed_mask(j, start, length), dot(k, qst), MASKED)
        p = jnp.exp(s - lse)
        ds = (p * (dot(v, dost) - delta)).astype(BF)
        rows = pl.ds(pl.multiple_of(j * BLOCK, BLOCK), BLOCK)
        dv_scr[rows] += dot(p.astype(BF), dos)
        dk_scr[rows] += dot(ds, qs)
        dq_scr[...] += dot(kt_scr[j].astype(BF), ds)
        return carry

    lax.fori_loop(lo_ref[i], hi_ref[i], body, 0)
    dq = (unstack_cols(dq_scr[...]) * 0.125).T.astype(BF)
    if wide:
        out_ref[i, :, :LANES] = dq
    else:
        out_ref[i, :BLOCK] = dq

    @pl.when(i == pl.num_programs(0) - 1)
    def _():
        n = GROUPS
        dk = dk_scr[...].astype(BF).reshape(n, kb, LANES)
        dv = dv_scr[...].astype(BF).reshape(n, kb, LANES)
        if wide:
            out_ref[:, :, LANES:2 * LANES] = dk
            out_ref[:, :, 2 * LANES:] = dv
        else:
            out_ref[:, BLOCK:BLOCK + kb] = dk
            out_ref[:, BLOCK + kb:] = dv


def row_spec(n):
    return pl.BlockSpec((1, 1, n), lambda i, lo, hi: (i, 0, 0))


def block_rows():
    return pl.BlockSpec((1, BLOCK, LANES), lambda i, lo, hi: (i, 0, 0))


def key_specs(kshape, kblock, vblock):
    return [
        pl.BlockSpec(kshape, lambda i, lo, hi: kblock),
        pl.BlockSpec(kshape, lambda i, lo, hi: vblock),
    ]


def attend_fwd(plan, q, kv, keys_at, pair, after=()):
    lo, hi, start, length = plan
    nq = lo.shape[0]
    keys = keys_at[0][0] * keys_at[0][1]
    return pl.pallas_call(
        without(functools.partial(attn_fwd_kernel, pair), 7, len(after)),
        grid_spec=pltpu.PrefetchScalarGridSpec(
            num_scalar_prefetch=2,
            grid=(nq,),
            in_specs=[row_spec(BLOCK), row_spec(BLOCK), block_rows()]
            + key_specs(*keys_at)
            + [pl.BlockSpec(memory_space=pl.ANY)] * len(after),
            out_specs=[block_rows(), row_spec(2 * BLOCK)],
            scratch_shapes=[
                pltpu.VMEM((keys // BLOCK, LANES, BLOCK), F32),
                pltpu.VMEM((keys, 2 * BLOCK), F32),
                pltpu.VMEM((LANES, 2 * BLOCK), F32),
            ],
        ),
        out_shape=[
            jax.ShapeDtypeStruct((nq, BLOCK, LANES), BF),
            jax.ShapeDtypeStruct((nq, 1, 2 * BLOCK), F32),
        ],
        compiler_params=params(),
        cost_estimate=cost(8e9, 4e6),
    )(lo, hi, start, length, q, kv, kv, *after)


def attend_bwd(plan, lse, q, kv, out, grad, keys_at, wide, after=()):
    lo, hi, start, length = plan
    nq = lo.shape[0]
    keys = keys_at[0][0] * keys_at[0][1]
    shape = (nq, BLOCK, 3 * LANES) if wide else (nq, BLOCK + 2 * keys_at[0][1], LANES)
    return pl.pallas_call(
        without(functools.partial(attn_bwd_kernel, wide), 10, len(after)),
        grid_spec=pltpu.PrefetchScalarGridSpec(
            num_scalar_prefetch=2,
            grid=(nq,),
            in_specs=[row_spec(BLOCK), row_spec(BLOCK), row_spec(2 * BLOCK), block_rows()]
            + key_specs(*keys_at)
            + [block_rows(), block_rows()]
            + [pl.BlockSpec(memory_space=pl.ANY)] * len(after),
            out_specs=pl.BlockSpec(shape, lambda i, lo, hi: (0, 0, 0)),
            scratch_shapes=[
                pltpu.VMEM((keys // BLOCK, LANES, BLOCK), F32),
                pltpu.VMEM((LANES, 2 * BLOCK), F32),
                pltpu.VMEM((keys, LANES), F32),
                pltpu.VMEM((keys, LANES), F32),
            ],
        ),
        out_shape=jax.ShapeDtypeStruct(shape, BF),
        compiler_params=params(),
        cost_estimate=cost(8e9, 6e6),
    )(lo, hi, start, length, lse, q, kv, kv, out, grad, *after)


def key_plan(query_ids, key_ids, causal):
    start = jnp.sum((key_ids[None, :] < query_ids[:, None]).astype(jnp.int32), axis=1)
    if causal:
        end = jnp.arange(query_ids.shape[0], dtype=jnp.int32) + 1
    else:
        end = jnp.sum((key_ids[None, :] <= query_ids[:, None]).astype(jnp.int32), axis=1)
    start = start.reshape(-1, 1, BLOCK)
    end = end.reshape(-1, 1, BLOCK)
    lo = jnp.min(start, axis=(1, 2)) // BLOCK
    hi = (jnp.max(end, axis=(1, 2)) + BLOCK - 1) // BLOCK
    return lo, hi, start, end - start


def params():
    return pltpu.CompilerParams(vmem_limit_bytes=58 * 2**20)


def cost(flops, size):
    return pl.CostEstimate(flops=int(flops), bytes_accessed=int(size), transcendentals=0)


def norm_forward(values, gain, shift):
    centered = values - jnp.mean(values, axis=-1, keepdims=True)
    inverse = lax.rsqrt(jnp.mean(centered * centered, axis=-1, keepdims=True) + EPS)
    normed = centered * inverse
    return normed * gain + shift, normed, inverse


def column_sum(x):
    return jnp.sum(x, axis=0, keepdims=True)


def norm_backward(upstream, normed, inverse, gain):
    scaled = upstream * gain
    inner = (
        scaled
        - jnp.mean(scaled, axis=-1, keepdims=True)
        - normed * jnp.mean(scaled * normed, axis=-1, keepdims=True)
    )
    return inverse * inner, column_sum(upstream * normed), column_sum(upstream)


PLACES = tuple(yh * 8 + yl * 4 + x for yh in range(2) for x in range(4) for yl in range(2))


def rows_of(ref):
    return jnp.concatenate([ref[p, 0] for p in PLACES], axis=0)


def plane_rows(ref):
    return ref[:, 0].reshape(512, ref.shape[3])


def put_rows(ref, value, other=None):
    for i, p in enumerate(PLACES):
        piece = value[i * 32:(i + 1) * 32]
        if other is not None:
            piece = piece + other[p, 0].astype(F32)
        ref[p, 0] = piece.astype(ref.dtype)


def halves(core, x):
    n = x.shape[1] // 2
    a, b = x[:, :n], x[:, n:]
    first = core == 0
    return jnp.where(first, a, b), jnp.where(first, b, a)


def ordered(core, mine, theirs):
    first = core == 0
    return jnp.concatenate(
        [jnp.where(first, mine, theirs), jnp.where(first, theirs, mine)], axis=1
    )


def to_place(x):
    pieces = [x[:, c * 512 + i * HALF:c * 512 + (i + 1) * HALF] for i in range(8) for c in range(2)]
    return jnp.concatenate(pieces, axis=1)


def joined(ref, first=0, count=None):
    count = ref.shape[1] if count is None else count
    return jnp.concatenate([ref[g, first:first + count] for g in range(GROUPS)], axis=1)


def put_groups(ref, value):
    for g in range(GROUPS):
        ref[g] = value[:, g * LANES:(g + 1) * LANES].astype(ref.dtype)


def qkv_kernel(core_ref, x_ref, own_tile_ref, other_tile_ref, own_ref, other_ref,
               qkv_ref, a1_ref, vec_ref, rows_ref):
    m = pl.program_id(0)
    core = core_ref[0]

    @pl.when(m == 0)
    def _():
        own = rows_of(own_tile_ref).astype(F32).T[:16]
        other = rows_of(other_tile_ref).astype(F32).T[:16]
        vec = ordered(core, own, other)
        vec_ref[...] = vec
        a, _, _ = norm_forward(x_ref[...].astype(F32), vec[0:1], vec[4:5])
        rows_ref[...] = a.astype(BF)
        mine, theirs = halves(core, a)
        a1_ref[0] = mine.astype(BF)
        a1_ref[1] = theirs.astype(BF)

    y = dot(a1_ref[0], rows_of(own_ref)) + dot(a1_ref[1], rows_of(other_ref))
    bias = vec_ref[8:9] * (m == 0).astype(F32) + vec_ref[9:10] * (m == 2).astype(F32)
    put_groups(qkv_ref, y + bias)


def text_kernel(core_ref, enc_ref, vec_ref, own_ref, other_ref, out_ref):
    m = pl.program_id(0)
    mine, theirs = halves(core_ref[0], enc_ref[...])
    y = dot(mine, rows_of(own_ref)) + dot(theirs, rows_of(other_ref))
    put_groups(out_ref, y + vec_ref[12:13] * m.astype(F32))


def middle_kernel(core_ref, o1_ref, x_ref, vec_ref, wo_own, wo_other, wq_own, wq_other, kv_ref,
                  x1_ref, a2_ref, q2_ref):
    core = core_ref[0]
    mine, theirs = halves(core, joined(o1_ref))
    x1 = (
        x_ref[...].astype(F32)
        + dot(mine, rows_of(wo_own))
        + dot(theirs, rows_of(wo_other))
        + vec_ref[10:11]
    )
    x1_ref[...] = x1
    a, _, _ = norm_forward(x1, vec_ref[1:2], vec_ref[5:6])
    mine, theirs = halves(core, a)
    mine, theirs = mine.astype(BF), theirs.astype(BF)
    a2_ref[0] = mine
    a2_ref[1] = theirs
    q2 = dot(mine, rows_of(wq_own)) + dot(theirs, rows_of(wq_other)) + vec_ref[11:12]
    for g in range(GROUPS):
        q2_ref[g, :BLOCK] = q2[:, g * LANES:(g + 1) * LANES].astype(BF)
        q2_ref[g, BLOCK:] = kv_ref[g]


def ffn_kernel(core_ref, o2_ref, x1_ref, vec_ref, upb_ref, cot_ref, wo_own, wo_other,
               up_own, up_other, dn_own, dn_other,
               out_ref, g2_ref, e2_ref, do2_ref, a3_ref, e3_ref, hid_ref, ep_ref, small_ref,
               dupb_ref, gup_ref, gdn_ref, go_ref,
               x2_scr, acc_scr, slope_scr, hid_scr, da_scr, dh_scr, a3t_scr):
    s = pl.program_id(0)
    t = lax.rem(s, 8)
    core = core_ref[0]

    @pl.when(s == 0)
    def _():
        mine, theirs = halves(core, joined(o2_ref))
        x2 = (
            x1_ref[...]
            + dot(mine, rows_of(wo_own))
            + dot(theirs, rows_of(wo_other))
            + vec_ref[13:14]
        )
        x2_scr[...] = x2
        a, _, _ = norm_forward(x2, vec_ref[2:3], vec_ref[6:7])
        mine, theirs = halves(core, a)
        a3_ref[0] = mine.astype(BF)
        a3_ref[1] = theirs.astype(BF)
        acc_scr[...] = jnp.zeros_like(acc_scr)

    @pl.when(s < 8)
    def _():
        pre = dot(a3_ref[0], rows_of(up_own)) + dot(a3_ref[1], rows_of(up_other)) + upb_ref[...]
        sig = jax.nn.sigmoid(pre)
        slope_scr[t] = sig * (1.0 + pre * (1.0 - sig))
        hidden = (pre * sig).astype(BF)
        hid_scr[t] = hidden

        @pl.when(t < 4)
        def _():
            acc_scr[...] += dot(hidden, plane_rows(dn_own))

        @pl.when(t >= 4)
        def _():
            acc_scr[...] += dot(hidden, plane_rows(dn_other))

    @pl.when(s == 7)
    def _():
        x3 = x2_scr[...] + acc_scr[...] + vec_ref[14:15]
        y, n4, r4 = norm_forward(x3, vec_ref[3:4], vec_ref[7:8])
        out_ref[...] = to_place(y)
        g3, dgain, dshift = norm_backward(cot_ref[...].astype(F32), n4, r4, vec_ref[3:4])
        acc_scr[...] = g3
        e3_ref[...] = g3.astype(BF)
        small_ref[0:1] = dgain
        small_ref[1:2] = dshift
        small_ref[2:3] = column_sum(g3)
        da_scr[...] = jnp.zeros_like(da_scr)
        a3t_scr[...] = a3_ref[1].astype(F32).T

    @pl.when(s >= 8)
    def _():
        e3 = e3_ref[...]

        @pl.when(t < 4)
        def _():
            dh_scr[...] = dot_nt(e3, plane_rows(dn_own))
            hid_ref[...] = hid_scr[t]

        @pl.when(t >= 4)
        def _():
            dh_scr[...] = dot_nt(e3, plane_rows(dn_other))
            gdn_ref[:, 0] = dot_tn(hid_scr[t], e3).astype(BF).reshape(16, 32, D)

        dpre = dh_scr[...] * slope_scr[t]
        ep = dpre.astype(BF)
        ep_ref[...] = ep
        dupb_ref[...] = column_sum(dpre)
        put_rows(gup_ref, dot(a3t_scr[...].astype(BF), ep))
        da_scr[0] += dot_nt(ep, rows_of(up_own))
        da_scr[1] += dot_nt(ep, rows_of(up_other))

    @pl.when(s == 15)
    def _():
        da3 = ordered(core, da_scr[0], da_scr[1])
        _, n3, r3 = norm_forward(x2_scr[...], vec_ref[2:3], vec_ref[6:7])
        back, dgain, dshift = norm_backward(da3, n3, r3, vec_ref[2:3])
        g2 = acc_scr[...] + back
        g2_ref[...] = g2
        small_ref[3:4] = dgain
        small_ref[4:5] = dshift
        small_ref[5:6] = column_sum(g2)
        e2 = g2.astype(BF)
        e2_ref[...] = e2
        put_groups(
            do2_ref, ordered(core, dot_nt(e2, rows_of(wo_own)), dot_nt(e2, rows_of(wo_other)))
        )
        put_rows(go_ref, dot_tn(halves(core, joined(o2_ref))[1], e2))


def ffn_grad_kernel(core_ref, a3_ref, ep_ref, hid_ref, e3_ref, up_ref, dn_ref, o2_ref, e2_ref,
                    go_ref, out_ref):
    m = pl.program_id(0)

    @pl.when(m < 4)
    def _():
        put_rows(out_ref, dot_tn(a3_ref[0], ep_ref[...]), up_ref)

    @pl.when(m == 8)
    def _():
        o2 = halves(core_ref[0], joined(o2_ref))[0]
        put_rows(out_ref, dot_tn(o2, e2_ref[...]), go_ref)

    @pl.when((m >= 4) & (m < 8))
    def _():
        g = dot_tn(hid_ref[...], e3_ref[...]).reshape(16, 32, D)
        out_ref[:, 0] = (g + dn_ref[:, 0].astype(F32)).astype(BF)


def cross_back_kernel(core_ref, b2_ref, x1_ref, g2_ref, vec_ref, wq_own, wq_other,
                      wo_own, wo_other, g1_ref, e1_ref, do1_ref, small_ref):
    core = core_ref[0]
    dq = joined(b2_ref, 0, BLOCK)
    da2 = ordered(core, dot_nt(dq, rows_of(wq_own)), dot_nt(dq, rows_of(wq_other)))
    _, n2, r2 = norm_forward(x1_ref[...], vec_ref[1:2], vec_ref[5:6])
    back, dgain, dshift = norm_backward(da2, n2, r2, vec_ref[1:2])
    g1 = g2_ref[...] + back
    g1_ref[...] = g1
    e1 = g1.astype(BF)
    e1_ref[...] = e1
    put_groups(
        do1_ref, ordered(core, dot_nt(e1, rows_of(wo_own)), dot_nt(e1, rows_of(wo_other)))
    )
    small_ref[0:1] = dgain
    small_ref[1:2] = dshift
    small_ref[2:3] = column_sum(g1)
    small_ref[3:4] = column_sum(dq.astype(F32))
    small_ref[4:5] = column_sum(joined(b2_ref, BLOCK + 128, 128).astype(F32))


def text_back_kernel(core_ref, b2_ref, wk_own, wk_other, wv_own, wv_other, out_ref):
    dk = joined(b2_ref, BLOCK, 128)
    dv = joined(b2_ref, BLOCK + 128, 128)
    mine = dot_nt(dk, rows_of(wk_own)) + dot_nt(dv, rows_of(wv_own))
    theirs = dot_nt(dk, rows_of(wk_other)) + dot_nt(dv, rows_of(wv_other))
    out_ref[...] = to_place(ordered(core_ref[0], mine, theirs))


def cross_grad_kernel(half, core_ref, a2_ref, enc_ref, b2_ref, *rest):
    other = rest[0] if len(rest) == 2 else None
    out_ref = rest[-1]
    core = core_ref[0]
    m = pl.program_id(0)

    def emit(at, a, g):
        @pl.when(m == at)
        def _():
            put_rows(out_ref, dot_tn(a(), g()), other)

    emit(0, lambda: a2_ref[half], lambda: joined(b2_ref, 0, BLOCK))
    emit(1, lambda: halves(core, enc_ref[...])[half], lambda: joined(b2_ref, BLOCK, 128))
    emit(2, lambda: halves(core, enc_ref[...])[half], lambda: joined(b2_ref, BLOCK + 128, 128))


def self_grad_kernel(half, core_ref, a_ref, d_ref, o1_ref, e1_ref, *rest):
    other = rest[0] if len(rest) == 2 else None
    out_ref = rest[-1]
    n = 3 * LANES
    a = a_ref[...].reshape(GROUPS * BLOCK, a_ref.shape[2])
    g = dot_tn(a, d_ref[...].reshape(GROUPS * BLOCK, n))
    go = dot_tn(halves(core_ref[0], joined(o1_ref))[half], e1_ref[...])
    if other is not None:
        g = g + other[:, :n].astype(F32)
        go = go + other[:, n:].astype(F32)
    out_ref[:, :n] = g.astype(BF)
    out_ref[:, n:n + D] = go.astype(BF)


def small_kernel(core_ref, small_ref, recv_ref, big_ref, out_ref):
    out_ref[...] = (small_ref[...] + recv_ref[...].astype(F32)).astype(BF)


def self_back_kernel(core_ref, d_ref, own_ref, other_ref, x_ref, g1_ref, vec_ref,
                     out_ref, small_ref, sum_ref, da_scr):
    g = pl.program_id(0)

    @pl.when(g == 0)
    def _():
        da_scr[...] = jnp.zeros_like(da_scr)

    d = joined(d_ref)
    sum_ref[0] = column_sum(d.astype(F32))
    da_scr[0] += dot_nt(d, rows_of(own_ref))
    da_scr[1] += dot_nt(d, rows_of(other_ref))

    @pl.when(g == pl.num_programs(0) - 1)
    def _():
        da1 = ordered(core_ref[0], da_scr[0], da_scr[1])
        _, n1, r1 = norm_forward(x_ref[...].astype(F32), vec_ref[0:1], vec_ref[4:5])
        back, dgain, dshift = norm_backward(da1, n1, r1, vec_ref[0:1])
        out_ref[...] = to_place(g1_ref[...] + back)
        small_ref[0:1] = dgain
        small_ref[1:2] = dshift


def finish_kernel(p0_ref, p1_ref, p2_ref, p3_ref, last_ref,
                  in_ref, out_ref, up_ref, down_ref, gain_ref, shift_ref, bias_ref, upb_ref):
    f = [p[...].astype(F32) for p in (p0_ref, p1_ref, p2_ref, p3_ref)]
    z = (f[0] + f[1]) + (f[2] + f[3])
    pieces = []
    for yh in range(2):
        for x in range(4):
            for c in range(2):
                for yl in range(2):
                    for zz in range(4):
                        block = c * 4 + zz
                        row = block // 2 * 8
                        col = block % 2 * 512 + (yh * 8 + yl * 4 + x) * 32
                        pieces.append(z[row:row + 8, col:col + 32])
    up_ref[...] = jnp.concatenate(pieces, axis=1)
    down_ref[...] = to_place(z[32:64])
    out_ref[1] = to_place(z[64:72])
    for m in range(3):
        in_ref[3 + m] = to_place(z[72 + 8 * m:80 + 8 * m])
    n = 3 * LANES
    heads = []
    rest = None
    for g in range(GROUPS):
        total = last_ref[g].astype(F32)
        for i in range(1, 8):
            total = total + last_ref[i * 8 + g].astype(F32)
        heads.append(total[:, :n])
        rest = total[:, n:] if rest is None else rest + total[:, n:]
    for m in range(3):
        cols = [h[:, m * LANES:(m + 1) * LANES] for h in heads]
        in_ref[m] = to_place(jnp.concatenate(cols, axis=1))
    out_ref[0] = to_place(rest[:, :D])
    tile = rest[:, D:]
    upb_ref[...] = tile
    rows = tile.T
    gain_ref[...] = rows[0:4]
    shift_ref[...] = rows[4:8]
    bias_ref[...] = rows[8:15]


def whole(shape):
    return pl.BlockSpec(shape, lambda *a: (0,) * len(shape))


def matrix(m):
    return pl.BlockSpec((16, 1, 32, D), lambda *a: (0, m, 0, 0))


def without(kernel, first, count):
    def run(*refs):
        return kernel(*refs[:first], *refs[first + count:])

    return run


def call(kernel, grid, in_specs, out_specs, out_shape, scratch, flops, size, after=()):
    def start(*args):
        return ordered_call(
            kernel, grid, in_specs, out_specs, out_shape, scratch, flops, size, args, after
        )

    return start


def ordered_call(
    kernel, grid, in_specs, out_specs, out_shape, scratch, flops, size, args, after
):
    return pl.pallas_call(
        without(kernel, len(args), len(after)),
        grid_spec=pltpu.PrefetchScalarGridSpec(
            num_scalar_prefetch=1,
            grid=grid,
            in_specs=list(in_specs) + [pl.BlockSpec(memory_space=pl.ANY)] * len(after),
            out_specs=out_specs,
            scratch_shapes=scratch,
        ),
        out_shape=out_shape,
        compiler_params=params(),
        cost_estimate=cost(flops, size),
    )(*args, *after)


def shape(dims, dtype=BF):
    return jax.ShapeDtypeStruct(dims, dtype)


def by_core(x):
    lead = x.shape[:-1]
    return x.reshape(*lead, 8, 2, HALF).swapaxes(-3, -2).reshape(*lead, D)


def by_place(x):
    lead = x.shape[:-1]
    return x.reshape(*lead, 2, 8, HALF).swapaxes(-3, -2).reshape(*lead, D)


def swap(x):
    return lax.ppermute(x, "c", [(0, 1), (1, 0)])


def local(
    tokens,
    encoded,
    unit_ids,
    text_ids,
    cotangent,
    attn_in,
    attn_out,
    w_up,
    w_down,
    norm_gains,
    shifts,
    biases,
    up_bias,
):
    core = lax.axis_index("c")
    first_core = core == 0
    core_arg = core.astype(jnp.int32).reshape(1)
    rows = tokens.shape[1]
    text_rows = encoded.shape[1]

    def mine(x):
        return lax.dynamic_slice_in_dim(x, core * (x.shape[0] // 2), x.shape[0] // 2, 0)

    def theirs(x):
        return lax.dynamic_slice_in_dim(x, (1 - core) * (x.shape[0] // 2), x.shape[0] // 2, 0)

    in_low = by_core(attn_in.astype(BF))
    out_low = by_core(attn_out.astype(BF))
    vectors = jnp.concatenate([norm_gains, shifts, biases], axis=0).astype(BF)
    tile = jnp.concatenate(
        [
            vectors.T,
            up_bias.astype(BF).reshape(8, 4),
            jnp.zeros((8, 13), BF),
            unit_ids.reshape(8, 32).astype(BF),
            text_ids.reshape(8, 16).astype(BF),
            jnp.zeros((8, 48), BF),
        ],
        axis=1,
    )
    up_low = w_up.astype(BF).reshape(8, 2, 4, 2, 2, 4, 32).transpose(0, 3, 5, 1, 4, 2, 6)
    up_low = up_low.reshape(8, 4, D).transpose(1, 0, 2).reshape(32, D)
    down_low = by_core(w_down.astype(BF))
    attn_low = jnp.concatenate([in_low[3:6], out_low], axis=0).reshape(40, D)
    self_low = jnp.concatenate(
        [in_low[0:3].reshape(24, D), jnp.pad(tile, ((0, 0), (0, D - LANES)))], axis=0
    )
    z_at = lax.axis_index("z")

    def over_z(pack):
        out = jnp.zeros((4,) + pack.shape, BF)
        for k in range(4):
            steps = [(i, (i + k) % 4) for i in range(4)]
            part = pack if k == 0 else lax.ppermute(pack, "z", steps)
            out = lax.dynamic_update_slice(out, part[None], (lax.rem(z_at + 4 - k, 4), 0, 0))
        return out

    self_z = over_z(self_low).reshape(4, 4, 8, D).transpose(1, 0, 2, 3).reshape(1, 4, 32, D)
    z_pack = jnp.concatenate([up_low, down_low, attn_low], axis=0)
    (z_pack, self_z) = lax.optimization_barrier((z_pack, self_z))
    z_all = over_z(z_pack)
    attn_z = z_all[:, 64:104].reshape(4, 5, 8, D).transpose(1, 0, 2, 3).reshape(1, 5, 32, D)
    up_z = z_all[:, :32].reshape(4, 4, 8, D).transpose(1, 0, 2, 3).reshape(4, 32, D)
    ffn_z = jnp.concatenate([up_z, z_all[:, 32:64]], axis=0)[None]

    def over_plane(x):
        n = x.shape[1]
        y = lax.all_gather(x.reshape(n * 32, D), PLANE, axis=0, tiled=True)
        return y.reshape(16, n, 32, D)

    self_own = over_plane(self_z)
    self_other = swap(self_own)
    attn_own = over_plane(attn_z)
    ffn_own = over_plane(ffn_z)

    x = by_core(tokens[0])
    enc = by_core(encoded[0])
    cot = by_core(cotangent[0])

    tile_own, tile_other = self_own[:, 3, :, :LANES], self_other[:, 3, :, :LANES]

    def up_part(t):
        return t[:, :, 15:19].reshape(16, 4, 32).transpose(1, 0, 2).reshape(1, 2048)

    up_own, up_other = up_part(tile_own), up_part(tile_other)
    up_vec = jnp.concatenate(
        [jnp.where(first_core, up_own, up_other), jnp.where(first_core, up_other, up_own)], axis=1
    ).astype(F32)
    at = (lax.axis_index("yh"), 0, lax.axis_index("x"), 0, 0, 0)
    seq_tile = lax.dynamic_slice(
        tile_own.reshape(2, 2, 4, 4, 8, LANES), at, (1, 2, 1, 4, 8, LANES)
    )
    seq_tile = seq_tile.reshape(8, 8, LANES).astype(F32).astype(jnp.int32)
    units = seq_tile[:, :, 32:64].reshape(-1)
    texts = seq_tile[:, :, 64:80].reshape(-1)
    self_plan = key_plan(units, units, True)
    cross_plan = key_plan(units, texts, False)

    qkv, _, vec, a1 = call(
        qkv_kernel,
        (3,),
        [
            whole((rows, D)),
            pl.BlockSpec((16, 1, 32, LANES), lambda m, c: (0, 3, 0, 0)),
            pl.BlockSpec((16, 1, 32, LANES), lambda m, c: (0, 3, 0, 0)),
            pl.BlockSpec((16, 1, 32, D), lambda m, c: (0, m, 0, 0)),
            pl.BlockSpec((16, 1, 32, D), lambda m, c: (0, m, 0, 0)),
        ],
        [
            pl.BlockSpec((GROUPS, rows, LANES), lambda m, c: (0, 0, m)),
            whole((2, rows, 512)),
            whole((16, D)),
            whole((rows, D)),
        ],
        [
            shape((GROUPS, rows, 384)),
            shape((2, rows, 512)),
            shape((16, D), F32),
            shape((rows, D)),
        ],
        [],
        1.6e9,
        8e6,
    )(core_arg, x, self_own, self_other, self_own, self_other)
    qkv = lax.all_to_all(qkv, SEQ, 0, 0, tiled=True)
    self_keys = ((GROUPS, rows, LANES), (0, 0, 1), (0, 0, 2))
    o1_heads, lse1 = attend_fwd(self_plan, qkv, qkv, self_keys, True)
    (attn_own, a1, _) = lax.optimization_barrier((attn_own, a1, o1_heads))
    attn_other = swap(attn_own)
    a1_all = lax.all_gather(a1, SEQ, axis=0, tiled=False)
    o1 = lax.all_to_all(o1_heads, SEQ, 0, 0, tiled=True)

    kv2 = call(
        text_kernel,
        (2,),
        [
            whole((text_rows, D)),
            whole((16, D)),
            pl.BlockSpec((16, 1, 32, D), lambda m, c: (0, 1 + m, 0, 0)),
            pl.BlockSpec((16, 1, 32, D), lambda m, c: (0, 1 + m, 0, 0)),
        ],
        pl.BlockSpec((GROUPS, text_rows, LANES), lambda m, c: (0, m, 0)),
        shape((GROUPS, 2 * text_rows, LANES)),
        [],
        0.5e9,
        4e6,
        after=(o1_heads,),
    )(core_arg, enc, vec, attn_own, attn_other)

    x1, a2, q2 = call(
        middle_kernel,
        (1,),
        [whole((GROUPS, rows, LANES)), whole((rows, D)), whole((16, D))]
        + [matrix(3), matrix(3), matrix(0), matrix(0), whole((GROUPS, 2 * text_rows, LANES))],
        [whole((rows, D)), whole((2, rows, 512)), whole((GROUPS, 2 * rows, LANES))],
        [shape((rows, D), F32), shape((2, rows, 512)), shape((GROUPS, 2 * rows, LANES))],
        [],
        1.1e9,
        8e6,
    )(core_arg, o1, x, vec, attn_own, attn_other, attn_own, attn_other, kv2)
    q2 = lax.all_to_all(q2, SEQ, 0, 0, tiled=True)
    cross_keys = ((GROUPS, text_rows, LANES), (0, 2, 0), (0, 3, 0))
    o2_heads, lse2 = attend_fwd(cross_plan, q2, q2, cross_keys, False)
    o2 = lax.all_to_all(o2_heads, SEQ, 0, 0, tiled=True)
    (ffn_own, _) = lax.optimization_barrier((ffn_own, o2))
    ffn_other = swap(ffn_own)

    def block_of(s, c):
        t = lax.rem(s, 8)
        return jnp.where(t < 4, c[0], 1 - c[0]) * 4 + lax.rem(t, 4)

    def back_block(s, c):
        return block_of(jnp.maximum(s, 8), c)

    up_spec = pl.BlockSpec(
        (16, 1, 32, 512), lambda s, c: (0, block_of(s, c) // 2, 0, lax.rem(block_of(s, c), 2))
    )
    gup_spec = pl.BlockSpec(
        (16, 1, 32, 512), lambda s, c: (0, back_block(s, c) // 2, 0, lax.rem(back_block(s, c), 2))
    )
    (layer_out, g2, e2, do2, a3, e3, hidden, ep, small_f, dup_bias, gup, gdn, go) = call(
        ffn_kernel,
        (16,),
        [
            whole((GROUPS, rows, LANES)),
            whole((rows, D)),
            whole((16, D)),
            pl.BlockSpec((1, 512), lambda s, c: (0, block_of(s, c))),
            whole((rows, D)),
            matrix(4),
            matrix(4),
            up_spec,
            up_spec,
            pl.BlockSpec(
                (16, 1, 32, D), lambda s, c: (0, 4 + jnp.minimum(lax.rem(s, 8), 3), 0, 0)
            ),
            pl.BlockSpec(
                (16, 1, 32, D), lambda s, c: (0, jnp.maximum(lax.rem(s, 8), 4), 0, 0)
            ),
        ],
        [
            whole((rows, D)),
            whole((rows, D)),
            whole((rows, D)),
            whole((GROUPS, rows, LANES)),
            whole((2, rows, 512)),
            whole((rows, D)),
            pl.BlockSpec((rows, 512), lambda s, c: (0, jnp.clip(s - 8, 0, 3))),
            pl.BlockSpec((rows, 512), lambda s, c: (0, back_block(s, c))),
            whole((8, D)),
            pl.BlockSpec((1, 512), lambda s, c: (0, back_block(s, c))),
            gup_spec,
            pl.BlockSpec((16, 1, 32, D), lambda s, c: (0, jnp.maximum(s - 12, 0), 0, 0)),
            matrix(0),
        ],
        [
            shape((rows, D), F32),
            shape((rows, D), F32),
            shape((rows, D)),
            shape((GROUPS, rows, LANES)),
            shape((2, rows, 512)),
            shape((rows, D)),
            shape((rows, FF // 2)),
            shape((rows, FF)),
            shape((8, D), F32),
            shape((1, FF), F32),
            shape((16, 4, 32, D)),
            shape((16, 4, 32, D)),
            shape((16, 1, 32, D)),
        ],
        [
            pltpu.VMEM((rows, D), F32),
            pltpu.VMEM((rows, D), F32),
            pltpu.VMEM((8, rows, 512), F32),
            pltpu.VMEM((8, rows, 512), BF),
            pltpu.VMEM((2, rows, 512), F32),
            pltpu.VMEM((rows, 512), F32),
            pltpu.VMEM((512, rows), F32),
        ],
        16e9,
        50e6,
    )(core_arg, o2, x1, vec, up_vec, cot, attn_own, attn_other, ffn_own, ffn_other,
      ffn_own, ffn_other)
    do2 = lax.all_to_all(do2, SEQ, 0, 0, tiled=True)
    gup_recv, gdn_recv, go_recv = swap(gup), swap(gdn), swap(go)

    back2_heads = attend_bwd(
        cross_plan, lse2, q2, q2, o2_heads, do2, cross_keys, False, after=(a1_all,)
    )
    back2 = lax.all_to_all(back2_heads, SEQ, 0, 0, tiled=True)
    ffn_grad = call(
        ffn_grad_kernel,
        (9,),
        [
            whole((2, rows, 512)),
            pl.BlockSpec((rows, D), lambda m, c: (0, jnp.minimum(m, 3))),
            pl.BlockSpec((rows, 512), lambda m, c: (0, jnp.clip(m - 4, 0, 3))),
            whole((rows, D)),
            pl.BlockSpec((16, 1, 32, D), lambda m, c: (0, jnp.minimum(m, 3), 0, 0)),
            pl.BlockSpec((16, 1, 32, D), lambda m, c: (0, jnp.clip(m - 4, 0, 3), 0, 0)),
            whole((GROUPS, rows, LANES)),
            whole((rows, D)),
            matrix(0),
        ],
        pl.BlockSpec((16, 1, 32, D), lambda m, c: (0, m, 0, 0)),
        shape((16, 12, 32, D)),
        [],
        2.4e9,
        20e6,
        after=(back2_heads,),
    )(core_arg, a3, ep, hidden, e3, gup_recv, gdn_recv, o2, e2, go_recv)

    def cross_grads(half, recv, into, after=()):
        args = (core_arg, a2, enc, back2) + tuple(recv)
        later = after if into is None else (into,)
        first, blocks = (0, 3) if into is None else (9, 12)
        block = pl.BlockSpec((16, 1, 32, D), lambda m, c: (0, m, 0, 0))
        return pl.pallas_call(
            without(functools.partial(cross_grad_kernel, half), len(args), len(later)),
            grid_spec=pltpu.PrefetchScalarGridSpec(
                num_scalar_prefetch=1,
                grid=(3,),
                in_specs=[
                    whole((2, rows, 512)),
                    whole((text_rows, D)),
                    whole((GROUPS, rows + 2 * text_rows, LANES)),
                ]
                + [block] * len(recv)
                + [pl.BlockSpec(memory_space=pl.ANY)] * len(later),
                out_specs=pl.BlockSpec((16, 1, 32, D), lambda m, c: (0, first + m, 0, 0)),
            ),
            out_shape=shape((16, blocks, 32, D)),
            input_output_aliases={} if into is None else {len(args): 0},
            compiler_params=params(),
            cost_estimate=cost(0.6e9, 5e6),
        )(*args, *later)

    cross_theirs = cross_grads(1, [], None, (ffn_grad,))
    cross_recv = swap(cross_theirs)

    g1, e1, do1, small_c = call(
        cross_back_kernel,
        (1,),
        [whole((GROUPS, rows + 2 * text_rows, LANES)), whole((rows, D)), whole((rows, D))]
        + [whole((16, D)), matrix(0), matrix(0), matrix(3), matrix(3)],
        [whole((rows, D)), whole((rows, D)), whole((GROUPS, rows, LANES)), whole((8, D))],
        [
            shape((rows, D), F32),
            shape((rows, D)),
            shape((GROUPS, rows, LANES)),
            shape((8, D), F32),
        ],
        [],
        1.1e9,
        10e6,
        after=(ffn_grad, cross_theirs),
    )(core_arg, back2, x1, g2, vec, attn_own, attn_other, attn_own, attn_other)
    do1_rows = do1
    do1 = lax.all_to_all(do1, SEQ, 0, 0, tiled=True)
    (cross_recv, _) = lax.optimization_barrier((cross_recv, do1_rows))
    all_grads = cross_grads(0, [cross_recv], ffn_grad)
    grads = lax.psum_scatter(
        all_grads.reshape(16 * 12 * 32, D), PLANE, scatter_dimension=0, tiled=True
    ).reshape(12, 32, D)

    dqkv_heads = attend_bwd(
        self_plan, lse1, qkv, qkv, o1_heads, do1, self_keys, True, after=(all_grads,)
    )
    dqkv = lax.all_to_all(dqkv_heads, SEQ, 0, 0, tiled=True)
    width = 3 * LANES + D + LANES

    def self_grads(half, recv, n, later):
        at = (lambda m, c: (0, 0, c[0])) if half == 0 else (lambda m, c: (0, 0, 1 - c[0]))
        return call(
            functools.partial(self_grad_kernel, half),
            (1,),
            [
                pl.BlockSpec((GROUPS, rows, 512), at),
                whole((GROUPS, rows, 3 * LANES)),
                whole((GROUPS, rows, LANES)),
                whole((rows, D)),
            ]
            + [whole((512, 3 * LANES + D))] * len(recv),
            whole((512, n)),
            shape((512, n)),
            [],
            1.1e9,
            8e6,
            after=later,
        )(core_arg, a1_all, dqkv_heads, o1, e1, *recv)

    self_theirs = self_grads(1, [], 3 * LANES + D, ())
    self_recv = swap(self_theirs)
    d_enc = call(
        text_back_kernel,
        (1,),
        [whole((GROUPS, rows + 2 * text_rows, LANES))]
        + [matrix(1), matrix(1), matrix(2), matrix(2)],
        whole((text_rows, D)),
        shape((text_rows, D), F32),
        [],
        0.5e9,
        5e6,
        after=(self_theirs,),
    )(core_arg, back2, attn_own, attn_other, attn_own, attn_other)
    own = self_grads(0, [self_recv], width, (d_enc,))

    d_tokens, small_s, dsum = call(
        self_back_kernel,
        (3,),
        [
            pl.BlockSpec((GROUPS, rows, LANES), lambda m, c: (0, 0, m)),
            pl.BlockSpec((16, 1, 32, D), lambda m, c: (0, m, 0, 0)),
            pl.BlockSpec((16, 1, 32, D), lambda m, c: (0, m, 0, 0)),
            whole((rows, D)),
            whole((rows, D)),
            whole((16, D)),
        ],
        [
            whole((rows, D)),
            whole((8, D)),
            pl.BlockSpec((1, 1, D), lambda m, c: (m, 0, 0)),
        ],
        [shape((rows, D), F32), shape((8, D), F32), shape((3, 1, D), F32)],
        [pltpu.VMEM((2, rows, 512), F32)],
        1.6e9,
        9e6,
        after=(own,),
    )(core_arg, dqkv, self_own, self_other, x, g1, vec)

    small = jnp.concatenate(
        [
            small_s[0:1],
            small_c[0:1],
            small_f[3:4],
            small_f[0:1],
            small_s[1:2],
            small_c[1:2],
            small_f[4:5],
            small_f[1:2],
            dsum[0],
            dsum[2],
            small_c[2:3],
            small_c[3:4],
            small_c[4:5],
            small_f[5:6],
            small_f[2:3],
        ],
        axis=0,
    )
    up_sums = dup_bias.reshape(2, 4, 2, 2, 4, 32).transpose(0, 2, 4, 3, 1, 5).reshape(D, 4)
    small = jnp.concatenate([small.T, up_sums, jnp.zeros((D, LANES - 19), F32)], axis=1)
    small_recv = swap(theirs(small).astype(BF))
    last = pl.pallas_call(
        small_kernel,
        grid_spec=pltpu.PrefetchScalarGridSpec(
            num_scalar_prefetch=1,
            grid=(1,),
            in_specs=[whole((512, LANES)), whole((512, LANES)), pl.BlockSpec(memory_space=pl.ANY)],
            out_specs=pl.BlockSpec((512, LANES), lambda m, c: (0, 3 + D // LANES)),
        ),
        out_shape=shape((512, width)),
        input_output_aliases={3: 0},
        compiler_params=params(),
        cost_estimate=cost(1e5, 5e5),
    )(core_arg, mine(small), small_recv, own)
    last = lax.all_to_all(last.reshape(64, 8, width), CHIPS, 0, 0, tiled=True)
    z_grad = jnp.concatenate(
        [
            grads[:4].reshape(4, 4, 8, D).transpose(1, 0, 2, 3).reshape(4, 32, D),
            grads[4:8],
            grads[8:].reshape(4, 4, 8, D).transpose(1, 0, 2, 3).reshape(4, 32, D),
        ],
        axis=1,
    )
    parts = []
    for k in range(4):
        to = lax.rem(z_at + k, 4)
        part = lax.dynamic_slice_in_dim(z_grad, to, 1, 0)[0]
        if k:
            part = lax.ppermute(part, "z", [(i, (i + k) % 4) for i in range(4)])
        parts.append(part)
    d_in, d_out, d_up, d_down, d_gain, d_shift, d_bias, tile_sum = pl.pallas_call(
        finish_kernel,
        out_shape=[
            shape((6, 8, D), F32),
            shape((2, 8, D), F32),
            shape((8, FF), F32),
            shape((32, D), F32),
            shape((4, 8), F32),
            shape((4, 8), F32),
            shape((7, 8), F32),
            shape((8, LANES), F32),
        ],
        compiler_params=params(),
        cost_estimate=cost(1e6, 3e6),
    )(*parts, last)
    d_up_bias = tile_sum[:, 15:19].reshape(32)
    return (
        layer_out[None],
        d_tokens[None],
        d_enc[None],
        d_in,
        d_out,
        d_up,
        d_down,
        d_gain,
        d_shift,
        d_bias,
        d_up_bias,
    )


def solution(mesh):
    fine = Mesh(mesh.devices.reshape(2, 4, 2, 2, 4), ("yh", "x", "c", "yl", "z"))
    fsdp = ("yh", "x", "c")
    every = fsdp + SEQ
    placed = (
        P(fsdp, SEQ, None),
        P(fsdp, SEQ, None),
        P(fsdp, SEQ),
        P(fsdp, SEQ),
        P(fsdp, SEQ, None),
        P(None, every, None),
        P(None, every, None),
        P(every, None),
        P(every, None),
        P(None, every),
        P(None, every),
        P(None, every),
        P(every),
    )
    return jax.shard_map(
        local,
        mesh=fine,
        in_specs=placed,
        out_specs=(
            P(fsdp, SEQ, None),
            P(fsdp, SEQ, None),
            P(fsdp, SEQ, None),
            P(None, every, None),
            P(None, every, None),
            P(every, None),
            P(every, None),
            P(None, every),
            P(None, every),
            P(None, every),
            P(every),
        ),
        check_vma=False,
    )
```

```python
import functools

import jax
import jax.numpy as jnp
from jax import lax
from jax.experimental import pallas as pl
from jax.experimental.pallas import tpu as pltpu
from jax.sharding import Mesh
from jax.sharding import PartitionSpec as P

D = 1024
FF = 4096
GROUPS = 8
LANES = 128
HALF = 64
BLOCK = 256
EPS = 1e-05
MASKED = -1e30

SEQ = ("yl", "z")
CHIPS = ("yh", "x", "yl", "z")
PLANE = ("yh", "yl", "x")
BF = jnp.bfloat16
F32 = jnp.float32


def dot(a, b):
    return jnp.dot(a, b, preferred_element_type=F32)


def dot_nt(a, b):
    return lax.dot_general(a, b, (((1,), (1,)), ((), ())), preferred_element_type=F32)


def dot_tn(a, b):
    return lax.dot_general(a, b, (((0,), (0,)), ((), ())), preferred_element_type=F32)


def stack_cols(xt):
    zero = jnp.zeros((HALF, xt.shape[1]), xt.dtype)
    return jnp.concatenate(
        [
            jnp.concatenate([xt[:HALF], zero], axis=0),
            jnp.concatenate([zero, xt[HALF:]], axis=0),
        ],
        axis=1,
    )


def stack_rows(x):
    lane = lax.broadcasted_iota(jnp.int32, x.shape, 1)
    zero = jnp.zeros_like(x)
    return jnp.concatenate(
        [jnp.where(lane < HALF, x, zero), jnp.where(lane < HALF, zero, x)], axis=0
    )


def unstack_cols(xt):
    n = xt.shape[1] // 2
    return jnp.concatenate([xt[:HALF, :n], xt[HALF:, n:]], axis=0)


def allowed_mask(j, start, length):
    pos = lax.broadcasted_iota(jnp.int32, (BLOCK, start.shape[1]), 0)
    off = pos - (start - j * BLOCK)
    return off.astype(jnp.uint32) < length.astype(jnp.uint32)


def attn_fwd_kernel(pair, lo_ref, hi_ref, start_ref, len_ref, q_ref, k_ref, v_ref, o_ref, lse_ref,
                    vt_scr, s_scr, o_scr):
    i = pl.program_id(0)
    nk = vt_scr.shape[0]
    per = BLOCK // k_ref.shape[1]

    @pl.when(i == 0)
    def _():
        for j in range(nk):
            vt_scr[j] = v_ref[j * per:(j + 1) * per].reshape(BLOCK, LANES).astype(F32).T

    q = q_ref[0] * jnp.asarray(0.125, BF)
    qst = stack_cols(q.T)
    start = jnp.concatenate([start_ref[0], start_ref[0]], axis=1)
    length = jnp.concatenate([len_ref[0], len_ref[0]], axis=1)
    lo, hi = lo_ref[i], hi_ref[i]
    width = 2 * BLOCK

    def first(j, m8):
        k = k_ref[pl.ds(j * per, per)].reshape(BLOCK, LANES)
        s = dot(k, qst)
        s = jnp.where(allowed_mask(j, start, length), s, MASKED)
        s_scr[pl.ds(pl.multiple_of(j * BLOCK, BLOCK), BLOCK)] = s
        return jnp.maximum(m8, jnp.max(s.reshape(BLOCK // 8, 8, width), axis=0))

    def first_step(j, m8):
        return first(2 * j + 1, first(2 * j, m8)) if pair else first(j, m8)

    if pair:
        lo, hi = lo // 2, (hi + 1) // 2
    m8 = lax.fori_loop(lo, hi, first_step, jnp.full((8, width), MASKED, F32))
    m = jnp.max(m8, axis=0, keepdims=True)
    o_scr[...] = jnp.zeros_like(o_scr)

    def second(j):
        p = jnp.exp(s_scr[pl.ds(pl.multiple_of(j * BLOCK, BLOCK), BLOCK)] - m)
        o = dot(vt_scr[j].astype(BF), p.astype(BF))
        return o, jnp.sum(p.reshape(BLOCK // 8, 8, width), axis=0)

    def second_step(j, l8):
        o, l = second(2 * j if pair else j)
        if pair:
            ob, lb = second(2 * j + 1)
            o, l = o + ob, l + lb
        o_scr[...] += o
        return l8 + l

    l8 = lax.fori_loop(lo, hi, second_step, jnp.zeros((8, width), F32))
    l = jnp.sum(l8, axis=0, keepdims=True)
    lse_ref[0] = m + jnp.log(l)
    ot = unstack_cols(o_scr[...] * (1.0 / l))
    o_ref[0] = ot.T.astype(BF)


def attn_bwd_kernel(wide, lo_ref, hi_ref, start_ref, len_ref, lse_ref, q_ref, k_ref, v_ref, o_ref,
                    do_ref, out_ref, kt_scr, dq_scr, dk_scr, dv_scr):
    i = pl.program_id(0)
    nk = kt_scr.shape[0]
    kb = k_ref.shape[1]
    per = BLOCK // kb

    @pl.when(i == 0)
    def _():
        for j in range(nk):
            kt_scr[j] = k_ref[j * per:(j + 1) * per].reshape(BLOCK, LANES).astype(F32).T
        dk_scr[...] = jnp.zeros_like(dk_scr)
        dv_scr[...] = jnp.zeros_like(dv_scr)

    q = q_ref[0] * jnp.asarray(0.125, BF)
    do = do_ref[0]
    qs, qst = stack_rows(q), stack_cols(q.T)
    dot_t = do.T
    dos, dost = stack_rows(do), stack_cols(dot_t)
    prod = dot_t.astype(F32) * o_ref[0].T.astype(F32)
    delta = jnp.concatenate(
        [
            jnp.sum(prod[:HALF], axis=0, keepdims=True),
            jnp.sum(prod[HALF:], axis=0, keepdims=True),
        ],
        axis=1,
    )
    lse = lse_ref[0]
    start = jnp.concatenate([start_ref[0], start_ref[0]], axis=1)
    length = jnp.concatenate([len_ref[0], len_ref[0]], axis=1)
    dq_scr[...] = jnp.zeros_like(dq_scr)

    def body(j, carry):
        k = k_ref[pl.ds(j * per, per)].reshape(BLOCK, LANES)
        v = v_ref[pl.ds(j * per, per)].reshape(BLOCK, LANES)
        s = jnp.where(allowed_mask(j, start, length), dot(k, qst), MASKED)
        p = jnp.exp(s - lse)
        ds = (p * (dot(v, dost) - delta)).astype(BF)
        rows = pl.ds(pl.multiple_of(j * BLOCK, BLOCK), BLOCK)
        dv_scr[rows] += dot(p.astype(BF), dos)
        dk_scr[rows] += dot(ds, qs)
        dq_scr[...] += dot(kt_scr[j].astype(BF), ds)
        return carry

    lax.fori_loop(lo_ref[i], hi_ref[i], body, 0)
    dq = (unstack_cols(dq_scr[...]) * 0.125).T.astype(BF)
    if wide:
        out_ref[i, :, :LANES] = dq
    else:
        out_ref[i, :BLOCK] = dq

    @pl.when(i == pl.num_programs(0) - 1)
    def _():
        n = GROUPS
        dk = dk_scr[...].astype(BF).reshape(n, kb, LANES)
        dv = dv_scr[...].astype(BF).reshape(n, kb, LANES)
        if wide:
            out_ref[:, :, LANES:2 * LANES] = dk
            out_ref[:, :, 2 * LANES:] = dv
        else:
            out_ref[:, BLOCK:BLOCK + kb] = dk
            out_ref[:, BLOCK + kb:] = dv


def row_spec(n):
    return pl.BlockSpec((1, 1, n), lambda i, lo, hi: (i, 0, 0))


def block_rows():
    return pl.BlockSpec((1, BLOCK, LANES), lambda i, lo, hi: (i, 0, 0))


def key_specs(kshape, kblock, vblock):
    return [
        pl.BlockSpec(kshape, lambda i, lo, hi: kblock),
        pl.BlockSpec(kshape, lambda i, lo, hi: vblock),
    ]


def attend_fwd(plan, q, kv, keys_at, pair, after=()):
    lo, hi, start, length = plan
    nq = lo.shape[0]
    keys = keys_at[0][0] * keys_at[0][1]
    return pl.pallas_call(
        without(functools.partial(attn_fwd_kernel, pair), 7, len(after)),
        grid_spec=pltpu.PrefetchScalarGridSpec(
            num_scalar_prefetch=2,
            grid=(nq,),
            in_specs=[row_spec(BLOCK), row_spec(BLOCK), block_rows()]
            + key_specs(*keys_at)
            + [pl.BlockSpec(memory_space=pl.ANY)] * len(after),
            out_specs=[block_rows(), row_spec(2 * BLOCK)],
            scratch_shapes=[
                pltpu.VMEM((keys // BLOCK, LANES, BLOCK), F32),
                pltpu.VMEM((keys, 2 * BLOCK), F32),
                pltpu.VMEM((LANES, 2 * BLOCK), F32),
            ],
        ),
        out_shape=[
            jax.ShapeDtypeStruct((nq, BLOCK, LANES), BF),
            jax.ShapeDtypeStruct((nq, 1, 2 * BLOCK), F32),
        ],
        compiler_params=params(),
        cost_estimate=cost(8e9, 4e6),
    )(lo, hi, start, length, q, kv, kv, *after)


def attend_bwd(plan, lse, q, kv, out, grad, keys_at, wide, after=()):
    lo, hi, start, length = plan
    nq = lo.shape[0]
    keys = keys_at[0][0] * keys_at[0][1]
    shape = (nq, BLOCK, 3 * LANES) if wide else (nq, BLOCK + 2 * keys_at[0][1], LANES)
    return pl.pallas_call(
        without(functools.partial(attn_bwd_kernel, wide), 10, len(after)),
        grid_spec=pltpu.PrefetchScalarGridSpec(
            num_scalar_prefetch=2,
            grid=(nq,),
            in_specs=[row_spec(BLOCK), row_spec(BLOCK), row_spec(2 * BLOCK), block_rows()]
            + key_specs(*keys_at)
            + [block_rows(), block_rows()]
            + [pl.BlockSpec(memory_space=pl.ANY)] * len(after),
            out_specs=pl.BlockSpec(shape, lambda i, lo, hi: (0, 0, 0)),
            scratch_shapes=[
                pltpu.VMEM((keys // BLOCK, LANES, BLOCK), F32),
                pltpu.VMEM((LANES, 2 * BLOCK), F32),
                pltpu.VMEM((keys, LANES), F32),
                pltpu.VMEM((keys, LANES), F32),
            ],
        ),
        out_shape=jax.ShapeDtypeStruct(shape, BF),
        compiler_params=params(),
        cost_estimate=cost(8e9, 6e6),
    )(lo, hi, start, length, lse, q, kv, kv, out, grad, *after)


def key_plan(query_ids, key_ids, causal):
    start = jnp.sum((key_ids[None, :] < query_ids[:, None]).astype(jnp.int32), axis=1)
    if causal:
        end = jnp.arange(query_ids.shape[0], dtype=jnp.int32) + 1
    else:
        end = jnp.sum((key_ids[None, :] <= query_ids[:, None]).astype(jnp.int32), axis=1)
    start = start.reshape(-1, 1, BLOCK)
    end = end.reshape(-1, 1, BLOCK)
    lo = jnp.min(start, axis=(1, 2)) // BLOCK
    hi = (jnp.max(end, axis=(1, 2)) + BLOCK - 1) // BLOCK
    return lo, hi, start, end - start


def params():
    return pltpu.CompilerParams(vmem_limit_bytes=58 * 2**20)


def cost(flops, size):
    return pl.CostEstimate(flops=int(flops), bytes_accessed=int(size), transcendentals=0)


def norm_forward(values, gain, shift):
    centered = values - jnp.mean(values, axis=-1, keepdims=True)
    inverse = lax.rsqrt(jnp.mean(centered * centered, axis=-1, keepdims=True) + EPS)
    normed = centered * inverse
    return normed * gain + shift, normed, inverse


def column_sum(x):
    return jnp.sum(x, axis=0, keepdims=True)


def norm_backward(upstream, normed, inverse, gain):
    scaled = upstream * gain
    inner = (
        scaled
        - jnp.mean(scaled, axis=-1, keepdims=True)
        - normed * jnp.mean(scaled * normed, axis=-1, keepdims=True)
    )
    return inverse * inner, column_sum(upstream * normed), column_sum(upstream)


PLACES = tuple(yh * 8 + yl * 4 + x for yh in range(2) for x in range(4) for yl in range(2))


def rows_of(ref):
    return jnp.concatenate([ref[p, 0] for p in PLACES], axis=0)


def plane_rows(ref):
    return ref[:, 0].reshape(512, ref.shape[3])


def put_rows(ref, value, other=None):
    for i, p in enumerate(PLACES):
        piece = value[i * 32:(i + 1) * 32]
        if other is not None:
            piece = piece + other[p, 0].astype(F32)
        ref[p, 0] = piece.astype(ref.dtype)


def halves(core, x):
    n = x.shape[1] // 2
    a, b = x[:, :n], x[:, n:]
    first = core == 0
    return jnp.where(first, a, b), jnp.where(first, b, a)


def ordered(core, mine, theirs):
    first = core == 0
    return jnp.concatenate(
        [jnp.where(first, mine, theirs), jnp.where(first, theirs, mine)], axis=1
    )


def to_place(x):
    pieces = [x[:, c * 512 + i * HALF:c * 512 + (i + 1) * HALF] for i in range(8) for c in range(2)]
    return jnp.concatenate(pieces, axis=1)


def joined(ref, first=0, count=None):
    count = ref.shape[1] if count is None else count
    return jnp.concatenate([ref[g, first:first + count] for g in range(GROUPS)], axis=1)


def put_groups(ref, value):
    for g in range(GROUPS):
        ref[g] = value[:, g * LANES:(g + 1) * LANES].astype(ref.dtype)


def qkv_kernel(core_ref, x_ref, own_tile_ref, other_tile_ref, own_ref, other_ref,
               qkv_ref, a1_ref, vec_ref, rows_ref):
    m = pl.program_id(0)
    core = core_ref[0]

    @pl.when(m == 0)
    def _():
        own = rows_of(own_tile_ref).astype(F32).T[:16]
        other = rows_of(other_tile_ref).astype(F32).T[:16]
        vec = ordered(core, own, other)
        vec_ref[...] = vec
        a, _, _ = norm_forward(x_ref[...].astype(F32), vec[0:1], vec[4:5])
        rows_ref[...] = a.astype(BF)
        mine, theirs = halves(core, a)
        a1_ref[0] = mine.astype(BF)
        a1_ref[1] = theirs.astype(BF)

    y = dot(a1_ref[0], rows_of(own_ref)) + dot(a1_ref[1], rows_of(other_ref))
    bias = vec_ref[8:9] * (m == 0).astype(F32) + vec_ref[9:10] * (m == 2).astype(F32)
    put_groups(qkv_ref, y + bias)


def text_kernel(core_ref, enc_ref, vec_ref, own_ref, other_ref, out_ref):
    m = pl.program_id(0)
    mine, theirs = halves(core_ref[0], enc_ref[...])
    y = dot(mine, rows_of(own_ref)) + dot(theirs, rows_of(other_ref))
    put_groups(out_ref, y + vec_ref[12:13] * m.astype(F32))


def middle_kernel(core_ref, o1_ref, x_ref, vec_ref, wo_own, wo_other, wq_own, wq_other, kv_ref,
                  x1_ref, a2_ref, q2_ref):
    core = core_ref[0]
    mine, theirs = halves(core, joined(o1_ref))
    x1 = (
        x_ref[...].astype(F32)
        + dot(mine, rows_of(wo_own))
        + dot(theirs, rows_of(wo_other))
        + vec_ref[10:11]
    )
    x1_ref[...] = x1
    a, _, _ = norm_forward(x1, vec_ref[1:2], vec_ref[5:6])
    mine, theirs = halves(core, a)
    mine, theirs = mine.astype(BF), theirs.astype(BF)
    a2_ref[0] = mine
    a2_ref[1] = theirs
    q2 = dot(mine, rows_of(wq_own)) + dot(theirs, rows_of(wq_other)) + vec_ref[11:12]
    for g in range(GROUPS):
        q2_ref[g, :BLOCK] = q2[:, g * LANES:(g + 1) * LANES].astype(BF)
        q2_ref[g, BLOCK:] = kv_ref[g]


def ffn_kernel(core_ref, o2_ref, x1_ref, vec_ref, upb_ref, cot_ref, wo_own, wo_other,
               up_own, up_other, dn_own, dn_other,
               out_ref, g2_ref, e2_ref, do2_ref, a3_ref, e3_ref, hid_ref, ep_ref, small_ref,
               dupb_ref, gup_ref, gdn_ref, go_ref,
               x2_scr, acc_scr, slope_scr, hid_scr, da_scr, dh_scr, a3t_scr):
    s = pl.program_id(0)
    t = lax.rem(s, 8)
    core = core_ref[0]

    @pl.when(s == 0)
    def _():
        mine, theirs = halves(core, joined(o2_ref))
        x2 = (
            x1_ref[...]
            + dot(mine, rows_of(wo_own))
            + dot(theirs, rows_of(wo_other))
            + vec_ref[13:14]
        )
        x2_scr[...] = x2
        a, _, _ = norm_forward(x2, vec_ref[2:3], vec_ref[6:7])
        mine, theirs = halves(core, a)
        a3_ref[0] = mine.astype(BF)
        a3_ref[1] = theirs.astype(BF)
        acc_scr[...] = jnp.zeros_like(acc_scr)

    @pl.when(s < 8)
    def _():
        pre = dot(a3_ref[0], rows_of(up_own)) + dot(a3_ref[1], rows_of(up_other)) + upb_ref[...]
        sig = jax.nn.sigmoid(pre)
        slope_scr[t] = sig * (1.0 + pre * (1.0 - sig))
        hidden = (pre * sig).astype(BF)
        hid_scr[t] = hidden

        @pl.when(t < 4)
        def _():
            acc_scr[...] += dot(hidden, plane_rows(dn_own))

        @pl.when(t >= 4)
        def _():
            acc_scr[...] += dot(hidden, plane_rows(dn_other))

    @pl.when(s == 7)
    def _():
        x3 = x2_scr[...] + acc_scr[...] + vec_ref[14:15]
        y, n4, r4 = norm_forward(x3, vec_ref[3:4], vec_ref[7:8])
        out_ref[...] = to_place(y)
        g3, dgain, dshift = norm_backward(cot_ref[...].astype(F32), n4, r4, vec_ref[3:4])
        acc_scr[...] = g3
        e3_ref[...] = g3.astype(BF)
        small_ref[0:1] = dgain
        small_ref[1:2] = dshift
        small_ref[2:3] = column_sum(g3)
        da_scr[...] = jnp.zeros_like(da_scr)
        a3t_scr[...] = a3_ref[1].astype(F32).T

    @pl.when(s >= 8)
    def _():
        e3 = e3_ref[...]

        @pl.when(t < 4)
        def _():
            dh_scr[...] = dot_nt(e3, plane_rows(dn_own))
            hid_ref[...] = hid_scr[t]

        @pl.when(t >= 4)
        def _():
            dh_scr[...] = dot_nt(e3, plane_rows(dn_other))
            gdn_ref[:, 0] = dot_tn(hid_scr[t], e3).astype(BF).reshape(16, 32, D)

        dpre = dh_scr[...] * slope_scr[t]
        ep = dpre.astype(BF)
        ep_ref[...] = ep
        dupb_ref[...] = column_sum(dpre)
        put_rows(gup_ref, dot(a3t_scr[...].astype(BF), ep))
        da_scr[0] += dot_nt(ep, rows_of(up_own))
        da_scr[1] += dot_nt(ep, rows_of(up_other))

    @pl.when(s == 15)
    def _():
        da3 = ordered(core, da_scr[0], da_scr[1])
        _, n3, r3 = norm_forward(x2_scr[...], vec_ref[2:3], vec_ref[6:7])
        back, dgain, dshift = norm_backward(da3, n3, r3, vec_ref[2:3])
        g2 = acc_scr[...] + back
        g2_ref[...] = g2
        small_ref[3:4] = dgain
        small_ref[4:5] = dshift
        small_ref[5:6] = column_sum(g2)
        e2 = g2.astype(BF)
        e2_ref[...] = e2
        put_groups(
            do2_ref, ordered(core, dot_nt(e2, rows_of(wo_own)), dot_nt(e2, rows_of(wo_other)))
        )
        put_rows(go_ref, dot_tn(halves(core, joined(o2_ref))[1], e2))


def ffn_grad_kernel(core_ref, a3_ref, ep_ref, hid_ref, e3_ref, up_ref, dn_ref, o2_ref, e2_ref,
                    go_ref, out_ref):
    m = pl.program_id(0)

    @pl.when(m < 4)
    def _():
        put_rows(out_ref, dot_tn(a3_ref[0], ep_ref[...]), up_ref)

    @pl.when(m == 8)
    def _():
        o2 = halves(core_ref[0], joined(o2_ref))[0]
        put_rows(out_ref, dot_tn(o2, e2_ref[...]), go_ref)

    @pl.when((m >= 4) & (m < 8))
    def _():
        g = dot_tn(hid_ref[...], e3_ref[...]).reshape(16, 32, D)
        out_ref[:, 0] = (g + dn_ref[:, 0].astype(F32)).astype(BF)


def cross_back_kernel(core_ref, b2_ref, x1_ref, g2_ref, vec_ref, wq_own, wq_other,
                      wo_own, wo_other, g1_ref, e1_ref, do1_ref, small_ref):
    core = core_ref[0]
    dq = joined(b2_ref, 0, BLOCK)
    da2 = ordered(core, dot_nt(dq, rows_of(wq_own)), dot_nt(dq, rows_of(wq_other)))
    _, n2, r2 = norm_forward(x1_ref[...], vec_ref[1:2], vec_ref[5:6])
    back, dgain, dshift = norm_backward(da2, n2, r2, vec_ref[1:2])
    g1 = g2_ref[...] + back
    g1_ref[...] = g1
    e1 = g1.astype(BF)
    e1_ref[...] = e1
    put_groups(
        do1_ref, ordered(core, dot_nt(e1, rows_of(wo_own)), dot_nt(e1, rows_of(wo_other)))
    )
    small_ref[0:1] = dgain
    small_ref[1:2] = dshift
    small_ref[2:3] = column_sum(g1)
    small_ref[3:4] = column_sum(dq.astype(F32))
    small_ref[4:5] = column_sum(joined(b2_ref, BLOCK + 128, 128).astype(F32))


def text_back_kernel(core_ref, b2_ref, wk_own, wk_other, wv_own, wv_other, out_ref):
    dk = joined(b2_ref, BLOCK, 128)
    dv = joined(b2_ref, BLOCK + 128, 128)
    mine = dot_nt(dk, rows_of(wk_own)) + dot_nt(dv, rows_of(wv_own))
    theirs = dot_nt(dk, rows_of(wk_other)) + dot_nt(dv, rows_of(wv_other))
    out_ref[...] = to_place(ordered(core_ref[0], mine, theirs))


def cross_grad_kernel(half, core_ref, a2_ref, enc_ref, b2_ref, *rest):
    other = rest[0] if len(rest) == 2 else None
    out_ref = rest[-1]
    core = core_ref[0]
    m = pl.program_id(0)

    def emit(at, a, g):
        @pl.when(m == at)
        def _():
            put_rows(out_ref, dot_tn(a(), g()), other)

    emit(0, lambda: a2_ref[half], lambda: joined(b2_ref, 0, BLOCK))
    emit(1, lambda: halves(core, enc_ref[...])[half], lambda: joined(b2_ref, BLOCK, 128))
    emit(2, lambda: halves(core, enc_ref[...])[half], lambda: joined(b2_ref, BLOCK + 128, 128))


def self_grad_kernel(half, core_ref, a_ref, d_ref, o1_ref, e1_ref, *rest):
    other = rest[0] if len(rest) == 2 else None
    out_ref = rest[-1]
    n = 3 * LANES
    a = a_ref[...].reshape(GROUPS * BLOCK, a_ref.shape[2])
    g = dot_tn(a, d_ref[...].reshape(GROUPS * BLOCK, n))
    go = dot_tn(halves(core_ref[0], joined(o1_ref))[half], e1_ref[...])
    if other is not None:
        g = g + other[:, :n].astype(F32)
        go = go + other[:, n:].astype(F32)
    out_ref[:, :n] = g.astype(BF)
    out_ref[:, n:n + D] = go.astype(BF)


def small_kernel(core_ref, small_ref, recv_ref, big_ref, out_ref):
    out_ref[...] = (small_ref[...] + recv_ref[...].astype(F32)).astype(BF)


def self_back_kernel(core_ref, d_ref, own_ref, other_ref, x_ref, g1_ref, vec_ref,
                     out_ref, small_ref, sum_ref, da_scr):
    g = pl.program_id(0)

    @pl.when(g == 0)
    def _():
        da_scr[...] = jnp.zeros_like(da_scr)

    d = joined(d_ref)
    sum_ref[0] = column_sum(d.astype(F32))
    da_scr[0] += dot_nt(d, rows_of(own_ref))
    da_scr[1] += dot_nt(d, rows_of(other_ref))

    @pl.when(g == pl.num_programs(0) - 1)
    def _():
        da1 = ordered(core_ref[0], da_scr[0], da_scr[1])
        _, n1, r1 = norm_forward(x_ref[...].astype(F32), vec_ref[0:1], vec_ref[4:5])
        back, dgain, dshift = norm_backward(da1, n1, r1, vec_ref[0:1])
        out_ref[...] = to_place(g1_ref[...] + back)
        small_ref[0:1] = dgain
        small_ref[1:2] = dshift


def finish_kernel(p0_ref, p1_ref, p2_ref, p3_ref, last_ref,
                  in_ref, out_ref, up_ref, down_ref, gain_ref, shift_ref, bias_ref, upb_ref):
    f = [p[...].astype(F32) for p in (p0_ref, p1_ref, p2_ref, p3_ref)]
    z = (f[0] + f[1]) + (f[2] + f[3])
    pieces = []
    for yh in range(2):
        for x in range(4):
            for c in range(2):
                for yl in range(2):
                    for zz in range(4):
                        block = c * 4 + zz
                        row = block // 2 * 8
                        col = block % 2 * 512 + (yh * 8 + yl * 4 + x) * 32
                        pieces.append(z[row:row + 8, col:col + 32])
    up_ref[...] = jnp.concatenate(pieces, axis=1)
    down_ref[...] = to_place(z[32:64])
    out_ref[1] = to_place(z[64:72])
    for m in range(3):
        in_ref[3 + m] = to_place(z[72 + 8 * m:80 + 8 * m])
    n = 3 * LANES
    heads = []
    rest = None
    for g in range(GROUPS):
        total = last_ref[g].astype(F32)
        for i in range(1, 8):
            total = total + last_ref[i * 8 + g].astype(F32)
        heads.append(total[:, :n])
        rest = total[:, n:] if rest is None else rest + total[:, n:]
    for m in range(3):
        cols = [h[:, m * LANES:(m + 1) * LANES] for h in heads]
        in_ref[m] = to_place(jnp.concatenate(cols, axis=1))
    out_ref[0] = to_place(rest[:, :D])
    tile = rest[:, D:]
    upb_ref[...] = tile
    rows = tile.T
    gain_ref[...] = rows[0:4]
    shift_ref[...] = rows[4:8]
    bias_ref[...] = rows[8:15]


def whole(shape):
    return pl.BlockSpec(shape, lambda *a: (0,) * len(shape))


def matrix(m):
    return pl.BlockSpec((16, 1, 32, D), lambda *a: (0, m, 0, 0))


def without(kernel, first, count):
    def run(*refs):
        return kernel(*refs[:first], *refs[first + count:])

    return run


def call(kernel, grid, in_specs, out_specs, out_shape, scratch, flops, size, after=()):
    def start(*args):
        return ordered_call(
            kernel, grid, in_specs, out_specs, out_shape, scratch, flops, size, args, after
        )

    return start


def ordered_call(
    kernel, grid, in_specs, out_specs, out_shape, scratch, flops, size, args, after
):
    return pl.pallas_call(
        without(kernel, len(args), len(after)),
        grid_spec=pltpu.PrefetchScalarGridSpec(
            num_scalar_prefetch=1,
            grid=grid,
            in_specs=list(in_specs) + [pl.BlockSpec(memory_space=pl.ANY)] * len(after),
            out_specs=out_specs,
            scratch_shapes=scratch,
        ),
        out_shape=out_shape,
        compiler_params=params(),
        cost_estimate=cost(flops, size),
    )(*args, *after)


def shape(dims, dtype=BF):
    return jax.ShapeDtypeStruct(dims, dtype)


def by_core(x):
    lead = x.shape[:-1]
    return x.reshape(*lead, 8, 2, HALF).swapaxes(-3, -2).reshape(*lead, D)


def by_place(x):
    lead = x.shape[:-1]
    return x.reshape(*lead, 2, 8, HALF).swapaxes(-3, -2).reshape(*lead, D)


def swap(x):
    return lax.ppermute(x, "c", [(0, 1), (1, 0)])


def local(
    tokens,
    encoded,
    unit_ids,
    text_ids,
    cotangent,
    attn_in,
    attn_out,
    w_up,
    w_down,
    norm_gains,
    shifts,
    biases,
    up_bias,
):
    core = lax.axis_index("c")
    first_core = core == 0
    core_arg = core.astype(jnp.int32).reshape(1)
    rows = tokens.shape[1]
    text_rows = encoded.shape[1]

    def mine(x):
        return lax.dynamic_slice_in_dim(x, core * (x.shape[0] // 2), x.shape[0] // 2, 0)

    def theirs(x):
        return lax.dynamic_slice_in_dim(x, (1 - core) * (x.shape[0] // 2), x.shape[0] // 2, 0)

    in_low = by_core(attn_in.astype(BF))
    out_low = by_core(attn_out.astype(BF))
    vectors = jnp.concatenate([norm_gains, shifts, biases], axis=0).astype(BF)
    tile = jnp.concatenate(
        [
            vectors.T,
            up_bias.astype(BF).reshape(8, 4),
            jnp.zeros((8, 13), BF),
            unit_ids.reshape(8, 32).astype(BF),
            text_ids.reshape(8, 16).astype(BF),
            jnp.zeros((8, 48), BF),
        ],
        axis=1,
    )
    up_low = w_up.astype(BF).reshape(8, 2, 4, 2, 2, 4, 32).transpose(0, 3, 5, 1, 4, 2, 6)
    up_low = up_low.reshape(8, 4, D).transpose(1, 0, 2).reshape(32, D)
    down_low = by_core(w_down.astype(BF))
    attn_low = jnp.concatenate([in_low[3:6], out_low], axis=0).reshape(40, D)
    self_low = jnp.concatenate(
        [in_low[0:3].reshape(24, D), jnp.pad(tile, ((0, 0), (0, D - LANES)))], axis=0
    )
    z_at = lax.axis_index("z")

    def over_z(pack):
        out = jnp.zeros((4,) + pack.shape, BF)
        for k in range(4):
            steps = [(i, (i + k) % 4) for i in range(4)]
            part = pack if k == 0 else lax.ppermute(pack, "z", steps)
            out = lax.dynamic_update_slice(out, part[None], (lax.rem(z_at + 4 - k, 4), 0, 0))
        return out

    self_z = over_z(self_low).reshape(4, 4, 8, D).transpose(1, 0, 2, 3).reshape(1, 4, 32, D)
    z_pack = jnp.concatenate([up_low, down_low, attn_low], axis=0)
    (z_pack, self_z) = lax.optimization_barrier((z_pack, self_z))
    z_all = over_z(z_pack)
    attn_z = z_all[:, 64:104].reshape(4, 5, 8, D).transpose(1, 0, 2, 3).reshape(1, 5, 32, D)
    up_z = z_all[:, :32].reshape(4, 4, 8, D).transpose(1, 0, 2, 3).reshape(4, 32, D)
    ffn_z = jnp.concatenate([up_z, z_all[:, 32:64]], axis=0)[None]

    def over_plane(x):
        n = x.shape[1]
        y = lax.all_gather(x.reshape(n * 32, D), PLANE, axis=0, tiled=True)
        return y.reshape(16, n, 32, D)

    self_own = over_plane(self_z)
    self_other = swap(self_own)
    attn_own = over_plane(attn_z)
    ffn_own = over_plane(ffn_z)

    x = by_core(tokens[0])
    enc = by_core(encoded[0])
    cot = by_core(cotangent[0])

    tile_own, tile_other = self_own[:, 3, :, :LANES], self_other[:, 3, :, :LANES]

    def up_part(t):
        return t[:, :, 15:19].reshape(16, 4, 32).transpose(1, 0, 2).reshape(1, 2048)

    up_own, up_other = up_part(tile_own), up_part(tile_other)
    up_vec = jnp.concatenate(
        [jnp.where(first_core, up_own, up_other), jnp.where(first_core, up_other, up_own)], axis=1
    ).astype(F32)
    at = (lax.axis_index("yh"), 0, lax.axis_index("x"), 0, 0, 0)
    seq_tile = lax.dynamic_slice(
        tile_own.reshape(2, 2, 4, 4, 8, LANES), at, (1, 2, 1, 4, 8, LANES)
    )
    seq_tile = seq_tile.reshape(8, 8, LANES).astype(F32).astype(jnp.int32)
    units = seq_tile[:, :, 32:64].reshape(-1)
    texts = seq_tile[:, :, 64:80].reshape(-1)
    self_plan = key_plan(units, units, True)
    cross_plan = key_plan(units, texts, False)

    qkv, _, vec, a1 = call(
        qkv_kernel,
        (3,),
        [
            whole((rows, D)),
            pl.BlockSpec((16, 1, 32, LANES), lambda m, c: (0, 3, 0, 0)),
            pl.BlockSpec((16, 1, 32, LANES), lambda m, c: (0, 3, 0, 0)),
            pl.BlockSpec((16, 1, 32, D), lambda m, c: (0, m, 0, 0)),
            pl.BlockSpec((16, 1, 32, D), lambda m, c: (0, m, 0, 0)),
        ],
        [
            pl.BlockSpec((GROUPS, rows, LANES), lambda m, c: (0, 0, m)),
            whole((2, rows, 512)),
            whole((16, D)),
            whole((rows, D)),
        ],
        [
            shape((GROUPS, rows, 384)),
            shape((2, rows, 512)),
            shape((16, D), F32),
            shape((rows, D)),
        ],
        [],
        1.6e9,
        8e6,
    )(core_arg, x, self_own, self_other, self_own, self_other)
    qkv = lax.all_to_all(qkv, SEQ, 0, 0, tiled=True)
    self_keys = ((GROUPS, rows, LANES), (0, 0, 1), (0, 0, 2))
    o1_heads, lse1 = attend_fwd(self_plan, qkv, qkv, self_keys, True)
    (attn_own, a1, _) = lax.optimization_barrier((attn_own, a1, o1_heads))
    attn_other = swap(attn_own)
    a1_all = lax.all_gather(a1, SEQ, axis=0, tiled=False)
    o1 = lax.all_to_all(o1_heads, SEQ, 0, 0, tiled=True)

    kv2 = call(
        text_kernel,
        (2,),
        [
            whole((text_rows, D)),
            whole((16, D)),
            pl.BlockSpec((16, 1, 32, D), lambda m, c: (0, 1 + m, 0, 0)),
            pl.BlockSpec((16, 1, 32, D), lambda m, c: (0, 1 + m, 0, 0)),
        ],
        pl.BlockSpec((GROUPS, text_rows, LANES), lambda m, c: (0, m, 0)),
        shape((GROUPS, 2 * text_rows, LANES)),
        [],
        0.5e9,
        4e6,
        after=(o1_heads,),
    )(core_arg, enc, vec, attn_own, attn_other)

    x1, a2, q2 = call(
        middle_kernel,
        (1,),
        [whole((GROUPS, rows, LANES)), whole((rows, D)), whole((16, D))]
        + [matrix(3), matrix(3), matrix(0), matrix(0), whole((GROUPS, 2 * text_rows, LANES))],
        [whole((rows, D)), whole((2, rows, 512)), whole((GROUPS, 2 * rows, LANES))],
        [shape((rows, D), F32), shape((2, rows, 512)), shape((GROUPS, 2 * rows, LANES))],
        [],
        1.1e9,
        8e6,
    )(core_arg, o1, x, vec, attn_own, attn_other, attn_own, attn_other, kv2)
    q2 = lax.all_to_all(q2, SEQ, 0, 0, tiled=True)
    cross_keys = ((GROUPS, text_rows, LANES), (0, 2, 0), (0, 3, 0))
    o2_heads, lse2 = attend_fwd(cross_plan, q2, q2, cross_keys, False)
    o2 = lax.all_to_all(o2_heads, SEQ, 0, 0, tiled=True)
    (ffn_own, _) = lax.optimization_barrier((ffn_own, o2))
    ffn_other = swap(ffn_own)

    def block_of(s, c):
        t = lax.rem(s, 8)
        return jnp.where(t < 4, c[0], 1 - c[0]) * 4 + lax.rem(t, 4)

    def back_block(s, c):
        return block_of(jnp.maximum(s, 8), c)

    up_spec = pl.BlockSpec(
        (16, 1, 32, 512), lambda s, c: (0, block_of(s, c) // 2, 0, lax.rem(block_of(s, c), 2))
    )
    gup_spec = pl.BlockSpec(
        (16, 1, 32, 512), lambda s, c: (0, back_block(s, c) // 2, 0, lax.rem(back_block(s, c), 2))
    )
    (layer_out, g2, e2, do2, a3, e3, hidden, ep, small_f, dup_bias, gup, gdn, go) = call(
        ffn_kernel,
        (16,),
        [
            whole((GROUPS, rows, LANES)),
            whole((rows, D)),
            whole((16, D)),
            pl.BlockSpec((1, 512), lambda s, c: (0, block_of(s, c))),
            whole((rows, D)),
            matrix(4),
            matrix(4),
            up_spec,
            up_spec,
            pl.BlockSpec(
                (16, 1, 32, D), lambda s, c: (0, 4 + jnp.minimum(lax.rem(s, 8), 3), 0, 0)
            ),
            pl.BlockSpec(
                (16, 1, 32, D), lambda s, c: (0, jnp.maximum(lax.rem(s, 8), 4), 0, 0)
            ),
        ],
        [
            whole((rows, D)),
            whole((rows, D)),
            whole((rows, D)),
            whole((GROUPS, rows, LANES)),
            whole((2, rows, 512)),
            whole((rows, D)),
            pl.BlockSpec((rows, 512), lambda s, c: (0, jnp.clip(s - 8, 0, 3))),
            pl.BlockSpec((rows, 512), lambda s, c: (0, back_block(s, c))),
            whole((8, D)),
            pl.BlockSpec((1, 512), lambda s, c: (0, back_block(s, c))),
            gup_spec,
            pl.BlockSpec((16, 1, 32, D), lambda s, c: (0, jnp.maximum(s - 12, 0), 0, 0)),
            matrix(0),
        ],
        [
            shape((rows, D), F32),
            shape((rows, D), F32),
            shape((rows, D)),
            shape((GROUPS, rows, LANES)),
            shape((2, rows, 512)),
            shape((rows, D)),
            shape((rows, FF // 2)),
            shape((rows, FF)),
            shape((8, D), F32),
            shape((1, FF), F32),
            shape((16, 4, 32, D)),
            shape((16, 4, 32, D)),
            shape((16, 1, 32, D)),
        ],
        [
            pltpu.VMEM((rows, D), F32),
            pltpu.VMEM((rows, D), F32),
            pltpu.VMEM((8, rows, 512), F32),
            pltpu.VMEM((8, rows, 512), BF),
            pltpu.VMEM((2, rows, 512), F32),
            pltpu.VMEM((rows, 512), F32),
            pltpu.VMEM((512, rows), F32),
        ],
        16e9,
        50e6,
    )(core_arg, o2, x1, vec, up_vec, cot, attn_own, attn_other, ffn_own, ffn_other,
      ffn_own, ffn_other)
    do2 = lax.all_to_all(do2, SEQ, 0, 0, tiled=True)
    gup_recv, gdn_recv, go_recv = swap(gup), swap(gdn), swap(go)

    back2_heads = attend_bwd(
        cross_plan, lse2, q2, q2, o2_heads, do2, cross_keys, False, after=(a1_all,)
    )
    back2 = lax.all_to_all(back2_heads, SEQ, 0, 0, tiled=True)
    ffn_grad = call(
        ffn_grad_kernel,
        (9,),
        [
            whole((2, rows, 512)),
            pl.BlockSpec((rows, D), lambda m, c: (0, jnp.minimum(m, 3))),
            pl.BlockSpec((rows, 512), lambda m, c: (0, jnp.clip(m - 4, 0, 3))),
            whole((rows, D)),
            pl.BlockSpec((16, 1, 32, D), lambda m, c: (0, jnp.minimum(m, 3), 0, 0)),
            pl.BlockSpec((16, 1, 32, D), lambda m, c: (0, jnp.clip(m - 4, 0, 3), 0, 0)),
            whole((GROUPS, rows, LANES)),
            whole((rows, D)),
            matrix(0),
        ],
        pl.BlockSpec((16, 1, 32, D), lambda m, c: (0, m, 0, 0)),
        shape((16, 12, 32, D)),
        [],
        2.4e9,
        20e6,
        after=(back2_heads,),
    )(core_arg, a3, ep, hidden, e3, gup_recv, gdn_recv, o2, e2, go_recv)

    def cross_grads(half, recv, into, after=()):
        args = (core_arg, a2, enc, back2) + tuple(recv)
        later = after if into is None else (into,)
        first, blocks = (0, 3) if into is None else (9, 12)
        block = pl.BlockSpec((16, 1, 32, D), lambda m, c: (0, m, 0, 0))
        return pl.pallas_call(
            without(functools.partial(cross_grad_kernel, half), len(args), len(later)),
            grid_spec=pltpu.PrefetchScalarGridSpec(
                num_scalar_prefetch=1,
                grid=(3,),
                in_specs=[
                    whole((2, rows, 512)),
                    whole((text_rows, D)),
                    whole((GROUPS, rows + 2 * text_rows, LANES)),
                ]
                + [block] * len(recv)
                + [pl.BlockSpec(memory_space=pl.ANY)] * len(later),
                out_specs=pl.BlockSpec((16, 1, 32, D), lambda m, c: (0, first + m, 0, 0)),
            ),
            out_shape=shape((16, blocks, 32, D)),
            input_output_aliases={} if into is None else {len(args): 0},
            compiler_params=params(),
            cost_estimate=cost(0.6e9, 5e6),
        )(*args, *later)

    cross_theirs = cross_grads(1, [], None, (ffn_grad,))
    cross_recv = swap(cross_theirs)

    g1, e1, do1, small_c = call(
        cross_back_kernel,
        (1,),
        [whole((GROUPS, rows + 2 * text_rows, LANES)), whole((rows, D)), whole((rows, D))]
        + [whole((16, D)), matrix(0), matrix(0), matrix(3), matrix(3)],
        [whole((rows, D)), whole((rows, D)), whole((GROUPS, rows, LANES)), whole((8, D))],
        [
            shape((rows, D), F32),
            shape((rows, D)),
            shape((GROUPS, rows, LANES)),
            shape((8, D), F32),
        ],
        [],
        1.1e9,
        10e6,
        after=(ffn_grad, cross_theirs),
    )(core_arg, back2, x1, g2, vec, attn_own, attn_other, attn_own, attn_other)
    do1_rows = do1
    do1 = lax.all_to_all(do1, SEQ, 0, 0, tiled=True)
    (cross_recv, _) = lax.optimization_barrier((cross_recv, do1_rows))
    all_grads = cross_grads(0, [cross_recv], ffn_grad)
    (scattered, _) = lax.optimization_barrier((all_grads, do1))
    grads = lax.psum_scatter(
        scattered.reshape(16 * 12 * 32, D), PLANE, scatter_dimension=0, tiled=True
    ).reshape(12, 32, D)

    dqkv_heads = attend_bwd(
        self_plan, lse1, qkv, qkv, o1_heads, do1, self_keys, True, after=(all_grads,)
    )
    dqkv = lax.all_to_all(dqkv_heads, SEQ, 0, 0, tiled=True)
    width = 3 * LANES + D + LANES

    def self_grads(half, recv, n, later):
        at = (lambda m, c: (0, 0, c[0])) if half == 0 else (lambda m, c: (0, 0, 1 - c[0]))
        return call(
            functools.partial(self_grad_kernel, half),
            (1,),
            [
                pl.BlockSpec((GROUPS, rows, 512), at),
                whole((GROUPS, rows, 3 * LANES)),
                whole((GROUPS, rows, LANES)),
                whole((rows, D)),
            ]
            + [whole((512, 3 * LANES + D))] * len(recv),
            whole((512, n)),
            shape((512, n)),
            [],
            1.1e9,
            8e6,
            after=later,
        )(core_arg, a1_all, dqkv_heads, o1, e1, *recv)

    self_theirs = self_grads(1, [], 3 * LANES + D, ())
    self_recv = swap(self_theirs)
    d_enc = call(
        text_back_kernel,
        (1,),
        [whole((GROUPS, rows + 2 * text_rows, LANES))]
        + [matrix(1), matrix(1), matrix(2), matrix(2)],
        whole((text_rows, D)),
        shape((text_rows, D), F32),
        [],
        0.5e9,
        5e6,
        after=(self_theirs,),
    )(core_arg, back2, attn_own, attn_other, attn_own, attn_other)
    own = self_grads(0, [self_recv], width, (d_enc,))

    d_tokens, small_s, dsum = call(
        self_back_kernel,
        (3,),
        [
            pl.BlockSpec((GROUPS, rows, LANES), lambda m, c: (0, 0, m)),
            pl.BlockSpec((16, 1, 32, D), lambda m, c: (0, m, 0, 0)),
            pl.BlockSpec((16, 1, 32, D), lambda m, c: (0, m, 0, 0)),
            whole((rows, D)),
            whole((rows, D)),
            whole((16, D)),
        ],
        [
            whole((rows, D)),
            whole((8, D)),
            pl.BlockSpec((1, 1, D), lambda m, c: (m, 0, 0)),
        ],
        [shape((rows, D), F32), shape((8, D), F32), shape((3, 1, D), F32)],
        [pltpu.VMEM((2, rows, 512), F32)],
        1.6e9,
        9e6,
        after=(own,),
    )(core_arg, dqkv, self_own, self_other, x, g1, vec)

    small = jnp.concatenate(
        [
            small_s[0:1],
            small_c[0:1],
            small_f[3:4],
            small_f[0:1],
            small_s[1:2],
            small_c[1:2],
            small_f[4:5],
            small_f[1:2],
            dsum[0],
            dsum[2],
            small_c[2:3],
            small_c[3:4],
            small_c[4:5],
            small_f[5:6],
            small_f[2:3],
        ],
        axis=0,
    )
    up_sums = dup_bias.reshape(2, 4, 2, 2, 4, 32).transpose(0, 2, 4, 3, 1, 5).reshape(D, 4)
    small = jnp.concatenate([small.T, up_sums, jnp.zeros((D, LANES - 19), F32)], axis=1)
    small_recv = swap(theirs(small).astype(BF))
    last = pl.pallas_call(
        small_kernel,
        grid_spec=pltpu.PrefetchScalarGridSpec(
            num_scalar_prefetch=1,
            grid=(1,),
            in_specs=[whole((512, LANES)), whole((512, LANES)), pl.BlockSpec(memory_space=pl.ANY)],
            out_specs=pl.BlockSpec((512, LANES), lambda m, c: (0, 3 + D // LANES)),
        ),
        out_shape=shape((512, width)),
        input_output_aliases={3: 0},
        compiler_params=params(),
        cost_estimate=cost(1e5, 5e5),
    )(core_arg, mine(small), small_recv, own)
    last = lax.all_to_all(last.reshape(64, 8, width), CHIPS, 0, 0, tiled=True)
    z_grad = jnp.concatenate(
        [
            grads[:4].reshape(4, 4, 8, D).transpose(1, 0, 2, 3).reshape(4, 32, D),
            grads[4:8],
            grads[8:].reshape(4, 4, 8, D).transpose(1, 0, 2, 3).reshape(4, 32, D),
        ],
        axis=1,
    )
    parts = []
    for k in range(4):
        to = lax.rem(z_at + k, 4)
        part = lax.dynamic_slice_in_dim(z_grad, to, 1, 0)[0]
        if k:
            part = lax.ppermute(part, "z", [(i, (i + k) % 4) for i in range(4)])
        parts.append(part)
    d_in, d_out, d_up, d_down, d_gain, d_shift, d_bias, tile_sum = pl.pallas_call(
        finish_kernel,
        out_shape=[
            shape((6, 8, D), F32),
            shape((2, 8, D), F32),
            shape((8, FF), F32),
            shape((32, D), F32),
            shape((4, 8), F32),
            shape((4, 8), F32),
            shape((7, 8), F32),
            shape((8, LANES), F32),
        ],
        compiler_params=params(),
        cost_estimate=cost(1e6, 3e6),
    )(*parts, last)
    d_up_bias = tile_sum[:, 15:19].reshape(32)
    return (
        layer_out[None],
        d_tokens[None],
        d_enc[None],
        d_in,
        d_out,
        d_up,
        d_down,
        d_gain,
        d_shift,
        d_bias,
        d_up_bias,
    )


def solution(mesh):
    fine = Mesh(mesh.devices.reshape(2, 4, 2, 2, 4), ("yh", "x", "c", "yl", "z"))
    fsdp = ("yh", "x", "c")
    every = fsdp + SEQ
    placed = (
        P(fsdp, SEQ, None),
        P(fsdp, SEQ, None),
        P(fsdp, SEQ),
        P(fsdp, SEQ),
        P(fsdp, SEQ, None),
        P(None, every, None),
        P(None, every, None),
        P(every, None),
        P(every, None),
        P(None, every),
        P(None, every),
        P(None, every),
        P(every),
    )
    return jax.shard_map(
        local,
        mesh=fine,
        in_specs=placed,
        out_specs=(
            P(fsdp, SEQ, None),
            P(fsdp, SEQ, None),
            P(fsdp, SEQ, None),
            P(None, every, None),
            P(None, every, None),
            P(every, None),
            P(every, None),
            P(None, every),
            P(None, every),
            P(None, every),
            P(every),
        ),
        check_vma=False,
    )
```
